32 devices in a mesh: expert: 8 (over z, y), shard: 4 (over x, core).
Axes of the slice: x: 2, y: 2, z: 4, core: 2. Of those that a mesh axis runs over, the one named last changes fastest.
Arguments:
- tokens: bfloat16 [4096, 2048], P(('expert', 'shard')), may hold values from -6 to 6
- segments: int32 [4096], P('expert'), may hold values from 0 to 8, as said below
- routes: int32 [4096, 6], P(('expert', 'shard')), may hold values from 0 to 15, all different within a row; in each aligned block of 128 rows (0 to 127, 128 to 255, ...) at most 96 rows name the same one
- cotangent: bfloat16 [4096, 2048], P(('expert', 'shard')), may hold values from -6 to 6
- attn_gain: bfloat16 [2048], P('expert'), may hold values from 0.5 to 1.5
- w_query: bfloat16 [2048, 3072], P('expert', 'shard'), may hold values from -0.125 to 0.125
- w_latent: bfloat16 [2048, 576], P('expert'), may hold values from -0.125 to 0.125
- latent_gain: bfloat16 [512], P('expert'), may hold values from 0.5 to 1.5
- w_expand: bfloat16 [512, 4096], P('expert', 'shard'), may hold values from -0.25 to 0.25
- w_output: bfloat16 [2048, 2048], P('shard', 'expert'), may hold values from -0.5 to 0.5
- ffn_gain: bfloat16 [2048], P('expert'), may hold values from 0.5 to 1.5
- w_router: bfloat16 [2048, 16], P('expert'), may hold values from -0.0625 to 0.0625
- w_shared_gate: bfloat16 [2048, 2816], P('expert', 'shard'), may hold values from -0.125 to 0.125
- w_shared_up: bfloat16 [2048, 2816], P('expert', 'shard'), may hold values from -0.125 to 0.125
- w_shared_down: bfloat16 [2816, 2048], P('shard', 'expert'), may hold values from -0.21875 to 0.21875
- w_expert_gate: bfloat16 [16, 2048, 1408], P('expert', None, 'shard'), may hold values from -0.125 to 0.125
- w_expert_up: bfloat16 [16, 2048, 1408], P('expert', None, 'shard'), may hold values from -0.125 to 0.125
- w_expert_down: bfloat16 [16, 1408, 2048], P('expert', 'shard'), may hold values from -0.3125 to 0.3125
Outputs:
- block_out: bfloat16 [4096, 2048], P(('expert', 'shard'))
- tokens_grad: float32 [4096, 2048], P(('expert', 'shard'))
- grad_attn_gain: float32 [2048], P('expert')
- grad_w_query: float32 [2048, 3072], P('expert', 'shard')
- grad_w_latent: float32 [2048, 576], P('expert')
- grad_latent_gain: float32 [512], P('expert')
- grad_w_expand: float32 [512, 4096], P('expert', 'shard')
- grad_w_output: float32 [2048, 2048], P('shard', 'expert')
- grad_ffn_gain: float32 [2048], P('expert')
- grad_w_router: float32 [2048, 16], P('expert')
- grad_w_shared_gate: float32 [2048, 2816], P('expert', 'shard')
- grad_w_shared_up: float32 [2048, 2816], P('expert', 'shard')
- grad_w_shared_down: float32 [2816, 2048], P('shard', 'expert')
- grad_w_expert_gate: float32 [16, 2048, 1408], P('expert', None, 'shard')
- grad_w_expert_up: float32 [16, 2048, 1408], P('expert', None, 'shard')
- grad_w_expert_down: float32 [16, 1408, 2048], P('expert', 'shard')
The draws below stay inside these ranges and needn't reach their ends.
Inputs may be any that keep to these rules, and one draw needn't show every extreme that they name: `routes`: each row names 6 different experts. Among the rows of one device (128 aligned rows) no expert is named more than 96 times, and in every draw some expert is named exactly 96 times. `segments`: in each aligned group of 512 tokens the ids are 0 over a leading prompt of 192 to 320 tokens, then rise by one at each new continuation up to 8 at the group's end; each continuation has one token or more.
All inputs are finite; a program needn't handle non-finite values.
Results may differ from the reference program's by a relative error of at most 0.024.
Values may be sent and summed in bfloat16 or wider, within the bound.
No kernel may reach another device: no remote copies, remote signals or barrier semaphores. Data moves between devices by JAX's collectives and lax.ppermute only.
A program may use at most 512 MiB of HBM per device.

```python
import math
import jax
import jax.numpy as jnp
import numpy as np
from jax import lax

D = 2048
H = 16
NOPE = 128
ROPE = 64
V_HEAD = 128
KV_RANK = 512
EXP_FF = 1408
SH_FF = 2816
TOP = 6
CONTS = 8
TOK_DEV = 128
EXPERTS = 16
GROUP = 512
TOKENS = 4096
CAP = 96


def draw_segments(key, part):
    key = jax.random.fold_in(key, 11)
    group_keys = jax.random.split(key, TOKENS // GROUP)

    def one_group(group_key):
        first_key, second_key = jax.random.split(group_key)
        prompt_len = jax.random.randint(first_key, (), GROUP // 2 - GROUP // 8, GROUP // 2 + GROUP // 8 + 1)
        remaining = GROUP - prompt_len
        indices = jnp.arange(1, GROUP, dtype=jnp.int32)
        ranking = jax.random.randint(second_key, (GROUP - 1,), 0, 2 ** 20) * GROUP + indices
        ranking = jnp.where(indices < remaining, ranking, -indices)
        chosen, unused = lax.top_k(ranking, CONTS - 1)
        cuts = chosen % GROUP
        offsets = jnp.arange(GROUP, dtype=jnp.int32) - prompt_len
        counted = jnp.sum((cuts[None, :] <= offsets[:, None]).astype(jnp.int32), axis=1)
        return jnp.where(offsets >= 0, 1 + counted, 0).astype(jnp.int32)
    return jax.vmap(one_group)(group_keys).reshape(-1)


def steps_of(key, dims, cuts, low, top_value):
    factor_of = 1.0
    for axis_at, shards_of in cuts:
        draws = jax.random.uniform(jax.random.fold_in(jax.random.fold_in(key, 6), axis_at), (shards_of,), jnp.float32, low / len(cuts), top_value / len(cuts))
        factor_of = factor_of * jnp.repeat(jnp.exp(draws), dims[axis_at] // shards_of).reshape((-1,) + (1,) * (len(dims) - 1 - axis_at))
    return factor_of


def routed_block(stream_key, own, number, rows, count, top, limit, lean):
    order = jax.random.permutation(stream_key, count)
    heavy_load, common = shares(count, rows * top, limit, lean, True), shares(count, rows * top, limit, lean, False)
    places = jnp.arange(count)

    def named(sizes, turn):
        used = int((sizes > 0).sum())
        fixed = max(1, used // 4)
        moved = fixed + (places - fixed + turn * (used - fixed)) % max(1, count - fixed)
        return jnp.zeros((count,), jnp.int32).at[order[jnp.where(places < fixed, places, moved)]].set(jnp.asarray(sizes, jnp.int32))

    sizes = jnp.where(number % 4 == 0, named(heavy_load, number // 4), named(common, number - number // 4 - 1))
    mixed = jax.random.permutation(jax.random.fold_in(own, 3), count)
    source_of, sink = mixed[0:count // 2 * 2:2], mixed[1:count // 2 * 2:2]
    slack = jnp.minimum(sizes[source_of] - 1, limit - sizes[sink]) // 2
    slack = jnp.where((source_of == order[0]) | (sink == order[0]) | (sizes[sink] == 0), 0, jnp.maximum(slack, 0))
    moved = jax.random.randint(jax.random.fold_in(own, 4), (count // 2,), 0, 1 << 20) % (slack + 1)
    sizes = sizes.at[source_of].add(-moved).at[sink].add(moved)
    items = jnp.searchsorted(jnp.cumsum(sizes), jnp.arange(rows * top), side="right").astype(jnp.int32)
    table = items.reshape(top, rows).T
    table = table[jax.random.permutation(jax.random.fold_in(own, 1), rows)]
    turn = jax.random.randint(jax.random.fold_in(own, 2), (rows, 1), 0, top)
    return jnp.take_along_axis(table, (jnp.arange(top)[None, :] + turn) % top, axis=1)


def shares(amount, total, bound, skew, full):
    portions = [(1 << 20) // math.isqrt(grade ** skew) + 1 for grade in range(1, amount + 1)]
    largest = bound if full else min(bound, max(-(-total // amount), total * portions[0] // sum(portions)))
    least = 1 if total - largest >= amount - 1 else 0
    counts, surplus = [largest] + [least] * (amount - 1), total - largest - least * (amount - 1)
    while surplus > 0:
        movable = [i for i in range(1, amount) if counts[i] < largest] or [i for i in range(1, amount) if counts[i] < bound]
        pool, budget = sum([portions[i] for i in movable]), surplus
        for i in movable:
            more = min(bound - counts[i], max(1, budget * portions[i] // pool), surplus)
            counts[i] = counts[i] + more
            surplus = surplus - more
    return np.array(counts)


def bell_draw(key, shape, scale, most, shards=(), held_as=jnp.bfloat16):
    entries = scale * jax.random.normal(key, shape, jnp.float32)
    if shards:
        entries = entries * steps_of(key, shape, shards, -0.22, 0.18)
    return jnp.clip(entries, -most, most).astype(held_as)


def setup_inputs(seed: int = 0) -> dict:
    key_of = jax.random.split(jax.random.key(seed), 19)
    tokens = bell_draw(key_of[0], (TOKENS, D), 1.0, 6.0, ((0, 32),))
    segments = draw_segments(jax.random.fold_in(key_of[18], 71), 0)
    routes_keys = jax.random.split(jax.random.fold_in(key_of[2], 1), TOKENS // TOK_DEV)
    routes_turns = jax.random.permutation(jax.random.fold_in(key_of[2], 3), TOKENS // TOK_DEV)
    routes = jax.vmap(lambda own, number: routed_block(jax.random.fold_in(key_of[2], 2), own, number, TOK_DEV, EXPERTS, TOP, CAP, 1))(routes_keys, routes_turns).reshape((TOKENS, TOP))
    cotangent = bell_draw(key_of[3], (TOKENS, D), 1.0, 6.0, ((0, 32),))
    attn_gain = jnp.clip(1.0 + 0.1 * jax.random.normal(key_of[4], (D,), jnp.float32), 0.5, 1.5).astype(jnp.bfloat16)
    w_query = bell_draw(key_of[5], (D, H * (NOPE + ROPE)), D ** -0.5, 0.125, ((0, 8), (1, 4)))
    w_latent = bell_draw(key_of[6], (D, KV_RANK + ROPE), D ** -0.5, 0.125, ((0, 8),))
    latent_gain = jnp.clip(1.0 + 0.1 * jax.random.normal(key_of[7], (KV_RANK,), jnp.float32), 0.5, 1.5).astype(jnp.bfloat16)
    w_expand = bell_draw(key_of[8], (KV_RANK, H * (NOPE + V_HEAD)), KV_RANK ** -0.5, 0.25, ((0, 8), (1, 4)))
    w_output = bell_draw(key_of[9], (H * V_HEAD, D), (H * V_HEAD // 16) ** -0.5, 0.5, ((0, 4), (1, 8)))
    ffn_gain = jnp.clip(1.0 + 0.1 * jax.random.normal(key_of[10], (D,), jnp.float32), 0.5, 1.5).astype(jnp.bfloat16)
    w_router = bell_draw(key_of[11], (D, EXPERTS), (4 * D) ** -0.5, 0.0625, ((0, 8),))
    w_shared_gate = bell_draw(key_of[12], (D, SH_FF), D ** -0.5, 0.125, ((0, 8), (1, 4)))
    w_shared_up = bell_draw(key_of[13], (D, SH_FF), D ** -0.5, 0.125, ((0, 8), (1, 4)))
    w_shared_down = bell_draw(key_of[14], (SH_FF, D), (SH_FF // 4) ** -0.5, 0.21875, ((0, 4), (1, 8)))
    w_expert_gate = bell_draw(key_of[15], (EXPERTS, D, EXP_FF), D ** -0.5, 0.125, ((0, 8), (2, 4)))
    w_expert_up = bell_draw(key_of[16], (EXPERTS, D, EXP_FF), D ** -0.5, 0.125, ((0, 8), (2, 4)))
    w_expert_down = bell_draw(key_of[17], (EXPERTS, EXP_FF, D), (EXP_FF // 4) ** -0.5, 0.3125, ((0, 8), (1, 4)))
    return {"tokens": tokens, "segments": segments, "routes": routes, "cotangent": cotangent, "attn_gain": attn_gain, "w_query": w_query, "w_latent": w_latent, "latent_gain": latent_gain, "w_expand": w_expand, "w_output": w_output, "ffn_gain": ffn_gain, "w_router": w_router, "w_shared_gate": w_shared_gate, "w_shared_up": w_shared_up, "w_shared_down": w_shared_down, "w_expert_gate": w_expert_gate, "w_expert_up": w_expert_up, "w_expert_down": w_expert_down}


@jax.custom_vjp
def low(v):
    return lax.optimization_barrier(v.astype(jnp.bfloat16)).astype(jnp.float32)

@jax.custom_vjp
def low_back(v):
    return v

def low_keep(v):
    return (low(v), None)

def low_pass(kept, grad):
    return (grad,)

def back_keep(v):
    return (v, None)

def back_low(kept, grad):
    return (low(grad),)
low.defvjp(low_keep, low_pass)
low_back.defvjp(back_keep, back_low)
epsilon = 1e-06
highest = lax.Precision.HIGHEST

def product(left, right):
    return jnp.dot(left, right, precision=highest, preferred_element_type=jnp.float32)

def rotate(values, cosine, sine):
    half_width = values.shape[-1] // 2
    first_half = values[..., :half_width]
    second_half = values[..., half_width:]
    return jnp.concatenate([first_half * cosine - second_half * sine, second_half * cosine + first_half * sine], axis=-1)

def angles(places, width):
    half_width = width // 2
    spacing = 10000.0 ** (-2.0 * jnp.arange(half_width, dtype=jnp.float32) / width)
    turned = places.astype(jnp.float32)[:, None] * spacing[None, :]
    return (jnp.cos(turned), jnp.sin(turned))

def positions(segment):
    indices = jnp.arange(segment.shape[0], dtype=jnp.int32)
    prompt_len = jnp.sum((segment == 0).astype(jnp.int32))
    earlier = lax.optimization_barrier(jnp.sum((segment[None, :] < segment[:, None]).astype(jnp.int32), axis=1))
    return jnp.where(segment == 0, indices, prompt_len + indices - earlier)

def inverse_rms(values):
    return lax.rsqrt(lax.optimization_barrier(jnp.mean(values * values, axis=-1, keepdims=True)) + epsilon)

def attend_group(w_expand, pieces):
    queries, latents, rotated, segment = pieces
    length = queries.shape[0]
    expanded = low(low_back(product(latents, w_expand))).reshape(length, H, NOPE + V_HEAD)
    keys_all = jnp.concatenate([expanded[..., :NOPE], jnp.broadcast_to(rotated[:, None, :], (length, H, ROPE))], axis=-1)
    scores = low_back((NOPE + ROPE) ** (-0.5) * jnp.einsum('qhd,khd->hqk', queries, keys_all, precision=highest))
    indices = jnp.arange(length, dtype=jnp.int32)
    allowed = (indices[None, :] <= indices[:, None]) & ((segment[None, :] == 0) | (segment[None, :] == segment[:, None]))
    scores = jnp.where(allowed[None], scores, -1e+30)
    largest = lax.optimization_barrier(jnp.max(scores, axis=-1, keepdims=True))
    exponent_vals = jnp.exp(scores - largest)
    soft_low = low(exponent_vals / lax.optimization_barrier(jnp.sum(exponent_vals, axis=-1, keepdims=True)))
    mixed_heads = jnp.einsum('hqk,khd->qhd', soft_low, expanded[..., NOPE:], precision=highest)
    return low(low_back(mixed_heads)).reshape(length, H * V_HEAD)

def forward(tokens, attn_gain, w_query, w_latent, latent_gain, w_expand, w_output, ffn_gain, w_router, w_shared_gate, w_shared_up, w_shared_down, w_expert_gate, w_expert_up, w_expert_down, segments, routes):
    row_count = tokens.shape[0]
    group_count = row_count // GROUP
    segment_groups = segments.reshape(group_count, GROUP)
    places = jax.vmap(positions)(segment_groups).reshape(-1)
    cosine, sine = angles(places, ROPE)
    normed_in = low(tokens * inverse_rms(tokens) * attn_gain)
    query_raw = low_back(product(normed_in, w_query)).reshape(row_count, H, NOPE + ROPE)
    query_use = low(jnp.concatenate([query_raw[..., :NOPE], rotate(query_raw[..., NOPE:], cosine[:, None, :], sine[:, None, :])], axis=-1))
    latent_raw = low_back(product(normed_in, w_latent))
    compressed = latent_raw[:, :KV_RANK]
    latent_use = low(compressed * inverse_rms(compressed) * latent_gain)
    rope_key = low(rotate(latent_raw[:, KV_RANK:], cosine, sine))

    def one_group(pieces):
        return attend_group(w_expand, pieces)
    attn_mixed = lax.map(jax.checkpoint(one_group), (query_use.reshape(group_count, GROUP, H, NOPE + ROPE), latent_use.reshape(group_count, GROUP, KV_RANK), rope_key.reshape(group_count, GROUP, ROPE), segment_groups)).reshape(row_count, H * V_HEAD)
    hidden_one = tokens + low_back(product(attn_mixed, w_output))
    normed_ffn = low(hidden_one * inverse_rms(hidden_one) * ffn_gain)
    logits = low_back(product(normed_ffn, w_router))
    picked = jnp.take_along_axis(logits, routes, axis=1)
    picked_top = lax.optimization_barrier(jnp.max(picked, axis=-1, keepdims=True))
    picked_exp = jnp.exp(picked - picked_top)
    gates = picked_exp / lax.optimization_barrier(jnp.sum(picked_exp, axis=-1, keepdims=True))
    gate_table = lax.optimization_barrier(jnp.sum(jnp.where(routes[:, :, None] == jnp.arange(EXPERTS, dtype=jnp.int32)[None, None, :], gates[:, :, None], 0.0), axis=1))
    shared_gate = low_back(product(normed_ffn, w_shared_gate))
    shared_upv = low_back(product(normed_ffn, w_shared_up))
    shared_out = low_back(product(low(jax.nn.silu(shared_gate) * shared_upv), w_shared_down))

    def expert_step(total, items):
        gate_weight, up_weight, down_weight, column = items
        copied = low_back(normed_ffn)
        expert_gate = low_back(product(copied, gate_weight))
        expert_upv = low_back(product(copied, up_weight))
        expert_out = low(low_back(product(low(jax.nn.silu(expert_gate) * expert_upv), down_weight)))
        return (total + column[:, None] * expert_out, None)
    routed, unused = lax.scan(jax.checkpoint(expert_step), jnp.zeros((row_count, D), jnp.float32), (w_expert_gate, w_expert_up, w_expert_down, gate_table.T))
    return hidden_one + shared_out + routed

def reference(tokens, segments, routes, cotangent, attn_gain, w_query, w_latent, latent_gain, w_expand, w_output, ffn_gain, w_router, w_shared_gate, w_shared_up, w_shared_down, w_expert_gate, w_expert_up, w_expert_down):
    floats = tuple((item.astype(jnp.float32) for item in (tokens, attn_gain, w_query, w_latent, latent_gain, w_expand, w_output, ffn_gain, w_router, w_shared_gate, w_shared_up, w_shared_down, w_expert_gate, w_expert_up, w_expert_down)))

    def layer(*values):
        return forward(*values, segments, routes)
    result, pull_back = jax.vjp(layer, *floats)
    grads = pull_back(cotangent.astype(jnp.float32))
    return (result.astype(jnp.bfloat16), grads[0], grads[1], grads[2], grads[3], grads[4], grads[5], grads[6], grads[7], grads[8], grads[9], grads[10], grads[11], grads[12], grads[13], grads[14])
```

```python
import jax
import jax.numpy as jnp
from jax import lax
from jax.sharding import PartitionSpec as P

NOPE = 128
ROPE = 64
V_HEAD = 128
KV_RANK = 512
TOP = 6
LANES = 128

epsilon = 1e-06
F32 = jnp.float32
BF16 = jnp.bfloat16


def pad_to(n, m):
    return -(-n // m) * m


def angles(places, width):
    half_width = width // 2
    spacing = 10000.0 ** (-2.0 * jnp.arange(half_width, dtype=F32) / width)
    turned = places.astype(F32)[:, None] * spacing[None, :]
    return (jnp.cos(turned), jnp.sin(turned))


def positions(segment):
    indices = jnp.arange(segment.shape[0], dtype=jnp.int32)
    prompt_len = jnp.sum((segment == 0).astype(jnp.int32))
    earlier = jnp.sum((segment[None, :] < segment[:, None]).astype(jnp.int32), axis=1)
    return jnp.where(segment == 0, indices, prompt_len + indices - earlier)


def inverse_rms(values):
    return lax.rsqrt(jnp.mean(values * values, axis=-1, keepdims=True) + epsilon)


def norm_back(values, scaling, gain, incoming):
    weighted = incoming * gain
    inner = jnp.mean(weighted * values, axis=-1, keepdims=True)
    return (
        scaling * weighted - values * scaling**3 * inner,
        jnp.sum(incoming * values * scaling, axis=0),
    )


def dot(a, b, dims):
    return lax.dot_general(a, b, (dims, ((), ())), preferred_element_type=F32)


def mm(a, b):
    return dot(a, b, ((1,), (0,)))


def mm_t(a, b):
    return dot(a, b, ((1,), (1,)))


def t_mm(a, b):
    return dot(a, b, ((0,), (0,)))


BOTH = ("expert", "shard")


def gather(values, axes, dim=0):
    return lax.all_gather(values, axes, axis=dim, tiled=True)


def total(values, axes, dim=0):
    return lax.psum_scatter(values, axes, scatter_dimension=dim, tiled=True)


def padded(parts, widths, dim):
    out = []
    for part, width in zip(parts, widths):
        pads = [(0, 0)] * part.ndim
        pads[dim] = (0, width - part.shape[dim])
        out.append(jnp.pad(part, pads))
    return jnp.concatenate(out, axis=dim)


def ffn_block(rows, grads, routed, gate_up, gate_up_t, down, down_t, sizes, first):
    seg, shared, experts, local = sizes
    width = down.shape[0]
    both = mm(rows, gate_up)
    logits = both[:, local * seg + shared : local * seg + shared + experts]
    masked = jnp.where(routed > 0, logits, -1e30)
    raised = jnp.where(routed > 0, jnp.exp(masked - jnp.max(masked, axis=1, keepdims=True)), 0.0)
    gates = raised / jnp.sum(raised, axis=1, keepdims=True)
    expert_lane = jnp.arange(experts, dtype=jnp.int32)[None, :]
    cols = [
        jnp.sum(jnp.where(expert_lane == first + j, gates, 0.0), axis=1, keepdims=True)
        for j in range(local)
    ]
    lane = jnp.arange(width, dtype=jnp.int32)[None, :]
    weight = jnp.where(lane < local * seg + shared, 1.0, 0.0)
    for j in range(local):
        weight = jnp.where((lane >= j * seg) & (lane < (j + 1) * seg), cols[j], weight)
    gate, up = both[:, :width], both[:, width:]
    logistic = jax.nn.sigmoid(gate)
    silu = gate * logistic
    hidden = silu * up
    scaled = (hidden * weight).astype(BF16)
    d_hidden = mm(grads, down_t)
    product = hidden * d_hidden
    d_gates = jnp.zeros(gates.shape, F32)
    for j in range(local):
        d_gates = d_gates + jnp.where(
            expert_lane == first + j,
            jnp.sum(product[:, j * seg : (j + 1) * seg], axis=1, keepdims=True),
            0.0,
        )
    d_hidden = d_hidden * weight
    d_gate = d_hidden * up * (logistic * (1.0 + gate * (1.0 - logistic)))
    d_up = d_hidden * silu
    d_both = jnp.concatenate([d_gate, d_up], axis=1).astype(BF16)
    out = mm(scaled, down).astype(BF16)
    d_rows = mm(d_both, gate_up_t).astype(BF16)
    return out, d_rows, scaled, d_both, d_gates


def body(
    tokens,
    segments,
    routes,
    cotangent,
    attn_gain,
    w_query,
    w_latent,
    latent_gain,
    w_expand,
    w_output,
    ffn_gain,
    w_router,
    w_shared_gate,
    w_shared_up,
    w_shared_down,
    w_expert_gate,
    w_expert_up,
    w_expert_down,
):
    own_rows, width = tokens.shape
    peers = lax.axis_size("expert")
    group_len = segments.shape[0]
    experts = w_router.shape[1]
    local, _, ff = w_expert_gate.shape
    rows_dev = w_query.shape[0]
    heads = w_query.shape[1] // (NOPE + ROPE)
    half = ROPE // 2
    rank_dev = w_expand.shape[0]
    expand_cols = w_expand.shape[1]
    value_cols = heads * V_HEAD
    query_cols = heads * (NOPE + ROPE)
    me_e = lax.axis_index("expert")
    me_s = lax.axis_index("shard")
    offset = me_s * own_rows
    score_scale = (NOPE + ROPE) ** (-0.5)
    shared_dev = w_shared_gate.shape[1]
    shared = shared_dev // peers

    token_group = gather(tokens, "shard")
    q3 = w_query.reshape(rows_dev, heads, NOPE + ROPE)
    query_parts = jnp.concatenate(
        [
            q3[..., :NOPE].reshape(rows_dev, -1),
            q3[..., NOPE : NOPE + half].reshape(rows_dev, -1),
            q3[..., NOPE + half :].reshape(rows_dev, -1),
        ],
        axis=1,
    )
    folds = rows_dev // rank_dev
    fold_cols = expand_cols // folds
    gain_latent_col = jnp.pad(latent_gain, (0, rows_dev - rank_dev))
    few = pad_to(KV_RANK + ROPE + experts + 3, LANES)
    few_pack = jnp.concatenate(
        [
            w_latent,
            w_router,
            attn_gain[:, None],
            ffn_gain[:, None],
            gain_latent_col[:, None],
            jnp.zeros((rows_dev, few - KV_RANK - ROPE - experts - 3), BF16),
        ],
        axis=1,
    )
    pack = jnp.concatenate(
        [query_parts, w_output.T, w_expand.reshape(rows_dev, fold_cols), few_pack], axis=1
    )
    pack = gather(pack, "expert")
    at = [0, query_cols, query_cols + value_cols, query_cols + value_cols + fold_cols]
    query_w = pack[:, at[0] : at[1]]
    output_t = pack[:, at[1] : at[2]]
    expand_w = pack[:, at[2] : at[3]].reshape(KV_RANK, expand_cols)
    few_all = pack[:, at[3] :]
    base = KV_RANK + ROPE
    latent_w = few_all[:, :base]
    router_w = few_all[:, base : base + experts]
    gain_attn = few_all[:, base + experts].astype(F32)
    gain_ffn = few_all[:, base + experts + 1].astype(F32)
    gain_latent = few_all[:, base + experts + 2].reshape(peers, rows_dev)[:, :rank_dev].reshape(-1).astype(F32)

    shared_pack = jnp.concatenate(
        [
            w_shared_gate.reshape(rows_dev, peers, shared),
            w_shared_up.reshape(rows_dev, peers, shared),
            w_shared_down.T.reshape(rows_dev, peers, shared),
        ],
        axis=2,
    ).transpose(1, 0, 2)
    shared_all = lax.all_to_all(shared_pack, "expert", 0, 0, tiled=True).reshape(width, 3 * shared)

    lane_experts = jnp.arange(experts, dtype=jnp.int32)
    routed_own = jnp.any(routes[:, :, None] == lane_experts[None, None, :], axis=1)
    routed_own_low = routed_own.astype(BF16)
    routed_all = gather(routed_own_low, BOTH)

    token_float = token_group.astype(F32)
    normed_in = (token_float * inverse_rms(token_float) * gain_attn).astype(BF16)
    cos_group, sin_group = angles(positions(segments), ROPE)
    latent_raw = mm(normed_in, latent_w)
    compressed = latent_raw[:, :KV_RANK]
    scale_latent = inverse_rms(compressed)
    latent_use = (compressed * scale_latent * gain_latent).astype(BF16)
    key_a = latent_raw[:, KV_RANK : KV_RANK + half]
    key_b = latent_raw[:, KV_RANK + half :]
    rope_key = jnp.concatenate(
        [key_a * cos_group - key_b * sin_group, key_b * cos_group + key_a * sin_group], axis=1
    ).astype(BF16)
    query_raw = mm(normed_in, query_w)
    cos_heads = jnp.tile(cos_group, (1, heads))
    sin_heads = jnp.tile(sin_group, (1, heads))
    nope_cols = heads * NOPE
    rope_cols = heads * half
    query_a = query_raw[:, nope_cols : nope_cols + rope_cols]
    query_b = query_raw[:, nope_cols + rope_cols :]
    query_nope = query_raw[:, :nope_cols].astype(BF16).reshape(group_len, heads, NOPE)
    query_rope = jnp.concatenate(
        [
            (query_a * cos_heads - query_b * sin_heads).reshape(group_len, heads, half),
            (query_b * cos_heads + query_a * sin_heads).reshape(group_len, heads, half),
        ],
        axis=2,
    ).astype(BF16)
    expanded = mm(latent_use, expand_w).astype(BF16).reshape(group_len, heads, NOPE + V_HEAD)
    key_nope = expanded[..., :NOPE]
    value_heads = expanded[..., NOPE:]
    index = jnp.arange(group_len, dtype=jnp.int32)
    allowed = (index[None, :] <= index[:, None]) & (
        (segments[None, :] == 0) | (segments[None, :] == segments[:, None])
    )

    def es(spec, *values):
        return jnp.einsum(spec, *values, preferred_element_type=F32)

    scores = es("qhd,khd->hqk", query_nope, key_nope) + es("qhd,kd->hqk", query_rope, rope_key)
    scores = jnp.where(allowed[None], scores * score_scale, -1e30)
    raised = jnp.exp(scores - jnp.max(scores, axis=-1, keepdims=True))
    soft = raised / jnp.sum(raised, axis=-1, keepdims=True)
    soft_low = soft.astype(BF16)
    attn_mixed = es("hqk,khd->qhd", soft_low, value_heads).astype(BF16).reshape(group_len, value_cols)
    attn_part = mm_t(attn_mixed, output_t).astype(BF16)
    attn_term = total(attn_part, "shard").astype(F32)
    own_float = tokens.astype(F32)
    hidden_one = own_float + attn_term
    scale_ffn = inverse_rms(hidden_one)
    normed_ffn = (hidden_one * scale_ffn * gain_ffn).astype(BF16)
    logits = mm(normed_ffn, router_w)
    masked = jnp.where(routed_own, logits, -1e30)
    lifted = jnp.where(routed_own, jnp.exp(masked - jnp.max(masked, axis=1, keepdims=True)), 0.0)
    gates = lifted / jnp.sum(lifted, axis=1, keepdims=True)

    seg = pad_to(ff, LANES)
    last = pad_to(shared + experts, LANES)
    shared_gate_w = shared_all[:, :shared]
    shared_up_w = shared_all[:, shared : 2 * shared]
    shared_down_t = shared_all[:, 2 * shared :]
    segs = [seg] * local + [last]
    gate_side = padded(
        [*(w_expert_gate[j] for j in range(local)), jnp.concatenate([shared_gate_w, router_w], axis=1)], segs, 1
    )
    gate_side_zero = padded([*(w_expert_gate[j] for j in range(local)), shared_gate_w], segs, 1)
    up_side = padded([*(w_expert_up[j] for j in range(local)), shared_up_w], segs, 1)
    gate_up = jnp.concatenate([gate_side, up_side], axis=1)
    gate_up_t = jnp.concatenate([gate_side_zero, up_side], axis=1).T
    down = padded([*(w_expert_down[j] for j in range(local)), shared_down_t.T], segs, 0)
    down_t = down.T
    chunks = max(1, own_rows * lax.axis_size(BOTH) // 4096)
    per = own_rows // chunks
    outs, d_rows_own, d_gates_own = [], [], []
    grad_gate_up = grad_down = 0.0
    for c in range(chunks):
        pick = slice(c * per, (c + 1) * per)
        rows_c = gather(normed_ffn[pick], BOTH)
        grad_c = gather(cotangent[pick], BOTH)
        routed_c = routed_all.reshape(-1, own_rows, experts)[:, pick].reshape(-1, experts)
        out, d_rows, scaled, d_both, d_gates = ffn_block(
            rows_c, grad_c, routed_c, gate_up, gate_up_t, down, down_t,
            (seg, shared, experts, local), me_e * local,
        )
        outs.append(total(out, BOTH))
        d_rows_own.append(total(d_rows, BOTH))
        d_gates_own.append(total(d_gates, BOTH))
        grad_gate_up = grad_gate_up + t_mm(rows_c, d_both)
        grad_down = grad_down + t_mm(scaled, grad_c)
    ffn_out = jnp.concatenate(outs, axis=0).astype(F32)
    d_normed = jnp.concatenate(d_rows_own, axis=0).astype(F32)
    d_gates = jnp.concatenate(d_gates_own, axis=0)
    block_out = (hidden_one + ffn_out).astype(BF16)
    side = down.shape[0]
    grad_expert_gate = jnp.stack([grad_gate_up[:, j * seg : j * seg + ff] for j in range(local)])
    grad_expert_up = jnp.stack([grad_gate_up[:, side + j * seg : side + j * seg + ff] for j in range(local)])
    grad_expert_down = jnp.stack([grad_down[j * seg : j * seg + ff] for j in range(local)])
    tail = local * seg
    shared_back = jnp.concatenate(
        [
            grad_gate_up[:, tail : tail + shared].astype(BF16),
            grad_gate_up[:, side + tail : side + tail + shared].astype(BF16),
            grad_down[tail : tail + shared].T.astype(BF16),
        ],
        axis=1,
    ).reshape(peers, rows_dev, 3 * shared)
    shared_home = lax.all_to_all(shared_back, "expert", 0, 0, tiled=True).transpose(1, 0, 2).astype(F32)
    grad_shared_gate = shared_home[..., :shared].reshape(rows_dev, shared_dev)
    grad_shared_up = shared_home[..., shared : 2 * shared].reshape(rows_dev, shared_dev)
    grad_shared_down = shared_home[..., 2 * shared :].reshape(rows_dev, shared_dev).T

    grad_in = cotangent.astype(F32)
    d_logits = (gates * (d_gates - jnp.sum(gates * d_gates, axis=1, keepdims=True))).astype(BF16)
    d_normed = d_normed + mm_t(d_logits, router_w)
    grad_router = t_mm(normed_ffn, d_logits)
    d_norm, grad_gain_ffn = norm_back(hidden_one, scale_ffn, gain_ffn, d_normed)
    d_hidden_one = grad_in + d_norm
    d_attn_group = gather(d_hidden_one.astype(BF16), "shard")
    grad_output_t = t_mm(d_attn_group, attn_mixed)
    d_mixed = mm(d_attn_group, output_t).astype(BF16).reshape(group_len, heads, V_HEAD)
    d_soft = es("qhd,khd->hqk", d_mixed, value_heads)
    d_values = es("hqk,qhd->khd", soft_low, d_mixed)
    d_scores = (score_scale * soft * (d_soft - jnp.sum(soft * d_soft, axis=-1, keepdims=True))).astype(BF16)
    d_query_nope = es("hqk,khd->qhd", d_scores, key_nope).reshape(group_len, nope_cols)
    d_query_rope = es("hqk,kd->qhd", d_scores, rope_key)
    d_key_nope = es("hqk,qhd->khd", d_scores, query_nope)
    d_key_rope = es("hqk,qhd->kd", d_scores, query_rope)
    d_expanded = jnp.concatenate([d_key_nope, d_values], axis=-1).reshape(group_len, expand_cols).astype(BF16)
    grad_expand = t_mm(latent_use, d_expanded)
    d_latent_use = mm_t(d_expanded, expand_w)
    d_compressed, grad_gain_latent = norm_back(compressed, scale_latent, gain_latent, d_latent_use)
    d_key_a, d_key_b = d_key_rope[:, :half], d_key_rope[:, half:]
    d_latent = jnp.concatenate(
        [
            d_compressed,
            d_key_a * cos_group + d_key_b * sin_group,
            d_key_b * cos_group - d_key_a * sin_group,
        ],
        axis=1,
    ).astype(BF16)
    d_a = d_query_rope[..., :half].reshape(group_len, rope_cols)
    d_b = d_query_rope[..., half:].reshape(group_len, rope_cols)
    d_query = jnp.concatenate(
        [d_query_nope, d_a * cos_heads + d_b * sin_heads, d_b * cos_heads - d_a * sin_heads], axis=1
    ).astype(BF16)
    grad_query = t_mm(normed_in, d_query)
    grad_latent = t_mm(normed_in, d_latent)
    d_normed_in = total((mm_t(d_query, query_w) + mm_t(d_latent, latent_w)).astype(BF16), "shard").astype(F32)
    d_token, grad_gain_attn = norm_back(own_float, inverse_rms(own_float), gain_attn, d_normed_in)
    tokens_grad = d_hidden_one + d_token

    latent_cols = jnp.pad(grad_gain_latent.reshape(peers, rank_dev), ((0, 0), (0, rows_dev - rank_dev))).reshape(-1)
    few_back = jnp.concatenate(
        [
            grad_latent,
            grad_router,
            grad_gain_attn[:, None],
            grad_gain_ffn[:, None],
            latent_cols[:, None],
            jnp.zeros((width, few - base - experts - 3), F32),
        ],
        axis=1,
    ).astype(BF16)
    back = jnp.concatenate(
        [
            grad_query.astype(BF16),
            grad_output_t.astype(BF16),
            grad_expand.reshape(width, fold_cols).astype(BF16),
            few_back,
        ],
        axis=1,
    )
    home = total(back, "expert").astype(F32)
    few_home = lax.psum(home[:, at[3] :].astype(BF16), "shard").astype(F32)
    gq = home[:, : at[1]]
    grad_query_own = jnp.concatenate(
        [
            gq[:, :nope_cols].reshape(rows_dev, heads, NOPE),
            gq[:, nope_cols : nope_cols + rope_cols].reshape(rows_dev, heads, half),
            gq[:, nope_cols + rope_cols :].reshape(rows_dev, heads, half),
        ],
        axis=2,
    ).reshape(rows_dev, query_cols)
    return (
        block_out,
        tokens_grad,
        few_home[:, base + experts],
        grad_query_own,
        few_home[:, :base],
        few_home[:rank_dev, base + experts + 2],
        home[:, at[2] : at[3]].reshape(rank_dev, expand_cols),
        home[:, at[1] : at[2]].T,
        few_home[:, base + experts + 1],
        few_home[:, base : base + experts],
        grad_shared_gate,
        grad_shared_up,
        grad_shared_down,
        grad_expert_gate,
        grad_expert_up,
        grad_expert_down,
    )


def solution(mesh):
    rows = P(("expert", "shard"), None)
    return jax.shard_map(
        body,
        mesh=mesh,
        in_specs=(
            rows,
            P("expert"),
            rows,
            rows,
            P("expert"),
            P("expert", "shard"),
            P("expert", None),
            P("expert"),
            P("expert", "shard"),
            P("shard", "expert"),
            P("expert"),
            P("expert", None),
            P("expert", "shard"),
            P("expert", "shard"),
            P("shard", "expert"),
            P("expert", None, "shard"),
            P("expert", None, "shard"),
            P("expert", "shard", None),
        ),
        out_specs=(
            rows,
            rows,
            P("expert"),
            P("expert", "shard"),
            P("expert", None),
            P("expert"),
            P("expert", "shard"),
            P("shard", "expert"),
            P("expert"),
            P("expert", None),
            P("expert", "shard"),
            P("expert", "shard"),
            P("shard", "expert"),
            P("expert", None, "shard"),
            P("expert", None, "shard"),
            P("expert", "shard", None),
        ),
        check_vma=False,
    )
```

```python
import jax
import jax.numpy as jnp
from jax import lax
from jax.experimental import pallas as pl
from jax.experimental.pallas import tpu as pltpu
from jax.sharding import PartitionSpec as P

NOPE = 128
ROPE = 64
V_HEAD = 128
KV_RANK = 512
TOP = 6
LANES = 128

epsilon = 1e-06
F32 = jnp.float32
BF16 = jnp.bfloat16


def pad_to(n, m):
    return -(-n // m) * m


def angles(places, width):
    half_width = width // 2
    spacing = 10000.0 ** (-2.0 * jnp.arange(half_width, dtype=F32) / width)
    turned = places.astype(F32)[:, None] * spacing[None, :]
    return (jnp.cos(turned), jnp.sin(turned))


def positions(segment):
    indices = jnp.arange(segment.shape[0], dtype=jnp.int32)
    prompt_len = jnp.sum((segment == 0).astype(jnp.int32))
    earlier = jnp.sum((segment[None, :] < segment[:, None]).astype(jnp.int32), axis=1)
    return jnp.where(segment == 0, indices, prompt_len + indices - earlier)


def inverse_rms(values):
    return lax.rsqrt(jnp.mean(values * values, axis=-1, keepdims=True) + epsilon)


def norm_back(values, scaling, gain, incoming):
    weighted = incoming * gain
    inner = jnp.mean(weighted * values, axis=-1, keepdims=True)
    return (
        scaling * weighted - values * scaling**3 * inner,
        jnp.sum(incoming * values * scaling, axis=0),
    )


def dot(a, b, dims):
    return lax.dot_general(a, b, (dims, ((), ())), preferred_element_type=F32)


def mm(a, b):
    return dot(a, b, ((1,), (0,)))


def mm_t(a, b):
    return dot(a, b, ((1,), (1,)))


def t_mm(a, b):
    return dot(a, b, ((0,), (0,)))


BOTH = ("expert", "shard")


def add(a, b):
    return (a.astype(F32) + b.astype(F32)).astype(BF16)


def padded(parts, widths, dim):
    out = []
    for part, width in zip(parts, widths):
        pads = [(0, 0)] * part.ndim
        pads[dim] = (0, width - part.shape[dim])
        out.append(jnp.pad(part, pads))
    return jnp.concatenate(out, axis=dim)


def routes_of(peers, shards):
    def table(step):
        return [
            (e * shards + s, step(e, s)[0] * shards + step(e, s)[1])
            for e in range(peers)
            for s in range(shards)
        ]

    ring = peers // 2
    return {
        "y": table(lambda e, s: (e ^ 1, s)),
        "x": table(lambda e, s: (e, s ^ 2)),
        "pair": table(lambda e, s: (e, s ^ 1)),
        "ring": table(lambda e, s: ((e // 2 + 1) % ring * 2 + e % 2, s)),
    }


def ffn_kernel(
    local, segs_per, n_seg, steps, width,
    first_ref, x0, x1, g0, g1, router, wg, wu, wdt,
    dx_keep, dx_send, out_keep, out_send, x_all, g_all, hs_all, dg_all, du_all,
    acc_out, acc_dx, gates_s, dgates_s,
):
    j = pl.program_id(0)
    half = x0.shape[0]
    slot = half // 2
    block = wg.shape[1]
    x = jnp.concatenate([x0[...], x1[...]], axis=0)
    g_in = jnp.concatenate([g0[:, :width], g1[:, :width]], axis=0)
    first = first_ref[0]
    lane = lax.broadcasted_iota(jnp.int32, (1, LANES), 1)

    @pl.when(j == 0)
    def _():
        logits = mm(x, router[...])
        routed = jnp.concatenate([g0[:, width:], g1[:, width:]], axis=0) > 0
        masked = jnp.where(routed, logits, -1e30)
        raised = jnp.where(routed, jnp.exp(masked - jnp.max(masked, axis=1, keepdims=True)), 0.0)
        gates_s[...] = raised / jnp.sum(raised, axis=1, keepdims=True)
        dgates_s[...] = jnp.zeros_like(dgates_s)
        acc_out[...] = jnp.zeros_like(acc_out)
        acc_dx[...] = jnp.zeros_like(acc_dx)
        x_all[0] = x
        g_all[0] = g_in

    gates = gates_s[...]
    wanted, columns = [], []
    for part in range(2):
        expert = lax.rem(2 * j + part, n_seg) // segs_per
        want = jnp.where(expert < local, first + expert, -1)
        column = jnp.sum(jnp.where(lane == want, gates, 0.0), axis=1, keepdims=True)
        wanted.append(want)
        columns.append(jnp.where(expert < local, column, 1.0))
    lane_block = lax.broadcasted_iota(jnp.int32, (1, block), 1)
    column = jnp.where(lane_block < LANES, columns[0], columns[1])
    gate, up, d_hidden = mm(x, wg[...]), mm(x, wu[...]), mm(g_in, wdt[...])
    logistic = 1.0 / (1.0 + jnp.exp(-gate))
    silu = gate * logistic
    hidden = silu * up
    scaled = (hidden * column).astype(BF16)
    product = hidden * d_hidden
    for part in range(2):
        dots = jnp.sum(product[:, part * LANES : (part + 1) * LANES], axis=1, keepdims=True)
        dgates_s[...] += jnp.where(lane == wanted[part], dots, 0.0)
    d_hidden = d_hidden * column
    d_gate = (d_hidden * up * (logistic * (1.0 + gate * (1.0 - logistic)))).astype(BF16)
    d_up = (d_hidden * silu).astype(BF16)
    hs_all[0], dg_all[0], du_all[0] = scaled, d_gate, d_up
    acc_out[...] += mm_t(scaled, wdt[...])
    acc_dx[...] += mm_t(d_gate, wg[...]) + mm_t(d_up, wu[...])

    @pl.when(j == steps - 1)
    def _():
        dx_keep[:, :width] = acc_dx[:half].astype(BF16)
        dx_send[:, :width] = acc_dx[half:].astype(BF16)
        dx_keep[:, width:] = dgates_s[:half].astype(BF16)
        dx_send[:, width:] = dgates_s[half:].astype(BF16)
        out_keep[:slot] = acc_out[:slot].astype(BF16)
        out_send[:slot] = acc_out[slot:half].astype(BF16)
        out_keep[slot:] = acc_out[half : half + slot].astype(BF16)
        out_send[slot:] = acc_out[half + slot :].astype(BF16)


def ffn_plane(first, rows, grads, router, weights, local, plane, planes, kept):
    half, width = rows[0].shape
    hid = weights[0].shape[1]
    block = 2 * LANES
    steps = hid // block
    n_seg = hid // LANES // 2
    segs_per = (n_seg - 1) // local

    def fixed(*shape):
        return pl.BlockSpec(shape, lambda j: (0,) * len(shape), pipeline_mode=pl.Buffered(1))

    def whole(*shape):
        return pl.BlockSpec(shape, lambda j: (0,) * len(shape))

    columns = pl.BlockSpec((width, block), lambda j: (0, j))
    in_specs = [
        pl.BlockSpec(memory_space=pltpu.SMEM),
        fixed(half, width), fixed(half, width), fixed(half, width + LANES), fixed(half, width + LANES),
        fixed(width, LANES), columns, columns, columns,
    ]
    args = [first, *rows, *grads, router, *weights]
    plain = len(args)
    aliases = {}
    if kept is not None:
        in_specs += [pl.BlockSpec(memory_space=pl.ANY)] * len(kept)
        args += list(kept)
        aliases = {plain + i: 4 + i for i in range(len(kept))}
    plane_rows = pl.BlockSpec((1, 2 * half, width), lambda j: (plane, 0, 0))
    plane_hidden = pl.BlockSpec((1, 2 * half, block), lambda j: (plane, 0, j))
    shape = jax.ShapeDtypeStruct
    out_shape = (
        [shape((half, width + LANES), BF16)] * 2
        + [shape((half, width), BF16)] * 2
        + [shape((planes, 2 * half, width), BF16)] * 2
        + [shape((planes, 2 * half, hid), BF16)] * 3
    )
    out_specs = [whole(half, width + LANES)] * 2 + [whole(half, width)] * 2 + [plane_rows] * 2 + [plane_hidden] * 3

    def kernel(*refs):
        ffn_kernel(local, segs_per, n_seg, steps, width, *refs[:plain], *refs[len(args) :])

    outs = pl.pallas_call(
        kernel,
        grid=(steps,),
        in_specs=in_specs,
        out_specs=out_specs,
        out_shape=out_shape,
        scratch_shapes=[pltpu.VMEM((2 * half, width), F32)] * 2 + [pltpu.VMEM((2 * half, LANES), F32)] * 2,
        input_output_aliases=aliases,
        compiler_params=pltpu.CompilerParams(
            vmem_limit_bytes=56 * 2**20, dimension_semantics=("arbitrary",)
        ),
        cost_estimate=pl.CostEstimate(
            flops=24 * half * width * hid,
            bytes_accessed=6 * width * hid + 16 * half * width,
            transcendentals=2 * half * hid,
        ),
    )(*args)
    return outs[:4], outs[4:]


def body(
    tokens,
    segments,
    routes,
    cotangent,
    attn_gain,
    w_query,
    w_latent,
    latent_gain,
    w_expand,
    w_output,
    ffn_gain,
    w_router,
    w_shared_gate,
    w_shared_up,
    w_shared_down,
    w_expert_gate,
    w_expert_up,
    w_expert_down,
):
    own_rows, width = tokens.shape
    peers = lax.axis_size("expert")
    shards = lax.axis_size("shard")
    ring = peers // 2
    group_len = segments.shape[0]
    experts = w_router.shape[1]
    local, _, ff = w_expert_gate.shape
    rows_dev = w_query.shape[0]
    heads = w_query.shape[1] // (NOPE + ROPE)
    half = ROPE // 2
    rank_dev = w_expand.shape[0]
    expand_cols = w_expand.shape[1]
    value_cols = heads * V_HEAD
    query_cols = heads * (NOPE + ROPE)
    me_e = lax.axis_index("expert")
    me_s = lax.axis_index("shard")
    score_scale = (NOPE + ROPE) ** (-0.5)
    shared_dev = w_shared_gate.shape[1]
    shared = shared_dev // peers
    tables = routes_of(peers, shards)

    def send(values, way):
        return lax.ppermute(values, BOTH, tables[way])

    def group_gather(block):
        near = jnp.concatenate([block, send(block, "x")], axis=0)
        return jnp.concatenate([near, send(near, "pair")], axis=0)

    def group_sum(parts):
        n = parts.shape[0]
        near = add(parts[: n // 2], send(parts[n // 2 :], "pair"))
        return add(near[: n // 4], send(near[n // 4 :], "x"))

    def expert_at(k):
        return lax.rem(me_e // 2 + ring - k, ring) * 2 + lax.rem(me_e, 2)

    def expert_gather(block):
        n = block.shape[0]
        whole = jnp.zeros((n * peers, block.shape[1]), block.dtype)
        for k in range(ring):
            other = send(block, "y")
            whole = lax.dynamic_update_slice_in_dim(whole, block, expert_at(k) * n, 0)
            whole = lax.dynamic_update_slice_in_dim(whole, other, (expert_at(k) ^ 1) * n, 0)
            if k < ring - 1:
                block = send(block, "ring")
        return whole

    def ring_sum(plane_part):
        total = None
        for k in [*range(1, ring), 0]:
            part = plane_part(k)
            total = part if total is None else add(part, send(total, "ring"))
        return total

    def expert_sum(parts):
        n = parts.shape[0] // peers

        def plane_part(k):
            keep = lax.dynamic_slice_in_dim(parts, expert_at(k) * n, n, 0)
            away = lax.dynamic_slice_in_dim(parts, (expert_at(k) ^ 1) * n, n, 0)
            return add(keep, send(away, "y"))

        return ring_sum(plane_part)

    def ways(k):
        return ("y", "x") if k % 2 == 0 else ("x", "y")

    def plane_gather(block):
        planes = []
        for k in range(ring):
            first, second = ways(k)
            near = jnp.concatenate([block, send(block, first)], axis=0)
            planes.append((near, send(near, second)))
            if k < ring - 1:
                block = send(block, "ring")
        return planes

    token_group = group_gather(tokens)
    q3 = w_query.reshape(rows_dev, heads, NOPE + ROPE)
    query_parts = jnp.concatenate(
        [
            q3[..., :NOPE].reshape(rows_dev, -1),
            q3[..., NOPE : NOPE + half].reshape(rows_dev, -1),
            q3[..., NOPE + half :].reshape(rows_dev, -1),
        ],
        axis=1,
    )
    folds = rows_dev // rank_dev
    fold_cols = expand_cols // folds
    pack = jnp.concatenate([query_parts, w_output.T, w_expand.reshape(rows_dev, fold_cols)], axis=1)
    pack = expert_gather(pack)
    at = [0, query_cols, query_cols + value_cols, query_cols + value_cols + fold_cols]
    query_w = pack[:, at[0] : at[1]]
    output_t = pack[:, at[1] : at[2]]
    expand_w = pack[:, at[2] : at[3]].reshape(KV_RANK, expand_cols)

    base = KV_RANK + ROPE
    few = pad_to(base + experts, LANES)
    few_rows = rows_dev + 32
    part_rows = few_rows // shards
    gains = jnp.concatenate([attn_gain, ffn_gain, latent_gain])
    few_pack = jnp.pad(jnp.concatenate([w_latent, w_router], axis=1), ((0, 32), (0, few - base - experts)))
    few_pack = few_pack.at[rows_dev, : gains.shape[0]].set(gains)
    few_part = lax.dynamic_slice_in_dim(few_pack, me_s * part_rows, part_rows, 0)
    few_all = lax.all_gather(few_part, BOTH, axis=0, tiled=True).reshape(peers, few_rows, few)
    latent_w = few_all[:, :rows_dev, :base].reshape(width, base)
    router_w = few_all[:, :rows_dev, base : base + experts].reshape(width, experts)
    gain_rows = few_all[:, rows_dev].astype(F32)
    gain_attn = gain_rows[:, :rows_dev].reshape(-1)
    gain_ffn = gain_rows[:, rows_dev : 2 * rows_dev].reshape(-1)
    gain_latent = gain_rows[:, 2 * rows_dev : 2 * rows_dev + rank_dev].reshape(-1)

    shared_pack = jnp.concatenate(
        [
            w_shared_gate.reshape(rows_dev, peers, shared),
            w_shared_up.reshape(rows_dev, peers, shared),
            w_shared_down.T.reshape(rows_dev, peers, shared),
        ],
        axis=2,
    ).transpose(1, 0, 2)
    shared_all = lax.all_to_all(shared_pack, "expert", 0, 0, tiled=True).reshape(width, 3 * shared)

    seg = pad_to(ff, LANES)
    segs = [seg] * local + [pad_to(shared, LANES)]
    side = sum(segs)
    sides = []
    for i, parts in enumerate(
        (
            [w_expert_gate[j] for j in range(local)],
            [w_expert_up[j] for j in range(local)],
            [w_expert_down[j].T for j in range(local)],
        )
    ):
        own = padded([*parts, shared_all[:, i * shared : (i + 1) * shared]], segs, 1)
        sides.append(jnp.concatenate([own, send(own, "pair")], axis=1))

    lane_experts = jnp.arange(experts, dtype=jnp.int32)
    routed_own = jnp.any(routes[:, :, None] == lane_experts[None, None, :], axis=1)
    grad_pack = jnp.concatenate(
        [cotangent, jnp.pad(routed_own.astype(BF16), ((0, 0), (0, LANES - experts)))], axis=1
    )
    grad_planes = plane_gather(grad_pack)

    def by_group(values):
        return jnp.concatenate(
            [lax.dynamic_slice_in_dim(values, (me_s ^ r) * own_rows, own_rows, 0) for r in (0, 2, 1, 3)], axis=0
        )

    index = by_group(jnp.arange(group_len, dtype=jnp.int32))
    segment = by_group(segments)
    cos_group, sin_group = angles(by_group(positions(segments)), ROPE)
    token_float = token_group.astype(F32)
    normed_in = (token_float * inverse_rms(token_float) * gain_attn).astype(BF16)
    latent_raw = mm(normed_in, latent_w)
    compressed = latent_raw[:, :KV_RANK]
    scale_latent = inverse_rms(compressed)
    latent_use = (compressed * scale_latent * gain_latent).astype(BF16)
    key_a = latent_raw[:, KV_RANK : KV_RANK + half]
    key_b = latent_raw[:, KV_RANK + half :]
    rope_key = jnp.concatenate(
        [key_a * cos_group - key_b * sin_group, key_b * cos_group + key_a * sin_group], axis=1
    ).astype(BF16)
    query_raw = mm(normed_in, query_w)
    cos_heads = jnp.tile(cos_group, (1, heads))
    sin_heads = jnp.tile(sin_group, (1, heads))
    nope_cols = heads * NOPE
    rope_cols = heads * half
    query_a = query_raw[:, nope_cols : nope_cols + rope_cols]
    query_b = query_raw[:, nope_cols + rope_cols :]
    query_nope = query_raw[:, :nope_cols].astype(BF16).reshape(group_len, heads, NOPE)
    query_rope = jnp.concatenate(
        [
            (query_a * cos_heads - query_b * sin_heads).reshape(group_len, heads, half),
            (query_b * cos_heads + query_a * sin_heads).reshape(group_len, heads, half),
        ],
        axis=2,
    ).astype(BF16)
    expanded = mm(latent_use, expand_w).astype(BF16).reshape(group_len, heads, NOPE + V_HEAD)
    key_nope = expanded[..., :NOPE]
    value_heads = expanded[..., NOPE:]
    allowed = (index[None, :] <= index[:, None]) & (
        (segment[None, :] == 0) | (segment[None, :] == segment[:, None])
    )

    def es(spec, *values):
        return jnp.einsum(spec, *values, preferred_element_type=F32)

    scores = es("qhd,khd->hqk", query_nope, key_nope) + es("qhd,kd->hqk", query_rope, rope_key)
    scores = jnp.where(allowed[None], scores * score_scale, -1e30)
    raised = jnp.exp(scores - jnp.max(scores, axis=-1, keepdims=True))
    soft = raised / jnp.sum(raised, axis=-1, keepdims=True)
    soft_low = soft.astype(BF16)
    attn_mixed = es("hqk,khd->qhd", soft_low, value_heads).astype(BF16).reshape(group_len, value_cols)
    attn_term = group_sum(mm_t(attn_mixed, output_t).astype(BF16)).astype(F32)
    own_float = tokens.astype(F32)
    hidden_one = own_float + attn_term
    scale_ffn = inverse_rms(hidden_one)
    normed_ffn = (hidden_one * scale_ffn * gain_ffn).astype(BF16)
    logits = mm(normed_ffn, router_w)
    masked = jnp.where(routed_own, logits, -1e30)
    lifted = jnp.where(routed_own, jnp.exp(masked - jnp.max(masked, axis=1, keepdims=True)), 0.0)
    gates = lifted / jnp.sum(lifted, axis=1, keepdims=True)

    router_pad = jnp.pad(router_w, ((0, 0), (0, LANES - experts)))
    first_expert = (me_e * local).astype(jnp.int32).reshape(1)
    row_planes = plane_gather(normed_ffn)
    plane_outs, kept = [], None
    for k in range(ring):
        outs, kept = ffn_plane(
            first_expert, row_planes[k], grad_planes[k], router_pad, sides, local, k, ring, kept
        )
        plane_outs.append(outs)

    def halves(keep, away, way_one, way_two):
        near = add(keep, send(away, way_one))
        n = near.shape[0] // 2
        return add(near[:n], send(near[n:], way_two))

    def d_rows_part(k):
        first, second = ways(k)
        return halves(plane_outs[k][0], plane_outs[k][1], second, first)

    def out_part(k):
        first, second = ways(k)
        return halves(plane_outs[k][2], plane_outs[k][3], first, second)

    d_rows = ring_sum(d_rows_part)
    ffn_out = ring_sum(out_part).astype(F32)
    d_normed = d_rows[:, :width].astype(F32)
    d_gates = d_rows[:, width : width + experts].astype(F32)
    block_out = (hidden_one + ffn_out).astype(BF16)

    x_all, g_all, hs_all, dg_all, du_all = (v.reshape(-1, v.shape[-1]) for v in kept)
    from_pair = [
        send(t_mm(x_all, dg_all[:, side:]).astype(BF16), "pair"),
        send(t_mm(x_all, du_all[:, side:]).astype(BF16), "pair"),
        send(t_mm(hs_all[:, side:], g_all).astype(BF16), "pair"),
    ]
    grad_gate = t_mm(x_all, dg_all[:, :side]) + from_pair[0].astype(F32)
    grad_up = t_mm(x_all, du_all[:, :side]) + from_pair[1].astype(F32)
    grad_down = t_mm(hs_all[:, :side], g_all) + from_pair[2].astype(F32)
    grad_expert_gate = jnp.stack([grad_gate[:, j * seg : j * seg + ff] for j in range(local)])
    grad_expert_up = jnp.stack([grad_up[:, j * seg : j * seg + ff] for j in range(local)])
    grad_expert_down = jnp.stack([grad_down[j * seg : j * seg + ff] for j in range(local)])
    tail = local * seg
    shared_back = jnp.concatenate(
        [
            grad_gate[:, tail : tail + shared].astype(BF16),
            grad_up[:, tail : tail + shared].astype(BF16),
            grad_down[tail : tail + shared].T.astype(BF16),
        ],
        axis=1,
    ).reshape(peers, rows_dev, 3 * shared)
    shared_home = lax.all_to_all(shared_back, "expert", 0, 0, tiled=True).transpose(1, 0, 2).astype(F32)
    grad_shared_gate = shared_home[..., :shared].reshape(rows_dev, shared_dev)
    grad_shared_up = shared_home[..., shared : 2 * shared].reshape(rows_dev, shared_dev)
    grad_shared_down = shared_home[..., 2 * shared :].reshape(rows_dev, shared_dev).T

    grad_in = cotangent.astype(F32)
    d_logits = (gates * (d_gates - jnp.sum(gates * d_gates, axis=1, keepdims=True))).astype(BF16)
    d_normed = d_normed + mm_t(d_logits, router_w)
    grad_router = t_mm(normed_ffn, d_logits)
    d_norm, grad_gain_ffn = norm_back(hidden_one, scale_ffn, gain_ffn, d_normed)
    d_hidden_one = grad_in + d_norm
    d_attn_group = group_gather(d_hidden_one.astype(BF16))
    grad_output_t = t_mm(d_attn_group, attn_mixed).astype(BF16)
    d_mixed = mm(d_attn_group, output_t).astype(BF16).reshape(group_len, heads, V_HEAD)
    d_soft = es("qhd,khd->hqk", d_mixed, value_heads)
    d_values = es("hqk,qhd->khd", soft_low, d_mixed)
    d_scores = (score_scale * soft * (d_soft - jnp.sum(soft * d_soft, axis=-1, keepdims=True))).astype(BF16)
    d_query_nope = es("hqk,khd->qhd", d_scores, key_nope).reshape(group_len, nope_cols)
    d_query_rope = es("hqk,kd->qhd", d_scores, rope_key)
    d_key_nope = es("hqk,qhd->khd", d_scores, query_nope)
    d_key_rope = es("hqk,qhd->kd", d_scores, query_rope)
    d_expanded = jnp.concatenate([d_key_nope, d_values], axis=-1).reshape(group_len, expand_cols).astype(BF16)
    grad_expand = t_mm(latent_use, d_expanded)
    d_latent_use = mm_t(d_expanded, expand_w)
    d_compressed, grad_gain_latent = norm_back(compressed, scale_latent, gain_latent, d_latent_use)
    d_key_a, d_key_b = d_key_rope[:, :half], d_key_rope[:, half:]
    d_latent = jnp.concatenate(
        [
            d_compressed,
            d_key_a * cos_group + d_key_b * sin_group,
            d_key_b * cos_group - d_key_a * sin_group,
        ],
        axis=1,
    ).astype(BF16)
    d_a = d_query_rope[..., :half].reshape(group_len, rope_cols)
    d_b = d_query_rope[..., half:].reshape(group_len, rope_cols)
    d_query = jnp.concatenate(
        [d_query_nope, d_a * cos_heads + d_b * sin_heads, d_b * cos_heads - d_a * sin_heads], axis=1
    ).astype(BF16)
    grad_query = t_mm(normed_in, d_query)
    grad_latent = t_mm(normed_in, d_latent)
    d_normed_in = group_sum((mm_t(d_query, query_w) + mm_t(d_latent, latent_w)).astype(BF16)).astype(F32)
    d_token, grad_gain_attn = norm_back(own_float, inverse_rms(own_float), gain_attn, d_normed_in)
    tokens_grad = d_hidden_one + d_token

    back = jnp.concatenate(
        [grad_query.astype(BF16), grad_output_t, grad_expand.astype(BF16).reshape(width, fold_cols)], axis=1
    )
    home = expert_sum(back).astype(F32)
    gain_back = jnp.concatenate(
        [
            grad_gain_attn.reshape(peers, rows_dev),
            grad_gain_ffn.reshape(peers, rows_dev),
            grad_gain_latent.reshape(peers, rank_dev),
        ],
        axis=1,
    )
    few_back = jnp.concatenate([grad_latent, grad_router], axis=1).reshape(peers, rows_dev, base + experts)
    few_back = jnp.concatenate(
        [
            jnp.pad(few_back.astype(BF16), ((0, 0), (0, 0), (0, few - base - experts))),
            jnp.pad(gain_back.astype(BF16)[:, None], ((0, 0), (0, 31), (0, few - gain_back.shape[1]))),
        ],
        axis=1,
    ).reshape(peers * few_rows, few)
    few_home = lax.psum_scatter(few_back, BOTH, scatter_dimension=0, tiled=True)
    few_home = lax.all_gather(few_home, "shard", axis=0, tiled=True).astype(F32)
    gains_home = few_home[rows_dev]
    gq = home[:, : at[1]]
    grad_query_own = jnp.concatenate(
        [
            gq[:, :nope_cols].reshape(rows_dev, heads, NOPE),
            gq[:, nope_cols : nope_cols + rope_cols].reshape(rows_dev, heads, half),
            gq[:, nope_cols + rope_cols :].reshape(rows_dev, heads, half),
        ],
        axis=2,
    ).reshape(rows_dev, query_cols)
    return (
        block_out,
        tokens_grad,
        gains_home[:rows_dev],
        grad_query_own,
        few_home[:rows_dev, :base],
        gains_home[2 * rows_dev : 2 * rows_dev + rank_dev],
        home[:, at[2] : at[3]].reshape(rank_dev, expand_cols),
        home[:, at[1] : at[2]].T,
        gains_home[rows_dev : 2 * rows_dev],
        few_home[:rows_dev, base : base + experts],
        grad_shared_gate,
        grad_shared_up,
        grad_shared_down,
        grad_expert_gate,
        grad_expert_up,
        grad_expert_down,
    )


def solution(mesh):
    rows = P(("expert", "shard"), None)
    return jax.shard_map(
        body,
        mesh=mesh,
        in_specs=(
            rows,
            P("expert"),
            rows,
            rows,
            P("expert"),
            P("expert", "shard"),
            P("expert", None),
            P("expert"),
            P("expert", "shard"),
            P("shard", "expert"),
            P("expert"),
            P("expert", None),
            P("expert", "shard"),
            P("expert", "shard"),
            P("shard", "expert"),
            P("expert", None, "shard"),
            P("expert", None, "shard"),
            P("expert", "shard", None),
        ),
        out_specs=(
            rows,
            rows,
            P("expert"),
            P("expert", "shard"),
            P("expert", None),
            P("expert"),
            P("expert", "shard"),
            P("shard", "expert"),
            P("expert"),
            P("expert", None),
            P("expert", "shard"),
            P("expert", "shard"),
            P("shard", "expert"),
            P("expert", None, "shard"),
            P("expert", None, "shard"),
            P("expert", "shard", None),
        ),
        check_vma=False,
    )
```

```python
import jax
import jax.numpy as jnp
from jax import lax
from jax.experimental import pallas as pl
from jax.experimental.pallas import tpu as pltpu
from jax.sharding import PartitionSpec as P

NOPE = 128
ROPE = 64
V_HEAD = 128
KV_RANK = 512
TOP = 6
LANES = 128

epsilon = 1e-06
F32 = jnp.float32
BF16 = jnp.bfloat16


def pad_to(n, m):
    return -(-n // m) * m


def angles(places, width):
    half_width = width // 2
    spacing = 10000.0 ** (-2.0 * jnp.arange(half_width, dtype=F32) / width)
    turned = places.astype(F32)[:, None] * spacing[None, :]
    return (jnp.cos(turned), jnp.sin(turned))


def positions(segment):
    indices = jnp.arange(segment.shape[0], dtype=jnp.int32)
    prompt_len = jnp.sum((segment == 0).astype(jnp.int32))
    earlier = jnp.sum((segment[None, :] < segment[:, None]).astype(jnp.int32), axis=1)
    return jnp.where(segment == 0, indices, prompt_len + indices - earlier)


def inverse_rms(values):
    return lax.rsqrt(jnp.mean(values * values, axis=-1, keepdims=True) + epsilon)


def norm_back(values, scaling, gain, incoming):
    weighted = incoming * gain
    inner = jnp.mean(weighted * values, axis=-1, keepdims=True)
    return (
        scaling * weighted - values * scaling**3 * inner,
        jnp.sum(incoming * values * scaling, axis=0),
    )


def dot(a, b, dims):
    return lax.dot_general(a, b, (dims, ((), ())), preferred_element_type=F32)


def mm(a, b):
    return dot(a, b, ((1,), (0,)))


def mm_t(a, b):
    return dot(a, b, ((1,), (1,)))


def t_mm(a, b):
    return dot(a, b, ((0,), (0,)))


BOTH = ("expert", "shard")


def add(a, b):
    return (a.astype(F32) + b.astype(F32)).astype(BF16)


def routes_of(peers, shards):
    def table(step):
        return [
            (e * shards + s, step(e, s)[0] * shards + step(e, s)[1])
            for e in range(peers)
            for s in range(shards)
        ]

    ring = peers // 2

    def around(k):
        return table(lambda e, s: ((e // 2 + k) % ring * 2 + e % 2, s))

    return {
        "y": table(lambda e, s: (e ^ 1, s)),
        "x": table(lambda e, s: (e, s ^ 2)),
        "pair": table(lambda e, s: (e, s ^ 1)),
        "ring": around(1),
        **{k: around(k) for k in range(1 - ring, ring)},
    }


def spread(values, first, lane):
    kept = jnp.where((lane >= first) & (lane < first + ROPE // 2), values, 0.0)
    kept = kept + pltpu.roll(kept, ROPE // 2, 1)
    return kept + pltpu.roll(kept, ROPE, 1)


def attn_forward_kernel(
    heads, peers, score_scale,
    places, tokens, latent_x, latent_pair, cos, sin, index_c, index_r, segment_c, segment_r,
    small, mains,
    part_keep, part_send, normed_o, query_o, key_rope_o, expanded_o, soft_o, mixed_o, compressed_o, latent_o,
    gains, gain_latent, query_w, output_t, expand_w, extra_w, latent_w,
    *, gain_at,
):
    group = tokens.shape[0]
    rank = KV_RANK // peers
    rows = mains[0].shape[0]
    shards = latent_w.shape[0]
    cut = (query_w.shape[1], query_w.shape[1] + output_t.shape[1])
    for p in range(peers):
        to = pl.ds(pl.multiple_of(places[p] * rows, rows), rows)
        query_w[to, :] = mains[p][:, : cut[0]]
        output_t[to, :] = mains[p][:, cut[0] : cut[1]]
        expand_w[to, :] = mains[p][:, cut[1] :]
        at = slice(p * rows, (p + 1) * rows)
        latent_w[places[peers], to, :] = small[at, :LANES]
        extra_w[to, :] = small[at, LANES:]
        latent_w[places[peers + 1], to, :] = latent_x[at]
        latent_w[places[peers + 2], to, :] = latent_pair[0, at]
        latent_w[places[peers + 3], to, :] = latent_pair[1, at]
    block, at = gain_at // LANES * LANES, gain_at % LANES
    gains[...] = extra_w[:, block : block + LANES].astype(F32).T[at : at + 8]
    few_rows = [extra_w[p * rows : p * rows + rank, block : block + LANES] for p in range(peers)]
    gain_latent[...] = jnp.concatenate(few_rows, axis=0).astype(F32).T[at + 2 : at + 3]
    x = tokens[...].astype(F32)
    x = x * lax.rsqrt(jnp.mean(x * x, axis=1, keepdims=True) + epsilon) * gains[0:1]
    normed_o[...] = x.astype(BF16)
    normed = normed_o[...]
    lane = lax.broadcasted_iota(jnp.int32, (1, LANES), 1)
    c, s = cos[...], sin[...]
    raw = mm(normed, extra_w[:, :LANES])
    a, b = spread(raw, 0, lane), spread(raw, ROPE // 2, lane)
    key_rope_o[:, :LANES] = (a * c - b * s).astype(BF16)
    key_rope_o[:, LANES:] = (b * c + a * s).astype(BF16)
    for j in range(shards):
        compressed_o[:, j * LANES : (j + 1) * LANES] = mm(normed, latent_w[j])
    u = compressed_o[...]
    r = lax.rsqrt(jnp.mean(u * u, axis=1, keepdims=True) + epsilon)
    latent_o[...] = (u * r * gain_latent[...]).astype(BF16)
    q = mm(normed, query_w[...])
    nope = heads * NOPE
    query_o[:, :nope] = q[:, :nope].astype(BF16)
    a, b = q[:, nope : nope + LANES], q[:, nope + LANES :]
    query_o[:, nope : nope + LANES] = (a * c - b * s).astype(BF16)
    query_o[:, nope + LANES :] = (b * c + a * s).astype(BF16)
    allowed = (index_r[...] <= index_c[...]) & ((segment_r[...] == 0) | (segment_r[...] == segment_c[...]))
    lane2 = lax.rem(lax.broadcasted_iota(jnp.int32, (1, 2 * LANES), 1), LANES)
    for h in range(heads):
        w = jnp.concatenate(
            [expand_w[pl.ds((e * heads + h) * rank, rank), :] for e in range(peers)], axis=0
        )
        expanded_o[h] = mm(latent_o[...], w).astype(BF16)
        key_rope = jnp.where((lane2 >= h * ROPE // 2) & (lane2 < (h + 1) * ROPE // 2), key_rope_o[...], jnp.zeros((), BF16))
        scores = mm_t(query_o[:, h * NOPE : (h + 1) * NOPE], expanded_o[h, :, :NOPE]) + mm_t(query_o[:, nope:], key_rope)
        scores = jnp.where(allowed, scores * score_scale, -1e30)
        raised = jnp.exp(scores - jnp.max(scores, axis=1, keepdims=True))
        soft = raised * (1.0 / jnp.sum(raised, axis=1, keepdims=True))
        soft_o[h] = soft
        mixed_o[:, h * V_HEAD : (h + 1) * V_HEAD] = mm(soft.astype(BF16), expanded_o[h, :, NOPE:]).astype(BF16)
    half = group // 2
    part_keep[...] = mm_t(mixed_o[:half], output_t[...]).astype(BF16)
    part_send[...] = mm_t(mixed_o[half:], output_t[...]).astype(BF16)


def attn_backward_kernel(
    heads, peers, score_scale,
    places, d_attn, query_w, output_t, expand_w, extra_w, latent_w, gain_latent, cos, sin,
    normed, query, key_rope_all, expanded, soft_all, mixed, compressed, latent,
    normed_ffn, d_logits, tokens, g_gain_ffn,
    g_mains, near_keep, near_send, d_in_keep, d_in_send,
    g_all, g_few, d_query_s, d_latent_s, d_use_s,
    *, gain_at,
):
    group = d_attn.shape[0]
    rank = KV_RANK // peers
    shards = latent_w.shape[0]
    nope = heads * NOPE
    lane = lax.broadcasted_iota(jnp.int32, (1, LANES), 1)
    lane2 = lax.rem(lax.broadcasted_iota(jnp.int32, (1, 2 * LANES), 1), LANES)
    rows = g_mains[0].shape[0]
    cut = (query_w.shape[1], query_w.shape[1] + output_t.shape[1])
    width = d_attn.shape[1]
    strips = [slice(lo, lo + width // 4) for lo in range(0, width, width // 4)]
    value_cols = output_t.shape[1]
    for strip in strips:
        g_all[strip, :value_cols] = t_mm(d_attn[:, strip], mixed[...]).astype(BF16)
    d_mixed = mm(d_attn[...], output_t[...]).astype(BF16)
    d_query_rope = jnp.zeros((group, 2 * LANES), F32)
    d_key_rope = jnp.zeros((group, 2 * LANES), F32)
    for h in range(heads):
        mine = (lane2 >= h * ROPE // 2) & (lane2 < (h + 1) * ROPE // 2)
        key_rope = jnp.where(mine, key_rope_all[...], jnp.zeros((), BF16))
        soft = soft_all[h]
        d_out = d_mixed[:, h * V_HEAD : (h + 1) * V_HEAD]
        d_soft = mm_t(d_out, expanded[h, :, NOPE:])
        d_scores = score_scale * soft * (d_soft - jnp.sum(soft * d_soft, axis=1, keepdims=True))
        d_scores = d_scores.astype(BF16)
        d_query_s[:, h * NOPE : (h + 1) * NOPE] = mm(d_scores, expanded[h, :, :NOPE]).astype(BF16)
        d_query_rope = d_query_rope + mm(d_scores, key_rope)
        both = jnp.concatenate([query[:, h * NOPE : (h + 1) * NOPE], query[:, nope:]], axis=1)
        d_key = t_mm(d_scores, both)
        d_key_rope = d_key_rope + jnp.where(mine, d_key[:, NOPE:], 0.0)
        d_values = t_mm(soft.astype(BF16), d_out)
        d_expanded = jnp.concatenate([d_key[:, :NOPE], d_values], axis=1).astype(BF16)
        w = jnp.concatenate(
            [expand_w[pl.ds((e * heads + h) * rank, rank), :] for e in range(peers)], axis=0
        )
        g_w = t_mm(latent[...], d_expanded).astype(BF16)
        for e in range(peers):
            g_all[pl.ds((e * heads + h) * rank, rank), value_cols:] = g_w[e * rank : (e + 1) * rank]
        back = mm_t(d_expanded, w)
        if h == 0:
            d_use_s[...] = back
        else:
            d_use_s[...] += back
    for p in range(peers):
        g_mains[p][:, cut[0] :] = g_all[pl.ds(pl.multiple_of(places[p] * rows, rows), rows), :]
    c, s = cos[...], sin[...]
    a, b = d_query_rope[:, :LANES], d_query_rope[:, LANES:]
    d_query_s[:, nope : nope + LANES] = (a * c + b * s).astype(BF16)
    d_query_s[:, nope + LANES :] = (b * c - a * s).astype(BF16)
    u, n = compressed[...], d_use_s[...]
    r = lax.rsqrt(jnp.mean(u * u, axis=1, keepdims=True) + epsilon)
    weighted = n * gain_latent[...]
    inner = jnp.mean(weighted * u, axis=1, keepdims=True)
    g_gain_latent = jnp.sum(n * u * r, axis=0, keepdims=True)
    d_latent_s[...] = (r * weighted - u * (r * r * r * inner)).astype(BF16)

    def folded(v):
        v = v + pltpu.roll(v, ROPE // 2, 1)
        return v + pltpu.roll(v, ROPE, 1)

    a, b = folded(d_key_rope[:, :LANES]), folded(d_key_rope[:, LANES:])
    d_extra = jnp.where(
        lane < ROPE // 2, a * c + b * s, jnp.where(lane < ROPE, b * c - a * s, 0.0)
    ).astype(BF16)
    half = group // 2
    g_gain_attn = jnp.zeros((1, tokens.shape[1]), F32)
    fine = half // 2
    for lo in range(0, group, fine):
        part, to = slice(lo, lo + fine), (d_in_keep if lo < half else d_in_send).at[pl.ds(lo % half, fine)]
        total = mm_t(d_query_s[part], query_w[...]) + mm_t(d_extra[part], extra_w[:, :LANES])
        for j in range(shards):
            total = total + mm_t(d_latent_s[part, j * LANES : (j + 1) * LANES], latent_w[j])
        to[...] = total.astype(BF16)
        x = tokens[part].astype(F32)
        x = x * lax.rsqrt(jnp.mean(x * x, axis=1, keepdims=True) + epsilon)
        g_gain_attn = g_gain_attn + jnp.sum(total * x, axis=0, keepdims=True)
    for strip in strips:
        g_all[strip, :] = t_mm(normed[:, strip], d_query_s[...]).astype(BF16)
    wide = extra_w.shape[1] // LANES
    line = lax.broadcasted_iota(jnp.int32, (LANES, 1), 0)
    at_line = gain_at % LANES
    for j in range(wide):
        g_extra = t_mm(normed_ffn[...], d_logits[:, j * LANES : (j + 1) * LANES])
        if j == 0:
            g_extra = g_extra + t_mm(normed[...], d_extra)
        if j == gain_at // LANES:
            both = jnp.where(line == at_line, g_gain_attn, jnp.where(line == at_line + 1, g_gain_ffn[...], 0.0))
            g_extra = g_extra + both.T
        g_few[shards + j] = g_extra.astype(BF16)
    tall = jnp.where(line == at_line + 2, g_gain_latent, 0.0).T.astype(BF16)
    j = shards + gain_at // LANES
    for e in range(peers):
        at = slice(e * rows, e * rows + rank)
        g_few[j, at] = g_few[j, at] + tall[e * rank : (e + 1) * rank]
    for strip in strips:
        g_lat = t_mm(normed[:, strip], d_latent_s[...]).astype(BF16)
        for j in range(shards):
            g_few[j, strip] = g_lat[:, j * LANES : (j + 1) * LANES]
    for p in range(peers):
        at = pl.ds(pl.multiple_of(places[p] * rows, rows), rows)
        to = slice(p * rows, (p + 1) * rows)
        g_mains[p][:, : cut[0]] = g_all[at, :]
        for j in range(2):
            near_keep[j, to] = g_few[places[peers + j], at, :]
            near_send[j, to] = g_few[places[peers + 2 + j], at, :]
        for j in range(wide):
            near_keep[2 + j, to] = g_few[shards + j, at, :]
            near_send[2 + j, to] = g_few[shards + j, at, :]


def in_vmem(kernel, outs, scratch, flops, args):
    spec = pl.BlockSpec(memory_space=pltpu.VMEM)
    return pl.pallas_call(
        kernel,
        in_specs=[pl.BlockSpec(memory_space=pltpu.SMEM)] + [spec] * (len(args) - 1),
        out_specs=[spec] * len(outs),
        out_shape=outs,
        scratch_shapes=scratch,
        compiler_params=pltpu.CompilerParams(vmem_limit_bytes=60 * 2**20),
        cost_estimate=pl.CostEstimate(flops=flops, bytes_accessed=24 * 2**20, transcendentals=2**20),
    )(*args)


def attn_forward(heads, peers, score_scale, gain_at, args, small, mains):
    group, width = args[1].shape
    query_cols = heads * (NOPE + ROPE)
    shape = jax.ShapeDtypeStruct
    outs = [
        shape((group // 2, width), BF16), shape((group // 2, width), BF16), shape((group, width), BF16),
        shape((group, query_cols), BF16), shape((group, 2 * LANES), BF16),
        shape((heads, group, NOPE + V_HEAD), BF16), shape((heads, group, group), F32),
        shape((group, heads * V_HEAD), BF16), shape((group, KV_RANK), F32), shape((group, KV_RANK), BF16),
        shape((8, width), F32), shape((1, KV_RANK), F32),
        shape((width, query_cols), BF16), shape((width, heads * V_HEAD), BF16), shape((width, NOPE + V_HEAD), BF16),
        shape((width, small.shape[1] - LANES), BF16), shape((KV_RANK // LANES, width, LANES), BF16),
    ]
    n = len(args)

    def kernel(*refs):
        attn_forward_kernel(
            heads, peers, score_scale, *refs[: n + 1], refs[n + 1 : n + 1 + peers], *refs[n + 1 + peers :],
            gain_at=gain_at,
        )

    return in_vmem(kernel, outs, [], 6 * 10**9, [*args, small, *mains])


def attn_backward(heads, peers, score_scale, gain_at, rows, args):
    group, width = args[1].shape
    query_w, output_t, expand_w, extra_w, latent_w = args[2:7]
    main = query_w.shape[1] + output_t.shape[1] + expand_w.shape[1]
    few = extra_w.shape[1] // LANES
    shape = jax.ShapeDtypeStruct
    outs = [shape((rows, main), BF16)] * peers + [
        shape((2 + few, width, LANES), BF16), shape((2 + few, width, LANES), BF16),
        shape((group // 2, width), BF16), shape((group // 2, width), BF16),
    ]
    scratch = [
        pltpu.VMEM((width, query_w.shape[1]), BF16),
        pltpu.VMEM((latent_w.shape[0] + few, width, LANES), BF16),
        pltpu.VMEM((group, heads * NOPE + 2 * LANES), BF16),
        pltpu.VMEM((group, KV_RANK), BF16),
        pltpu.VMEM((group, KV_RANK), F32),
    ]
    n = len(args)

    def kernel(*refs):
        attn_backward_kernel(heads, peers, score_scale, *refs[:n], refs[n : n + peers], *refs[n + peers :], gain_at=gain_at)

    outs = in_vmem(kernel, outs, scratch, 12 * 10**9, args)
    return outs[:peers], outs[peers:]


def ffn_kernel(
    local, segs_side, steps, width, crossed,
    first_ref, x0, x1, g0, g1, router, wg, wu, wd,
    dx_keep, dx_send, out_keep, out_send, x_all, g_all, hs_all, dg_all, du_all,
    acc_out, acc_dx, gates_s, dgates_s,
):
    j = pl.program_id(0)
    half = x0.shape[0]
    slot = half // 2
    block = wg.shape[0]
    x = jnp.concatenate([x0[...], x1[...]], axis=0)
    g_in = jnp.concatenate([g0[:, :width], g1[:, :width]], axis=0)
    first = first_ref[0]
    lane = lax.broadcasted_iota(jnp.int32, (1, LANES), 1)

    @pl.when(j == 0)
    def _():
        logits = mm(x, router[...])
        routed = jnp.concatenate([g0[:, width:], g1[:, width:]], axis=0) > 0
        masked = jnp.where(routed, logits, -1e30)
        raised = jnp.where(routed, jnp.exp(masked - jnp.max(masked, axis=1, keepdims=True)), 0.0)
        gates_s[...] = raised / jnp.sum(raised, axis=1, keepdims=True)
        dgates_s[...] = jnp.zeros_like(dgates_s)
        acc_out[...] = jnp.zeros_like(acc_out)
        acc_dx[...] = jnp.zeros_like(acc_dx)
        x_all[0] = x
        g_all[0] = g_in

    gates = gates_s[...]
    wanted, columns = [], []
    for part in range(2):
        seg = 2 * j + part
        expert = jnp.where(seg < 2 * segs_side, lax.rem(seg, segs_side) * local // segs_side, local)
        want = jnp.where(expert < local, first + expert, -1)
        column = jnp.sum(jnp.where(lane == want, gates, 0.0), axis=1, keepdims=True)
        wanted.append(want)
        columns.append(jnp.where(expert < local, column, 1.0))
    lane_block = lax.broadcasted_iota(jnp.int32, (1, block), 1)
    column = jnp.where(lane_block < LANES, columns[0], columns[1])
    gate, up, d_hidden = mm_t(x, wg[...]), mm_t(x, wu[...]), mm_t(g_in, wd[...])
    logistic = 1.0 / (1.0 + jnp.exp(-gate))
    silu = gate * logistic
    hidden = silu * up
    scaled = (hidden * column).astype(BF16)
    product = hidden * d_hidden
    for part in range(2):
        dots = jnp.sum(product[:, part * LANES : (part + 1) * LANES], axis=1, keepdims=True)
        dgates_s[...] += jnp.where(lane == wanted[part], dots, 0.0)
    d_hidden = d_hidden * column
    d_gate = (d_hidden * up * (logistic * (1.0 + gate * (1.0 - logistic)))).astype(BF16)
    d_up = (d_hidden * silu).astype(BF16)
    hs_all[0], dg_all[0], du_all[0] = scaled, d_gate, d_up
    acc_out[...] += mm(scaled, wd[...])
    acc_dx[...] += mm(d_gate, wg[...]) + mm(d_up, wu[...])

    @pl.when(j == steps - 1)
    def _():
        straight = [(dx_keep, 0, 0, half), (dx_send, 0, half, 2 * half)]
        across = [
            (out_keep, 0, 0, slot), (out_send, 0, slot, half),
            (out_keep, slot, half, half + slot), (out_send, slot, half + slot, 2 * half),
        ]
        if crossed:
            swap = {id(dx_keep): out_keep, id(dx_send): out_send, id(out_keep): dx_keep, id(out_send): dx_send}
            straight = [(swap[id(ref)], *at) for ref, *at in straight]
            across = [(swap[id(ref)], *at) for ref, *at in across]
        for ref, at, lo, hi in straight + across:
            if ref is dx_keep or ref is dx_send:
                ref[at : at + hi - lo, :width] = acc_dx[lo:hi].astype(BF16)
                ref[at : at + hi - lo, width:] = dgates_s[lo:hi].astype(BF16)
            else:
                ref[at : at + hi - lo] = acc_out[lo:hi].astype(BF16)


def ffn_tile(first, rows, grads, router, weights, local, call, calls, kept, crossed):
    half, width = rows[0].shape
    hid = weights.shape[1]
    block = 2 * LANES
    steps = hid // block
    segs_side = (hid // LANES - 2) // 2

    def fixed(*shape):
        return pl.BlockSpec(shape, lambda j: (0,) * len(shape), pipeline_mode=pl.Buffered(1))

    def whole(*shape):
        return pl.BlockSpec(shape, lambda j: (0,) * len(shape))

    in_specs = [
        pl.BlockSpec(memory_space=pltpu.SMEM),
        fixed(half, width), fixed(half, width), fixed(half, width + LANES), fixed(half, width + LANES), fixed(width, LANES),
        *(pl.BlockSpec((None, block, width), lambda j, i=i: (i, j, 0)) for i in range(3)),
    ]
    args = [first, *rows, *grads, router, weights, weights, weights]
    plain = len(args)
    aliases = {}
    if kept is not None:
        in_specs += [pl.BlockSpec(memory_space=pl.ANY)] * len(kept)
        args += list(kept)
        aliases = {plain + i: 4 + i for i in range(len(kept))}
    tile_rows = pl.BlockSpec((1, 2 * half, width), lambda j: (call, 0, 0))
    tile_hidden = pl.BlockSpec((1, 2 * half, block), lambda j: (call, 0, j))
    shape = jax.ShapeDtypeStruct
    out_shape = (
        [shape((half, width + LANES), BF16)] * 2
        + [shape((half, width), BF16)] * 2
        + [shape((calls, 2 * half, width), BF16)] * 2
        + [shape((calls, 2 * half, hid), BF16)] * 3
    )
    out_specs = [whole(half, width + LANES)] * 2 + [whole(half, width)] * 2 + [tile_rows] * 2 + [tile_hidden] * 3

    def kernel(*refs):
        ffn_kernel(local, segs_side, steps, width, crossed, *refs[:plain], *refs[len(args) :])

    outs = pl.pallas_call(
        kernel,
        grid=(steps,),
        in_specs=in_specs,
        out_specs=out_specs,
        out_shape=out_shape,
        scratch_shapes=[pltpu.VMEM((2 * half, width), F32)] * 2
        + [pltpu.VMEM((2 * half, LANES), F32)] * 2,
        input_output_aliases=aliases,
        compiler_params=pltpu.CompilerParams(
            vmem_limit_bytes=56 * 2**20, dimension_semantics=("arbitrary",)
        ),
        cost_estimate=pl.CostEstimate(
            flops=24 * half * width * hid,
            bytes_accessed=6 * width * hid + 16 * half * width,
            transcendentals=2 * half * hid,
        ),
    )(*args)
    return outs[:4], outs[4:]


def pack_experts(parts, seg, room):
    local, ff, width = parts[0].shape
    side = local * seg
    block = 2 * LANES
    shape = jax.ShapeDtypeStruct

    def kernel(gate, up, down, own, both):
        for i, ref in enumerate((gate, up, down)):
            for j in range(local):
                own[i, j * seg : j * seg + ff] = ref[j]
                own[i, j * seg + ff : (j + 1) * seg] = jnp.zeros((seg - ff, block), BF16)
        both[...] = own[...]

    return pl.pallas_call(
        kernel,
        grid=(width // block,),
        in_specs=[pl.BlockSpec((local, ff, block), lambda i: (0, 0, i))] * 3,
        out_specs=[pl.BlockSpec((3, side, block), lambda i: (0, 0, i))] * 2,
        out_shape=[shape((3, side, width), BF16), shape((3, 2 * side + room, width), BF16)],
        compiler_params=pltpu.CompilerParams(vmem_limit_bytes=40 * 2**20),
        cost_estimate=pl.CostEstimate(flops=0, bytes_accessed=30 * 2**20, transcendentals=0),
    )(*parts)


def join_pair(both, other, shared):
    _, side, width = other.shape
    high, wide = shared.shape[1], 8 * LANES
    blocks = side // high

    def kernel(other_ref, shared_ref, _, out):
        @pl.when(pl.program_id(1) < blocks)
        def _():
            out[...] = other_ref[...]

        @pl.when(pl.program_id(1) == blocks)
        def _():
            out[...] = shared_ref[...]

    return pl.pallas_call(
        kernel,
        grid=(width // wide, blocks + 1),
        in_specs=[
            pl.BlockSpec((3, high, wide), lambda i, r: (0, jnp.minimum(r, blocks - 1), i)),
            pl.BlockSpec((3, high, wide), lambda i, r: (0, 0, i)),
            pl.BlockSpec(memory_space=pl.ANY),
        ],
        out_specs=pl.BlockSpec((3, high, wide), lambda i, r: (0, blocks + r, i)),
        out_shape=jax.ShapeDtypeStruct(both.shape, both.dtype),
        input_output_aliases={2: 0},
        compiler_params=pltpu.CompilerParams(vmem_limit_bytes=40 * 2**20),
        cost_estimate=pl.CostEstimate(flops=0, bytes_accessed=22 * 2**20, transcendentals=0),
    )(other, shared, both)


def after(values, *first):
    return lax.optimization_barrier((values, *first))[0]


def body(
    tokens,
    segments,
    routes,
    cotangent,
    attn_gain,
    w_query,
    w_latent,
    latent_gain,
    w_expand,
    w_output,
    ffn_gain,
    w_router,
    w_shared_gate,
    w_shared_up,
    w_shared_down,
    w_expert_gate,
    w_expert_up,
    w_expert_down,
):
    own_rows, width = tokens.shape
    peers = lax.axis_size("expert")
    shards = lax.axis_size("shard")
    ring = peers // 2
    group_len = segments.shape[0]
    experts = w_router.shape[1]
    local, _, ff = w_expert_gate.shape
    rows_dev = w_query.shape[0]
    heads = w_query.shape[1] // (NOPE + ROPE)
    half = ROPE // 2
    rank_dev = w_expand.shape[0]
    expand_cols = w_expand.shape[1]
    value_cols = heads * V_HEAD
    query_cols = heads * (NOPE + ROPE)
    me_e = lax.axis_index("expert").astype(jnp.int32)
    me_s = lax.axis_index("shard").astype(jnp.int32)
    score_scale = (NOPE + ROPE) ** (-0.5)
    shared_dev = w_shared_gate.shape[1]
    shared = shared_dev // peers
    tables = routes_of(peers, shards)
    last = []

    def send(values, way):
        return lax.ppermute(values, BOTH, tables[way])

    def step(sends, work=None, *args):
        nonlocal last
        values, args = after(([v for v, _ in sends], args), last)
        got = [send(v, way) for v, (_, way) in zip(values, sends)]
        done = work(*args) if work else None
        last = [got, done]
        return (got, done) if work else got

    plane_e = [lax.rem(me_e // 2 + ring - k, ring) * 2 + lax.rem(me_e, 2) for k in range(ring)]
    piece_e = plane_e + [e ^ 1 for e in plane_e]
    shard_order = [me_s, me_s ^ 2, me_s ^ 1, me_s ^ 3]
    places = jnp.stack([*piece_e, *shard_order]).astype(jnp.int32)

    orders = (("y", "x"), ("x", "y"))
    zones = [list(range(k, min(k + 2, ring))) for k in range(0, ring, 2)]
    calls = 2 * len(zones)

    def zone_halves(planes):
        zone = jnp.stack(planes)
        n = zone.shape[1] // 2
        return [zone[:, i * n : (i + 1) * n].reshape(zone.shape[0] * n, zone.shape[2]) for i in range(2)]

    def firsts(halves):
        return [(half, one) for half, (one, _) in zip(halves, orders)]

    def nears(halves, got):
        return [jnp.concatenate([half, g], axis=0) for half, g in zip(halves, got)]

    def split_half(near):
        n = near.shape[0] // 2
        return near[:n], near[n:]

    few = pad_to(ROPE + experts + 3, LANES)
    latent_own = lax.dynamic_slice_in_dim(w_latent, me_s * LANES, LANES, 1)
    gain_cols = jnp.stack([attn_gain, ffn_gain, jnp.pad(latent_gain, (0, rows_dev - rank_dev))], axis=1)
    small = jnp.concatenate(
        [
            latent_own,
            w_latent[:, KV_RANK:],
            w_router,
            gain_cols,
            jnp.zeros((rows_dev, few - ROPE - experts - 3), BF16),
        ],
        axis=1,
    )
    q3 = w_query.reshape(rows_dev, heads, NOPE + ROPE)
    main = jnp.concatenate(
        [
            q3[..., :NOPE].reshape(rows_dev, -1),
            q3[..., NOPE : NOPE + half].reshape(rows_dev, -1),
            q3[..., NOPE + half :].reshape(rows_dev, -1),
            w_output.T,
            jnp.concatenate([w_expand[:, h * (NOPE + V_HEAD) : (h + 1) * (NOPE + V_HEAD)] for h in range(heads)], axis=0),
        ],
        axis=1,
    )
    seg = pad_to(ff, LANES)
    side = seg * local
    tail = pad_to(shared, LANES)
    expert_parts = [w_expert_gate.transpose(0, 2, 1), w_expert_up.transpose(0, 2, 1), w_expert_down]
    shared_pack = jnp.concatenate(
        [
            w_shared_gate.T.reshape(peers, shared, rows_dev),
            w_shared_up.T.reshape(peers, shared, rows_dev),
            w_shared_down.reshape(peers, shared, rows_dev),
        ],
        axis=1,
    )
    lane_experts = jnp.arange(experts, dtype=jnp.int32)
    routed_own = jnp.any(routes[:, :, None] == lane_experts[None, None, :], axis=1)
    grad_pack = jnp.concatenate(
        [cotangent, jnp.pad(routed_own.astype(BF16), ((0, 0), (0, LANES - experts)))], axis=1
    )

    def pack(*parts):
        return pack_experts(parts, seg, 2 * tail)

    main_own, main_other = [main], []
    got, (own_side, both_sides) = step(
        [(main, "ring"), (main, "y")] + [(small, k) for k in range(1, ring)], pack, *expert_parts
    )
    main_own.append(got[0])
    main_other.append(got[1])
    small_own = jnp.concatenate([small, *got[2:]], axis=0)
    shared_all = lax.all_to_all(after(shared_pack, got), "expert", 0, 0, tiled=True)
    shared_all = shared_all.transpose(1, 0, 2).reshape(3, shared, width)
    shared_own = jnp.pad(shared_all, ((0, 0), (0, tail - shared), (0, 0)))

    got = step([(main_own[1], "ring"), (main_own[1], "y"), (small_own, "y"), (tokens, "x"), (own_side, "pair")])
    main_own.append(got[0])
    main_other.append(got[1])
    small_all = jnp.concatenate([small_own, got[2]], axis=0)
    latent_all = small_all[:, :LANES]
    token_near = jnp.concatenate([tokens, got[3]], axis=0)
    other_side = got[4]

    got = step(
        [(main_own[2], "ring"), (main_own[2], "y"), (latent_all, "x"), (token_near, "pair"), (shared_own, "pair")]
    )
    main_own.append(got[0])
    main_other.append(got[1])
    latent_x = got[2]
    token_group = jnp.concatenate([token_near, got[3]], axis=0)
    shared_both = jnp.concatenate([shared_own, got[4]], axis=1)

    got, both_sides = step(
        [(main_own[3], "y"), (jnp.stack([latent_all, latent_x]), "pair"), (grad_pack, "ring")],
        join_pair, both_sides, other_side, shared_both,
    )
    main_other.append(got[0])
    latent_pair = got[1]
    grad_blocks = [grad_pack, got[2]]
    for k in range(4, ring):
        got = step([(main_own[k - 1], "ring")])
        main_own.append(got[0])
        got = step([(main_own[k], "y")])
        main_other.append(got[0])
    mains = main_own + main_other

    def by_group(values):
        return jnp.concatenate(
            [lax.dynamic_slice_in_dim(values, s * own_rows, own_rows, 0) for s in shard_order], axis=0
        )

    index = by_group(jnp.arange(group_len, dtype=jnp.int32))
    segment = by_group(segments)
    cos, sin = angles(by_group(positions(segments)), ROPE)
    cos, sin = jnp.tile(cos, (1, heads)), jnp.tile(sin, (1, heads))
    gain_at = ROPE + experts
    def attend(small_in, mains_in, *args):
        return attn_forward(heads, peers, score_scale, gain_at, list(args), small_in, mains_in)

    grad_halves = zone_halves(grad_blocks)
    got, outs = step(
        firsts(grad_halves) + [(grad_blocks[1], "ring")],
        attend, small_all, mains,
        places, token_group, latent_x, latent_pair, cos, sin,
        index[:, None], index[None, :], segment[:, None], segment[None, :],
    )
    grad_nears = nears(grad_halves, got)
    grad_blocks.append(got[2])
    saved, attn_weights = outs[2:10], outs[12:]
    gain_attn, gain_ffn, gain_latent = outs[10][0:1], outs[10][1:2], outs[11]
    router_w = outs[15][:, ROPE : ROPE + experts]
    got = step([(outs[1], "pair")])
    keep, away = split_half(add(outs[0], got[0]))
    got = step([(away, "x"), (grad_blocks[2], "ring")])
    attn_term = keep.astype(F32) + got[0].astype(F32)
    grad_blocks.append(got[1])
    own_float = tokens.astype(F32)
    hidden_one = own_float + attn_term
    scale_ffn = inverse_rms(hidden_one)
    normed_ffn = (hidden_one * scale_ffn * gain_ffn).astype(BF16)
    logits = mm(normed_ffn, router_w)
    masked = jnp.where(routed_own, logits, -1e30)
    lifted = jnp.where(routed_own, jnp.exp(masked - jnp.max(masked, axis=1, keepdims=True)), 0.0)
    gates = lifted / jnp.sum(lifted, axis=1, keepdims=True)

    router_pad = jnp.pad(router_w, ((0, 0), (0, LANES - experts)))
    first_expert = (me_e * local).reshape(1)
    row_blocks = [normed_ffn]
    got = step([(normed_ffn, "ring")] + [(near, two) for near, (_, two) in zip(grad_nears, orders)])
    row_blocks.append(got[0])
    grad_tiles = {0: list(zip(grad_nears, got[1:]))}
    row_halves = zone_halves(row_blocks)
    got = step(firsts(row_halves) + [(row_blocks[1], "ring")])
    row_nears = nears(row_halves, got)
    row_blocks.append(got[2])
    got = step([(near, two) for near, (_, two) in zip(row_nears, orders)] + [(row_blocks[2], "ring")])
    row_tiles = {0: list(zip(row_nears, got))}
    row_blocks.append(got[2])

    kept = None
    dx, dx_near, dx_home, outs_of, out_near, out_home = {}, {}, {}, {}, {}, {}
    for_pair, from_pair = [], []

    def ways(call):
        one, two = orders[call % 2]
        return (two, one) if call == calls - 1 else (one, two)

    def moves(jobs):
        sends = []
        for what, call, stage in jobs:
            one, two = ways(call)
            if what == "out":
                one, two = two, one
            parts, near = (dx, dx_near) if what == "dx" else (outs_of, out_near)
            sends.append((parts[call][1], one) if stage == 1 else (split_half(near[call])[1], two))

        def arrived(got):
            for (what, call, stage), g in zip(jobs, got):
                parts, near, home = (dx, dx_near, dx_home) if what == "dx" else (outs_of, out_near, out_home)
                if stage == 1:
                    near[call] = add(parts[call][0], g)
                else:
                    home[call] = add(split_half(near[call])[0], g)

        return sends, arrived

    for call in range(calls):
        i, turn = call // 2, call % 2
        more = i + 1 < len(zones)
        sends, jobs = [], []
        if turn == 0 and more:
            row_halves = zone_halves([row_blocks[k] for k in zones[i + 1]])
            grad_halves = zone_halves([grad_blocks[k] for k in zones[i + 1]])
            sends += firsts(row_halves) + firsts(grad_halves)
        if turn == 1 and more:
            sends += [(near, two) for near, (_, two) in zip(row_nears, orders)] + [(grad_nears[0], orders[0][1])]
        if turn == 0 and i > 0:
            sends += [(grad_last, orders[1][1])]
        if len(row_blocks) < ring:
            sends += [(row_blocks[-1], "ring"), (grad_blocks[-1], "ring")]
        if call >= 1:
            jobs.append(("dx", call - 1, 1))
        if call >= 2:
            jobs.append(("dx", call - 2, 2))
        if call >= 3:
            jobs.append(("out", call - 3, 1))
        if call >= 4:
            jobs.append(("out", call - 4, 2))
        moved, arrived = moves(jobs)

        def tile(rows, grads, kept_in, call=call):
            return ffn_tile(
                first_expert, rows, grads, router_pad, both_sides, local, call, calls, kept_in, call < calls - 1
            )

        if turn == 1:
            grads = grad_tiles[i][1]
        else:
            grads = grad_tiles[i][0]
        got, (outs, kept) = step(moved + sends, tile, row_tiles[i][turn], grads, kept)
        arrived(got[: len(moved)])
        got = got[len(moved) :]
        dx[call], outs_of[call] = outs[:2], outs[2:4]
        if turn == 0 and i > 0:
            grad_tiles[i].append((grad_last, got[2 * len(orders) if more else 0]))
        if turn == 0 and more:
            row_nears = nears(row_halves, got[:2])
            grad_nears = nears(grad_halves, got[2:4])
        if turn == 1 and more:
            row_tiles[i + 1] = list(zip(row_nears, got[:2]))
            grad_tiles[i + 1] = [(grad_nears[0], got[2])]
            grad_last = grad_nears[1]
        if len(row_blocks) < ring:
            row_blocks.append(got[-2])
            grad_blocks.append(got[-1])

    def planes_of(home, zone_list, turns):
        return {
            (k, turn): home[2 * i + turn].reshape(len(zones[i]), -1, home[2 * i + turn].shape[1])[j]
            for i in zone_list
            for j, k in enumerate(zones[i])
            for turn in turns
        }

    def weight_part(d, v):
        return t_mm(d.reshape(-1, d.shape[-1])[:, side:], v.reshape(-1, v.shape[-1])).astype(BF16)

    x_all, g_all, hs_all, dg_all, du_all = kept
    end = calls - 1
    early = planes_of(dx_home, range(len(zones) - 1), range(2))
    early_keys = [key for key in early if key[0] > 0]
    jobs = [("dx", end, 1), ("dx", end - 1, 2)]
    moved, arrived = moves(jobs)
    got, part = step(moved + [(early[key], -key[0]) for key in early_keys], weight_part, dg_all, x_all)
    arrived(got)
    ring_terms = {turn: [early[(0, turn)]] for turn in range(2)}
    for key, g in zip(early_keys, got[2:]):
        ring_terms[key[1]].append(g)
    for_pair.append(part)

    a_late = planes_of(dx_home, [len(zones) - 1], [0])
    moved, arrived = moves([("dx", end, 2)])
    got, part = step(
        moved + [(v, -k) for (k, _), v in a_late.items()] + [(for_pair[0], "pair")], weight_part, du_all, x_all
    )
    arrived(got)
    ring_terms[0] += got[1:-1]
    from_pair.append(got[-1])
    for_pair.append(part)

    b_late = planes_of(dx_home, [len(zones) - 1], [1])
    moved, arrived = moves([("out", end - 3, 2), ("out", end - 1, 1)])
    got, part = step(
        [(v, -k) for (k, _), v in b_late.items()] + [(for_pair[1], "pair")] + moved, weight_part, hs_all, g_all
    )
    ring_terms[1] += got[: len(b_late)]
    from_pair.append(got[len(b_late)])
    arrived(got[len(b_late) + 1 :])
    for_pair.append(part)

    def summed(terms):
        total = terms[0].astype(F32)
        for term in terms[1:]:
            total = total + term.astype(F32)
        return total

    d_rows = jnp.concatenate([summed(ring_terms[turn]) for turn in range(2)], axis=0)
    d_normed = d_rows[:, :width]
    d_gates = d_rows[:, width : width + experts]
    grad_in = cotangent.astype(F32)
    d_logits = (gates * (d_gates - jnp.sum(gates * d_gates, axis=1, keepdims=True))).astype(BF16)
    d_normed = d_normed + mm_t(d_logits, router_w)
    d_norm, grad_gain_ffn = norm_back(hidden_one, scale_ffn, gain_ffn, d_normed)
    d_hidden_one = grad_in + d_norm
    d_attn_own = d_hidden_one.astype(BF16)
    moved, arrived = moves([("out", end - 2, 1)])
    got = step([(d_attn_own, "x"), (for_pair[2], "pair")] + moved)
    d_near = jnp.concatenate([d_attn_own, got[0]], axis=0)
    from_pair.append(got[1])
    arrived(got[2:])
    got = step([(d_near, "pair")])
    d_attn_group = jnp.concatenate([d_near, got[0]], axis=0)
    shared_back = jnp.concatenate(
        [
            add(own[side : side + shared], g[side + tail : side + tail + shared]).reshape(shared, peers, rows_dev)
            for own, g in zip(for_pair, from_pair)
        ],
        axis=0,
    ).transpose(1, 0, 2)

    def attend_back(*args):
        return attn_backward(heads, peers, score_scale, gain_at, rows_dev, list(args))

    waiting = [("out", end, 1)]
    waiting += [("out", call, 2) for call in range(calls) if call not in out_home and call in out_near]
    waiting += [("out", call, 1) for call in range(calls) if call not in out_near and call != end]
    moved, arrived = moves(waiting)
    got, (g_mains, (near_keep, near_send, d_in_keep, d_in_send)) = step(
        moved, attend_back,
        places, d_attn_group, *attn_weights, gain_latent, cos, sin, *saved, normed_ffn,
        jnp.pad(d_logits, ((0, 0), (ROPE, few - ROPE - experts))), token_group, grad_gain_ffn.reshape(1, width),
    )
    arrived(got)
    waiting = [("out", call, 2) for call in range(calls) if call not in out_home]

    def own_part(d, v, g):
        return t_mm(d.reshape(-1, d.shape[-1])[:, :side], v.reshape(-1, v.shape[-1])) + g[:side].astype(F32)

    parts = {}

    def mains_y(k):
        return (g_mains[ring + k], "y")

    order = [*range(1, ring), 0]
    moved, arrived = moves(waiting)
    got, grad_gate = step(
        [mains_y(order[0]), (near_send, "pair"), (d_in_send, "pair")] + moved, own_part, dg_all, x_all, from_pair[0]
    )
    total = add(g_mains[order[0]], got[0])
    near = add(near_keep, got[1])
    keep, d_away = split_half(add(d_in_keep, got[2]))
    arrived(got[3:])
    out_planes = planes_of(out_home, range(len(zones)), range(2))
    out_rows = [jnp.concatenate([out_planes[(k, turn)] for turn in range(2)], axis=0) for k in range(ring)]
    out_terms = [out_rows[0]]

    few_away = jnp.concatenate([near[1:2], near[2:]], axis=0)
    few_keep = jnp.concatenate([near[0:1], near[2:]], axis=0)
    got, grad_up = step(
        [mains_y(order[1]), (total, "ring"), (few_away, "x"), (d_away, "x"), (out_rows[1], -1)],
        own_part, du_all, x_all, from_pair[1],
    )
    total = add(add(g_mains[order[1]], got[0]), got[1])
    few_sum = add(few_keep, got[2])
    few_sum = jnp.concatenate([few_sum[j] for j in range(few_sum.shape[0])], axis=1)
    d_normed_in = keep.astype(F32) + got[3].astype(F32)
    out_terms.append(got[4])

    few_half = few_sum.shape[0] // 2
    got, grad_down = step(
        [mains_y(order[2]), (total, "ring"), (few_sum[few_half:], "y")], own_part, hs_all, g_all, from_pair[2]
    )
    total = add(add(g_mains[order[2]], got[0]), got[1])
    few_sum = add(few_sum[:few_half], got[2])
    few_planes = [few_sum[k * rows_dev : (k + 1) * rows_dev] for k in range(ring)]
    shared_home = lax.all_to_all(after(shared_back, got), "expert", 0, 0, tiled=True).astype(F32)

    got = step([mains_y(order[3]), (total, "ring"), *((few_planes[k], -k) for k in range(1, ring))])
    total = add(add(g_mains[order[3]], got[0]), got[1])
    few_home = summed([few_planes[0], *got[2:]])
    latent_home = few_home[:, :LANES].astype(BF16)
    for j in order[4:]:
        got = step([mains_y(j), (total, "ring")])
        total = add(add(g_mains[j], got[0]), got[1])
    home = total.astype(F32)

    got = step([(latent_home, "x")] + [(out_rows[k], -k) for k in range(2, ring)])
    latent_two = jnp.stack([latent_home, got[0]])
    block_out = (hidden_one + summed(out_terms + got[1:])).astype(BF16)
    got = step([(latent_two, "pair")])
    latent_four = jnp.concatenate([latent_two, got[0]], axis=0)
    grad_latent = jnp.zeros((shards, rows_dev, LANES), BF16)
    for r in range(shards):
        grad_latent = lax.dynamic_update_slice_in_dim(grad_latent, latent_four[r : r + 1], shard_order[r], 0)
    grad_latent = jnp.concatenate([*(grad_latent[j] for j in range(shards)), few_home[:, LANES : LANES + ROPE].astype(BF16)], axis=1)
    grad_router = few_home[:, LANES + ROPE : LANES + ROPE + experts].astype(F32)
    d_token, _ = norm_back(own_float, inverse_rms(own_float), gain_attn, d_normed_in)
    tokens_grad = d_hidden_one + d_token
    gain_home = few_home[:, LANES + gain_at : LANES + gain_at + 3].astype(F32).T

    grad_experts = [
        jnp.stack([g[j * seg : j * seg + ff] for j in range(local)]) for g in (grad_gate, grad_up, grad_down)
    ]
    grad_shared = [shared_home[:, i * shared : (i + 1) * shared].reshape(shared_dev, rows_dev) for i in range(3)]

    nope_cols = heads * NOPE
    rope_cols = heads * half
    gq = home[:, :query_cols]
    grad_query_own = jnp.concatenate(
        [
            gq[:, :nope_cols].reshape(rows_dev, heads, NOPE),
            gq[:, nope_cols : nope_cols + rope_cols].reshape(rows_dev, heads, half),
            gq[:, nope_cols + rope_cols :].reshape(rows_dev, heads, half),
        ],
        axis=2,
    ).reshape(rows_dev, query_cols)
    g_expand = home[:, query_cols + value_cols :]
    return (
        block_out,
        tokens_grad,
        gain_home[0],
        grad_query_own,
        grad_latent.astype(F32),
        gain_home[2, :rank_dev],
        jnp.concatenate([g_expand[h * rank_dev : (h + 1) * rank_dev] for h in range(heads)], axis=1),
        home[:, query_cols : query_cols + value_cols].T,
        gain_home[1],
        grad_router,
        grad_shared[0].T,
        grad_shared[1].T,
        grad_shared[2],
        grad_experts[0].transpose(0, 2, 1),
        grad_experts[1].transpose(0, 2, 1),
        grad_experts[2],
    )


def solution(mesh):
    rows = P(("expert", "shard"), None)
    return jax.shard_map(
        body,
        mesh=mesh,
        in_specs=(
            rows,
            P("expert"),
            rows,
            rows,
            P("expert"),
            P("expert", "shard"),
            P("expert", None),
            P("expert"),
            P("expert", "shard"),
            P("shard", "expert"),
            P("expert"),
            P("expert", None),
            P("expert", "shard"),
            P("expert", "shard"),
            P("shard", "expert"),
            P("expert", None, "shard"),
            P("expert", None, "shard"),
            P("expert", "shard", None),
        ),
        out_specs=(
            rows,
            rows,
            P("expert"),
            P("expert", "shard"),
            P("expert", None),
            P("expert"),
            P("expert", "shard"),
            P("shard", "expert"),
            P("expert"),
            P("expert", None),
            P("expert", "shard"),
            P("expert", "shard"),
            P("shard", "expert"),
            P("expert", None, "shard"),
            P("expert", None, "shard"),
            P("expert", "shard", None),
        ),
        check_vma=False,
    )
```

```python
import jax
import jax.numpy as jnp
from jax import lax
from jax.experimental import pallas as pl
from jax.experimental.pallas import tpu as pltpu
from jax.sharding import PartitionSpec as P

NOPE = 128
ROPE = 64
V_HEAD = 128
KV_RANK = 512
TOP = 6
LANES = 128

epsilon = 1e-06
F32 = jnp.float32
BF16 = jnp.bfloat16


def pad_to(n, m):
    return -(-n // m) * m


def angles(places, width):
    half_width = width // 2
    spacing = 10000.0 ** (-2.0 * jnp.arange(half_width, dtype=F32) / width)
    turned = places.astype(F32)[:, None] * spacing[None, :]
    return (jnp.cos(turned), jnp.sin(turned))


def positions(segment):
    indices = jnp.arange(segment.shape[0], dtype=jnp.int32)
    prompt_len = jnp.sum((segment == 0).astype(jnp.int32))
    earlier = jnp.sum((segment[None, :] < segment[:, None]).astype(jnp.int32), axis=1)
    return jnp.where(segment == 0, indices, prompt_len + indices - earlier)


def inverse_rms(values):
    return lax.rsqrt(jnp.mean(values * values, axis=-1, keepdims=True) + epsilon)


def norm_back(values, scaling, gain, incoming):
    weighted = incoming * gain
    inner = jnp.mean(weighted * values, axis=-1, keepdims=True)
    return (
        scaling * weighted - values * scaling**3 * inner,
        jnp.sum(incoming * values * scaling, axis=0),
    )


def dot(a, b, dims):
    return lax.dot_general(a, b, (dims, ((), ())), preferred_element_type=F32)


def mm(a, b):
    return dot(a, b, ((1,), (0,)))


def mm_t(a, b):
    return dot(a, b, ((1,), (1,)))


def t_mm(a, b):
    return dot(a, b, ((0,), (0,)))


BOTH = ("expert", "shard")


def add(a, b):
    return (a.astype(F32) + b.astype(F32)).astype(BF16)


def routes_of(peers, shards):
    def table(step):
        return [
            (e * shards + s, step(e, s)[0] * shards + step(e, s)[1])
            for e in range(peers)
            for s in range(shards)
        ]

    ring = peers // 2

    def around(k):
        return table(lambda e, s: ((e // 2 + k) % ring * 2 + e % 2, s))

    return {
        "y": table(lambda e, s: (e ^ 1, s)),
        "x": table(lambda e, s: (e, s ^ 2)),
        "pair": table(lambda e, s: (e, s ^ 1)),
        "ring": around(1),
        **{k: around(k) for k in range(1 - ring, ring)},
    }


def spread(values, first, lane):
    kept = jnp.where((lane >= first) & (lane < first + ROPE // 2), values, 0.0)
    kept = kept + pltpu.roll(kept, ROPE // 2, 1)
    return kept + pltpu.roll(kept, ROPE, 1)


def attn_forward_kernel(
    heads, peers, score_scale,
    places, tokens, latent_x, latent_pair, cos, sin, index_c, index_r, segment_c, segment_r,
    small, mains,
    part_keep, part_send, normed_o, query_o, key_rope_o, expanded_o, soft_o, mixed_o, compressed_o, latent_o,
    gains, gain_latent, query_w, output_t, expand_w, extra_w, latent_w,
    *, gain_at,
):
    group = tokens.shape[0]
    rank = KV_RANK // peers
    rows = mains[0].shape[0]
    shards = latent_w.shape[0]
    cut = (query_w.shape[1], query_w.shape[1] + output_t.shape[1])
    for p in range(peers):
        to = pl.ds(pl.multiple_of(places[p] * rows, rows), rows)
        query_w[to, :] = mains[p][:, : cut[0]]
        output_t[to, :] = mains[p][:, cut[0] : cut[1]]
        expand_w[to, :] = mains[p][:, cut[1] : cut[1] + expand_w.shape[1]]
        at = slice(p * rows, (p + 1) * rows)
        latent_w[places[peers], to, :] = small[at, :LANES]
        extra_w[to, :] = small[at, LANES:]
        latent_w[places[peers + 1], to, :] = latent_x[at]
        latent_w[places[peers + 2], to, :] = latent_pair[0, at]
        latent_w[places[peers + 3], to, :] = latent_pair[1, at]
    block, at = gain_at // LANES * LANES, gain_at % LANES
    gains[...] = extra_w[:, block : block + LANES].astype(F32).T[at : at + 8]
    few_rows = [extra_w[p * rows : p * rows + rank, block : block + LANES] for p in range(peers)]
    gain_latent[...] = jnp.concatenate(few_rows, axis=0).astype(F32).T[at + 2 : at + 3]
    x = tokens[...].astype(F32)
    x = x * lax.rsqrt(jnp.mean(x * x, axis=1, keepdims=True) + epsilon) * gains[0:1]
    normed_o[...] = x.astype(BF16)
    normed = normed_o[...]
    lane = lax.broadcasted_iota(jnp.int32, (1, LANES), 1)
    c, s = cos[...], sin[...]
    raw = mm(normed, extra_w[:, :LANES])
    a, b = spread(raw, 0, lane), spread(raw, ROPE // 2, lane)
    key_rope_o[:, :LANES] = (a * c - b * s).astype(BF16)
    key_rope_o[:, LANES:] = (b * c + a * s).astype(BF16)
    for j in range(shards):
        compressed_o[:, j * LANES : (j + 1) * LANES] = mm(normed, latent_w[j])
    u = compressed_o[...]
    r = lax.rsqrt(jnp.mean(u * u, axis=1, keepdims=True) + epsilon)
    latent_o[...] = (u * r * gain_latent[...]).astype(BF16)
    q = mm(normed, query_w[...])
    nope = heads * NOPE
    query_o[:, :nope] = q[:, :nope].astype(BF16)
    a, b = q[:, nope : nope + LANES], q[:, nope + LANES :]
    query_o[:, nope : nope + LANES] = (a * c - b * s).astype(BF16)
    query_o[:, nope + LANES :] = (b * c + a * s).astype(BF16)
    allowed = (index_r[...] <= index_c[...]) & ((segment_r[...] == 0) | (segment_r[...] == segment_c[...]))
    lane2 = lax.rem(lax.broadcasted_iota(jnp.int32, (1, 2 * LANES), 1), LANES)
    for h in range(heads):
        w = jnp.concatenate(
            [expand_w[pl.ds((e * heads + h) * rank, rank), :] for e in range(peers)], axis=0
        )
        expanded_o[h] = mm(latent_o[...], w).astype(BF16)
        key_rope = jnp.where((lane2 >= h * ROPE // 2) & (lane2 < (h + 1) * ROPE // 2), key_rope_o[...], jnp.zeros((), BF16))
        scores = mm_t(query_o[:, h * NOPE : (h + 1) * NOPE], expanded_o[h, :, :NOPE]) + mm_t(query_o[:, nope:], key_rope)
        scores = jnp.where(allowed, scores * score_scale, -1e30)
        raised = jnp.exp(scores - jnp.max(scores, axis=1, keepdims=True))
        soft = raised * (1.0 / jnp.sum(raised, axis=1, keepdims=True))
        soft_o[h] = soft
        mixed_o[:, h * V_HEAD : (h + 1) * V_HEAD] = mm(soft.astype(BF16), expanded_o[h, :, NOPE:]).astype(BF16)
    half = group // 2
    part_keep[...] = mm_t(mixed_o[:half], output_t[...]).astype(BF16)
    part_send[...] = mm_t(mixed_o[half:], output_t[...]).astype(BF16)


def attn_backward_kernel(
    heads, peers, score_scale,
    places, d_attn, query_w, output_t, expand_w, extra_w, latent_w, gain_latent, cos, sin,
    normed, query, key_rope_all, expanded, soft_all, compressed, latent,
    normed_ffn, d_logits, tokens, g_gain_ffn,
    g_mains, near_keep, near_send, d_in_keep, d_in_send,
    g_all, g_few, d_query_s, d_latent_s, d_use_s,
    *, gain_at,
):
    group = d_attn.shape[0]
    rank = KV_RANK // peers
    shards = latent_w.shape[0]
    nope = heads * NOPE
    lane = lax.broadcasted_iota(jnp.int32, (1, LANES), 1)
    lane2 = lax.rem(lax.broadcasted_iota(jnp.int32, (1, 2 * LANES), 1), LANES)
    rows = g_mains[0][0].shape[0]
    query_cols = query_w.shape[1]
    width = d_attn.shape[1]
    strips = [slice(lo, lo + width // 4) for lo in range(0, width, width // 4)]
    expand_cols = expand_w.shape[1]
    d_mixed = mm(d_attn[...], output_t[...]).astype(BF16)
    d_query_rope = jnp.zeros((group, 2 * LANES), F32)
    d_key_rope = jnp.zeros((group, 2 * LANES), F32)
    for h in range(heads):
        mine = (lane2 >= h * ROPE // 2) & (lane2 < (h + 1) * ROPE // 2)
        key_rope = jnp.where(mine, key_rope_all[...], jnp.zeros((), BF16))
        soft = soft_all[h]
        d_out = d_mixed[:, h * V_HEAD : (h + 1) * V_HEAD]
        d_soft = mm_t(d_out, expanded[h, :, NOPE:])
        d_scores = score_scale * soft * (d_soft - jnp.sum(soft * d_soft, axis=1, keepdims=True))
        d_scores = d_scores.astype(BF16)
        d_query_s[:, h * NOPE : (h + 1) * NOPE] = mm(d_scores, expanded[h, :, :NOPE]).astype(BF16)
        d_query_rope = d_query_rope + mm(d_scores, key_rope)
        both = jnp.concatenate([query[:, h * NOPE : (h + 1) * NOPE], query[:, nope:]], axis=1)
        d_key = t_mm(d_scores, both)
        d_key_rope = d_key_rope + jnp.where(mine, d_key[:, NOPE:], 0.0)
        d_values = t_mm(soft.astype(BF16), d_out)
        d_expanded = jnp.concatenate([d_key[:, :NOPE], d_values], axis=1).astype(BF16)
        w = jnp.concatenate(
            [expand_w[pl.ds((e * heads + h) * rank, rank), :] for e in range(peers)], axis=0
        )
        g_w = t_mm(latent[...], d_expanded).astype(BF16)
        for e in range(peers):
            g_all[pl.ds((e * heads + h) * rank, rank), :expand_cols] = g_w[e * rank : (e + 1) * rank]
        back = mm_t(d_expanded, w)
        if h == 0:
            d_use_s[...] = back
        else:
            d_use_s[...] += back
    for p in range(peers):
        ref, to = g_mains[p]
        ref[to : to + rows, query_cols:] = g_all[pl.ds(pl.multiple_of(places[p] * rows, rows), rows), :expand_cols]
    c, s = cos[...], sin[...]
    a, b = d_query_rope[:, :LANES], d_query_rope[:, LANES:]
    d_query_s[:, nope : nope + LANES] = (a * c + b * s).astype(BF16)
    d_query_s[:, nope + LANES :] = (b * c - a * s).astype(BF16)
    u, n = compressed[...], d_use_s[...]
    r = lax.rsqrt(jnp.mean(u * u, axis=1, keepdims=True) + epsilon)
    weighted = n * gain_latent[...]
    inner = jnp.mean(weighted * u, axis=1, keepdims=True)
    g_gain_latent = jnp.sum(n * u * r, axis=0, keepdims=True)
    d_latent_s[...] = (r * weighted - u * (r * r * r * inner)).astype(BF16)

    def folded(v):
        v = v + pltpu.roll(v, ROPE // 2, 1)
        return v + pltpu.roll(v, ROPE, 1)

    a, b = folded(d_key_rope[:, :LANES]), folded(d_key_rope[:, LANES:])
    d_extra = jnp.where(
        lane < ROPE // 2, a * c + b * s, jnp.where(lane < ROPE, b * c - a * s, 0.0)
    ).astype(BF16)
    half = group // 2
    g_gain_attn = jnp.zeros((1, tokens.shape[1]), F32)
    fine = half // 2
    for lo in range(0, group, fine):
        part, to = slice(lo, lo + fine), (d_in_keep if lo < half else d_in_send).at[pl.ds(lo % half, fine)]
        total = mm_t(d_query_s[part], query_w[...]) + mm_t(d_extra[part], extra_w[:, :LANES])
        for j in range(shards):
            total = total + mm_t(d_latent_s[part, j * LANES : (j + 1) * LANES], latent_w[j])
        to[...] = total.astype(BF16)
        x = tokens[part].astype(F32)
        x = x * lax.rsqrt(jnp.mean(x * x, axis=1, keepdims=True) + epsilon)
        g_gain_attn = g_gain_attn + jnp.sum(total * x, axis=0, keepdims=True)
    for strip in strips:
        g_all[strip, :] = t_mm(normed[:, strip], d_query_s[...]).astype(BF16)
    wide = extra_w.shape[1] // LANES
    line = lax.broadcasted_iota(jnp.int32, (LANES, 1), 0)
    at_line = gain_at % LANES
    for j in range(wide):
        g_extra = t_mm(normed_ffn[...], d_logits[:, j * LANES : (j + 1) * LANES])
        if j == 0:
            g_extra = g_extra + t_mm(normed[...], d_extra)
        if j == gain_at // LANES:
            both = jnp.where(line == at_line, g_gain_attn, jnp.where(line == at_line + 1, g_gain_ffn[...], 0.0))
            g_extra = g_extra + both.T
        g_few[shards + j] = g_extra.astype(BF16)
    tall = jnp.where(line == at_line + 2, g_gain_latent, 0.0).T.astype(BF16)
    j = shards + gain_at // LANES
    for e in range(peers):
        at = slice(e * rows, e * rows + rank)
        g_few[j, at] = g_few[j, at] + tall[e * rank : (e + 1) * rank]
    for strip in strips:
        g_lat = t_mm(normed[:, strip], d_latent_s[...]).astype(BF16)
        for j in range(shards):
            g_few[j, strip] = g_lat[:, j * LANES : (j + 1) * LANES]
    for p in range(peers):
        at = pl.ds(pl.multiple_of(places[p] * rows, rows), rows)
        to = slice(p * rows, (p + 1) * rows)
        ref, down = g_mains[p]
        ref[down : down + rows, :query_cols] = g_all[at, :]
        for j in range(2):
            near_keep[j, to] = g_few[places[peers + j], at, :]
            near_send[j, to] = g_few[places[peers + 2 + j], at, :]
        for j in range(wide):
            near_keep[2 + j, to] = g_few[shards + j, at, :]
            near_send[2 + j, to] = g_few[shards + j, at, :]


def in_vmem(kernel, outs, scratch, flops, args):
    spec = pl.BlockSpec(memory_space=pltpu.VMEM)
    return pl.pallas_call(
        kernel,
        in_specs=[pl.BlockSpec(memory_space=pltpu.SMEM)] + [spec] * (len(args) - 1),
        out_specs=[spec] * len(outs),
        out_shape=outs,
        scratch_shapes=scratch,
        compiler_params=pltpu.CompilerParams(vmem_limit_bytes=60 * 2**20),
        cost_estimate=pl.CostEstimate(flops=flops, bytes_accessed=24 * 2**20, transcendentals=2**20),
    )(*args)


def attn_forward(heads, peers, score_scale, gain_at, args, small, mains):
    group, width = args[1].shape
    query_cols = heads * (NOPE + ROPE)
    shape = jax.ShapeDtypeStruct
    outs = [
        shape((group // 2, width), BF16), shape((group // 2, width), BF16), shape((group, width), BF16),
        shape((group, query_cols), BF16), shape((group, 2 * LANES), BF16),
        shape((heads, group, NOPE + V_HEAD), BF16), shape((heads, group, group), F32),
        shape((group, heads * V_HEAD), BF16), shape((group, KV_RANK), F32), shape((group, KV_RANK), BF16),
        shape((8, width), F32), shape((1, KV_RANK), F32),
        shape((width, query_cols), BF16), shape((width, heads * V_HEAD), BF16), shape((width, NOPE + V_HEAD), BF16),
        shape((width, small.shape[1] - LANES), BF16), shape((KV_RANK // LANES, width, LANES), BF16),
    ]
    n = len(args)

    def kernel(*refs):
        attn_forward_kernel(
            heads, peers, score_scale, *refs[: n + 1], refs[n + 1 : n + 1 + peers], *refs[n + 1 + peers :],
            gain_at=gain_at,
        )

    return in_vmem(kernel, outs, [], 6 * 10**9, [*args, small, *mains])


def attn_backward(heads, peers, score_scale, gain_at, rows, args):
    group, width = args[1].shape
    query_w, output_t, expand_w, extra_w, latent_w = args[2:7]
    main = query_w.shape[1] + expand_w.shape[1]
    few = extra_w.shape[1] // LANES
    shape = jax.ShapeDtypeStruct
    ring = peers // 2
    order = [*range(1, ring), 0]
    outs = [shape((rows, main), BF16)] * ring + [shape((2 * rows, main), BF16)] * (ring // 2) + [
        shape((2 + few, width, LANES), BF16), shape((2 + few, width, LANES), BF16),
        shape((group // 2, width), BF16), shape((group // 2, width), BF16),
    ]
    scratch = [
        pltpu.VMEM((width, query_w.shape[1]), BF16),
        pltpu.VMEM((latent_w.shape[0] + few, width, LANES), BF16),
        pltpu.VMEM((group, heads * NOPE + 2 * LANES), BF16),
        pltpu.VMEM((group, KV_RANK), BF16),
        pltpu.VMEM((group, KV_RANK), F32),
    ]
    n = len(args)

    def kernel(*refs):
        pieces = [(ref, 0) for ref in refs[n : n + ring]] + [None] * ring
        for i, k in enumerate(order):
            pieces[ring + k] = (refs[n + ring + i // 2], i % 2 * rows)
        rest = refs[n + ring + ring // 2 :]
        attn_backward_kernel(heads, peers, score_scale, *refs[:n], pieces, *rest, gain_at=gain_at)

    outs = in_vmem(kernel, outs, scratch, 12 * 10**9, args)
    return outs[:ring], outs[ring : ring + ring // 2], outs[ring + ring // 2 :]


PARTS = {
    "far": ((0, 1, 2, 3), (4, 5, 6, 7)),
    "near": ((0, 1, 4, 5), (2, 3, 6, 7)),
    "ring": ((0, 2, 4, 6), (1, 3, 5, 7)),
}


def ffn_kernel(
    local, segs_side, steps, width, dx_mode, out_mode,
    first_ref, x0, x1, g0, g1, router, wg, wu, wd,
    dx_keep, dx_send, out_keep, out_send, x_all, g_all, hs_all, dg_all, du_all,
    acc_out, acc_dx, gates_s, dgates_s,
):
    j = pl.program_id(0)
    half = x0.shape[0]
    unit = half // 4
    block = wg.shape[0]
    x = jnp.concatenate([x0[...], x1[...]], axis=0)
    g_in = jnp.concatenate([g0[:, :width], g1[:, :width]], axis=0)
    first = first_ref[0]
    lane = lax.broadcasted_iota(jnp.int32, (1, LANES), 1)

    @pl.when(j == 0)
    def _():
        logits = mm(x, router[...])
        routed = jnp.concatenate([g0[:, width:], g1[:, width:]], axis=0) > 0
        masked = jnp.where(routed, logits, -1e30)
        raised = jnp.where(routed, jnp.exp(masked - jnp.max(masked, axis=1, keepdims=True)), 0.0)
        gates_s[...] = raised / jnp.sum(raised, axis=1, keepdims=True)
        dgates_s[...] = jnp.zeros_like(dgates_s)
        acc_out[...] = jnp.zeros_like(acc_out)
        acc_dx[...] = jnp.zeros_like(acc_dx)
        x_all[0] = x
        g_all[0] = g_in

    gates = gates_s[...]
    wanted, columns = [], []
    for part in range(2):
        seg = 2 * j + part
        expert = jnp.where(seg < 2 * segs_side, lax.rem(seg, segs_side) * local // segs_side, local)
        want = jnp.where(expert < local, first + expert, -1)
        column = jnp.sum(jnp.where(lane == want, gates, 0.0), axis=1, keepdims=True)
        wanted.append(want)
        columns.append(jnp.where(expert < local, column, 1.0))
    lane_block = lax.broadcasted_iota(jnp.int32, (1, block), 1)
    column = jnp.where(lane_block < LANES, columns[0], columns[1])
    gate, up, d_hidden = mm_t(x, wg[...]), mm_t(x, wu[...]), mm_t(g_in, wd[...])
    logistic = 1.0 / (1.0 + jnp.exp(-gate))
    silu = gate * logistic
    hidden = silu * up
    scaled = (hidden * column).astype(BF16)
    product = hidden * d_hidden
    for part in range(2):
        dots = jnp.sum(product[:, part * LANES : (part + 1) * LANES], axis=1, keepdims=True)
        dgates_s[...] += jnp.where(lane == wanted[part], dots, 0.0)
    d_hidden = d_hidden * column
    d_gate = (d_hidden * up * (logistic * (1.0 + gate * (1.0 - logistic)))).astype(BF16)
    d_up = (d_hidden * silu).astype(BF16)
    hs_all[0], dg_all[0], du_all[0] = scaled, d_gate, d_up
    acc_out[...] += mm(scaled, wd[...])
    acc_dx[...] += mm(d_gate, wg[...]) + mm(d_up, wu[...])

    @pl.when(j == steps - 1)
    def _():
        for (keep, away), ranges, is_dx in (
            ((dx_keep, dx_send), PARTS[dx_mode], True),
            ((out_keep, out_send), PARTS[out_mode], False),
        ):
            for ref, blocks in zip((keep, away), ranges):
                for at, block_of in enumerate(blocks):
                    to, rows = pl.ds(at * unit, unit), pl.ds(block_of * unit, unit)
                    if is_dx:
                        ref[to, :width] = acc_dx[rows].astype(BF16)
                        ref[to, width:] = dgates_s[rows].astype(BF16)
                    else:
                        ref[to] = acc_out[rows].astype(BF16)


def ffn_tile(first, rows, grads, router, weights, local, call, calls, kept, dx_mode, out_mode):
    half, width = rows[0].shape
    hid = weights.shape[1]
    block = 2 * LANES
    steps = hid // block
    segs_side = (hid // LANES - 2) // 2

    def fixed(*shape):
        return pl.BlockSpec(shape, lambda j: (0,) * len(shape), pipeline_mode=pl.Buffered(1))

    def whole(*shape):
        return pl.BlockSpec(shape, lambda j: (0,) * len(shape))

    in_specs = [
        pl.BlockSpec(memory_space=pltpu.SMEM),
        fixed(half, width), fixed(half, width), fixed(half, width + LANES), fixed(half, width + LANES), fixed(width, LANES),
        *(pl.BlockSpec((None, block, width), lambda j, i=i: (i, j, 0)) for i in range(3)),
    ]
    args = [first, *rows, *grads, router, weights, weights, weights]
    plain = len(args)
    aliases = {}
    if kept is not None:
        in_specs += [pl.BlockSpec(memory_space=pl.ANY)] * len(kept)
        args += list(kept)
        aliases = {plain + i: 4 + i for i in range(len(kept))}
    tile_rows = pl.BlockSpec((1, 2 * half, width), lambda j: (call, 0, 0))
    tile_hidden = pl.BlockSpec((1, 2 * half, block), lambda j: (call, 0, j))
    shape = jax.ShapeDtypeStruct
    out_shape = (
        [shape((half, width + LANES), BF16)] * 2
        + [shape((half, width), BF16)] * 2
        + [shape((calls, 2 * half, width), BF16)] * 2
        + [shape((calls, 2 * half, hid), BF16)] * 3
    )
    out_specs = [whole(half, width + LANES)] * 2 + [whole(half, width)] * 2 + [tile_rows] * 2 + [tile_hidden] * 3

    def kernel(*refs):
        ffn_kernel(local, segs_side, steps, width, dx_mode, out_mode, *refs[:plain], *refs[len(args) :])

    outs = pl.pallas_call(
        kernel,
        grid=(steps,),
        in_specs=in_specs,
        out_specs=out_specs,
        out_shape=out_shape,
        scratch_shapes=[pltpu.VMEM((2 * half, width), F32)] * 2
        + [pltpu.VMEM((2 * half, LANES), F32)] * 2,
        input_output_aliases=aliases,
        compiler_params=pltpu.CompilerParams(
            vmem_limit_bytes=56 * 2**20, dimension_semantics=("arbitrary",)
        ),
        cost_estimate=pl.CostEstimate(
            flops=24 * half * width * hid,
            bytes_accessed=6 * width * hid + 16 * half * width,
            transcendentals=2 * half * hid,
        ),
    )(*args)
    return outs[:4], outs[4:]


def pick_pieces(order, sources):
    n, lanes = sources[0].shape[0], sources[0].shape[2]
    heights = [v.shape[1] for v in sources]
    shape = (n, sum(heights), lanes)

    def kernel(_, *refs):
        at = 0
        for ref, high in zip(refs, heights):
            refs[-1][0, at : at + high] = ref[0]
            at += high

    return pl.pallas_call(
        kernel,
        grid_spec=pltpu.PrefetchScalarGridSpec(
            num_scalar_prefetch=1,
            grid=(n,),
            in_specs=[pl.BlockSpec((1, h, lanes), lambda p, order: (order[p], 0, 0)) for h in heights],
            out_specs=pl.BlockSpec((1, *shape[1:]), lambda p, order: (p, 0, 0)),
        ),
        out_shape=jax.ShapeDtypeStruct(shape, sources[0].dtype),
        cost_estimate=pl.CostEstimate(flops=0, bytes_accessed=2**21, transcendentals=0),
    )(order, *sources)


def expert_grad(d, v, got, local, ff, seg):
    rows, width = v.shape
    side = local * seg
    block = 2 * LANES

    def kernel(d_ref, v_ref, got_ref, out, turned):
        @pl.when(pl.program_id(0) == 0)
        def _():
            turned[...] = d_ref[...].T

        total = mm(turned[...], v_ref[...]) + got_ref[...].astype(F32)
        for j in range(local):
            out[j] = total[j * seg : j * seg + ff]

    return pl.pallas_call(
        kernel,
        grid=(width // block,),
        in_specs=[
            pl.BlockSpec((rows, side), lambda i: (0, 0), pipeline_mode=pl.Buffered(1)),
            pl.BlockSpec((rows, block), lambda i: (0, i)),
            pl.BlockSpec((side, block), lambda i: (0, i)),
        ],
        out_specs=pl.BlockSpec((local, ff, block), lambda i: (0, 0, i)),
        out_shape=jax.ShapeDtypeStruct((local, ff, width), F32),
        scratch_shapes=[pltpu.VMEM((side, rows), BF16)],
        compiler_params=pltpu.CompilerParams(vmem_limit_bytes=56 * 2**20, dimension_semantics=("arbitrary",)),
        cost_estimate=pl.CostEstimate(flops=2 * rows * width * side, bytes_accessed=20 * 2**20, transcendentals=0),
    )(d, v, got)


def pack_experts(parts, seg, room):
    local, ff, width = parts[0].shape
    side = local * seg
    block = 2 * LANES
    shape = jax.ShapeDtypeStruct

    def kernel(gate, up, down, own, both):
        for i, ref in enumerate((gate, up, down)):
            for j in range(local):
                own[i, j * seg : j * seg + ff] = ref[j]
                own[i, j * seg + ff : (j + 1) * seg] = jnp.zeros((seg - ff, block), BF16)
        both[...] = own[...]

    return pl.pallas_call(
        kernel,
        grid=(width // block,),
        in_specs=[pl.BlockSpec((local, ff, block), lambda i: (0, 0, i))] * 3,
        out_specs=[pl.BlockSpec((3, side, block), lambda i: (0, 0, i))] * 2,
        out_shape=[shape((3, side, width), BF16), shape((3, 2 * side + room, width), BF16)],
        compiler_params=pltpu.CompilerParams(vmem_limit_bytes=40 * 2**20),
        cost_estimate=pl.CostEstimate(flops=0, bytes_accessed=30 * 2**20, transcendentals=0),
    )(*parts)


def join_pair(both, other, shared):
    _, side, width = other.shape
    high, wide = shared.shape[1], 8 * LANES
    blocks = side // high

    def kernel(other_ref, shared_ref, _, out):
        @pl.when(pl.program_id(1) < blocks)
        def _():
            out[...] = other_ref[...]

        @pl.when(pl.program_id(1) == blocks)
        def _():
            out[...] = shared_ref[...]

    return pl.pallas_call(
        kernel,
        grid=(width // wide, blocks + 1),
        in_specs=[
            pl.BlockSpec((3, high, wide), lambda i, r: (0, jnp.minimum(r, blocks - 1), i)),
            pl.BlockSpec((3, high, wide), lambda i, r: (0, 0, i)),
            pl.BlockSpec(memory_space=pl.ANY),
        ],
        out_specs=pl.BlockSpec((3, high, wide), lambda i, r: (0, blocks + r, i)),
        out_shape=jax.ShapeDtypeStruct(both.shape, both.dtype),
        input_output_aliases={2: 0},
        compiler_params=pltpu.CompilerParams(vmem_limit_bytes=40 * 2**20),
        cost_estimate=pl.CostEstimate(flops=0, bytes_accessed=22 * 2**20, transcendentals=0),
    )(other, shared, both)


def after(values, *first):
    return lax.optimization_barrier((values, *first))[0]


def body(
    tokens,
    segments,
    routes,
    cotangent,
    attn_gain,
    w_query,
    w_latent,
    latent_gain,
    w_expand,
    w_output,
    ffn_gain,
    w_router,
    w_shared_gate,
    w_shared_up,
    w_shared_down,
    w_expert_gate,
    w_expert_up,
    w_expert_down,
):
    own_rows, width = tokens.shape
    peers = lax.axis_size("expert")
    shards = lax.axis_size("shard")
    ring = peers // 2
    group_len = segments.shape[0]
    experts = w_router.shape[1]
    local, _, ff = w_expert_gate.shape
    rows_dev = w_query.shape[0]
    heads = w_query.shape[1] // (NOPE + ROPE)
    half = ROPE // 2
    rank_dev = w_expand.shape[0]
    expand_cols = w_expand.shape[1]
    value_cols = heads * V_HEAD
    query_cols = heads * (NOPE + ROPE)
    me_e = lax.axis_index("expert").astype(jnp.int32)
    me_s = lax.axis_index("shard").astype(jnp.int32)
    score_scale = (NOPE + ROPE) ** (-0.5)
    shared_dev = w_shared_gate.shape[1]
    shared = shared_dev // peers
    tables = routes_of(peers, shards)
    last = []

    def send(values, way):
        return lax.ppermute(values, BOTH, tables[way])

    def step(sends, work=None, *args):
        nonlocal last
        values, args = after(([v for v, _ in sends], args), last)
        got = [send(v, way) for v, (_, way) in zip(values, sends)]
        done = work(*args) if work else None
        last = [got, done]
        return (got, done) if work else got

    plane_e = [lax.rem(me_e // 2 + ring - k, ring) * 2 + lax.rem(me_e, 2) for k in range(ring)]
    piece_e = plane_e + [e ^ 1 for e in plane_e]
    shard_order = [me_s, me_s ^ 2, me_s ^ 1, me_s ^ 3]
    places = jnp.stack([*piece_e, *shard_order]).astype(jnp.int32)
    piece_of = jnp.stack(
        [lax.rem(me_e // 2 + ring - e // 2, ring) + ring * (lax.rem(me_e, 2) ^ (e % 2)) for e in range(peers)]
    ).astype(jnp.int32)

    orders = (("y", "x"), ("x", "y"))
    zones = [list(range(k, min(k + 2, ring))) for k in range(0, ring, 2)]
    calls = 2 * len(zones)

    def zone_halves(planes):
        zone = jnp.stack(planes)
        n = zone.shape[1] // 2
        return [zone[:, i * n : (i + 1) * n].reshape(zone.shape[0] * n, zone.shape[2]) for i in range(2)]

    def firsts(halves):
        return [(half, one) for half, (one, _) in zip(halves, orders)]

    def nears(halves, got):
        return [jnp.concatenate([half, g], axis=0) for half, g in zip(halves, got)]

    def split_half(near):
        n = near.shape[0] // 2
        return near[:n], near[n:]

    few = pad_to(ROPE + experts + 3, LANES)
    latent_own = lax.dynamic_slice_in_dim(w_latent, me_s * LANES, LANES, 1)
    gain_cols = jnp.stack([attn_gain, ffn_gain, jnp.pad(latent_gain, (0, rows_dev - rank_dev))], axis=1)
    small = jnp.concatenate(
        [
            latent_own,
            w_latent[:, KV_RANK:],
            w_router,
            gain_cols,
            jnp.zeros((rows_dev, few - ROPE - experts - 3), BF16),
        ],
        axis=1,
    )
    q3 = w_query.reshape(rows_dev, heads, NOPE + ROPE)
    main = jnp.concatenate(
        [
            q3[..., :NOPE].reshape(rows_dev, -1),
            q3[..., NOPE : NOPE + half].reshape(rows_dev, -1),
            q3[..., NOPE + half :].reshape(rows_dev, -1),
            w_output.T,
            jnp.concatenate([w_expand[:, h * (NOPE + V_HEAD) : (h + 1) * (NOPE + V_HEAD)] for h in range(heads)], axis=0),
        ],
        axis=1,
    )
    seg = pad_to(ff, LANES)
    side = seg * local
    tail = pad_to(shared, LANES)
    expert_parts = [w_expert_gate.transpose(0, 2, 1), w_expert_up.transpose(0, 2, 1), w_expert_down]
    ahead = [lax.rem(me_e // 2 + k, ring) * 2 + lax.rem(me_e, 2) for k in range(ring)]
    shared_pack = pick_pieces(
        jnp.stack(ahead + [e ^ 1 for e in ahead]).astype(jnp.int32),
        [
            w_shared_gate.T.reshape(peers, shared, rows_dev),
            w_shared_up.T.reshape(peers, shared, rows_dev),
            w_shared_down.reshape(peers, shared, rows_dev),
        ],
    )
    shared_keep, shared_away = shared_pack[:ring], shared_pack[ring:]
    lane_experts = jnp.arange(experts, dtype=jnp.int32)
    routed_own = jnp.any(routes[:, :, None] == lane_experts[None, None, :], axis=1)
    grad_pack = jnp.concatenate(
        [cotangent, jnp.pad(routed_own.astype(BF16), ((0, 0), (0, LANES - experts)))], axis=1
    )

    def pack(*parts):
        return pack_experts(parts, seg, 2 * tail)

    got = step([(tokens, "x"), (grad_pack, "ring"), (shared_away, "y")])
    token_near = jnp.concatenate([tokens, got[0]], axis=0)
    grad_blocks = [grad_pack, got[1]]
    grad_halves = zone_halves(grad_blocks)
    shared_ways = [jnp.stack([shared_keep[k], got[2][k]]) for k in range(ring)]

    def places_in_group():
        order = jnp.concatenate([s * own_rows + jnp.arange(own_rows, dtype=jnp.int32) for s in shard_order])
        segment = jnp.concatenate(
            [lax.dynamic_slice_in_dim(segments, s * own_rows, own_rows, 0) for s in shard_order], axis=0
        )
        place = positions(segments)
        place = jnp.concatenate(
            [lax.dynamic_slice_in_dim(place, s * own_rows, own_rows, 0) for s in shard_order], axis=0
        )
        cos, sin = angles(place, ROPE)
        return (
            jnp.tile(cos, (1, heads)), jnp.tile(sin, (1, heads)),
            order[:, None], order[None, :], segment[:, None], segment[None, :],
        )

    piece = jnp.concatenate([main, small], axis=1)
    main_own, main_other = [piece], []
    got, (own_side, both_sides) = step(
        [(piece, "ring"), (piece, "y"), firsts(grad_halves)[0]] + [(small, k) for k in range(2, ring)],
        pack, *expert_parts,
    )
    main_own.append(got[0])
    main_other.append(got[1])
    grad_first = [got[2]]
    main_cols = main.shape[1]
    small_far = jnp.concatenate(got[3:], axis=0)

    got, around = step(
        [
            (main_own[1][:, :main_cols], "ring"), (main_own[1], "y"), (small_far, "y"), (token_near, "pair"),
            (own_side, "pair"),
        ],
        places_in_group,
    )
    cos, sin = around[:2]
    main_own.append(got[0])
    main_other.append(got[1])
    small_all = jnp.concatenate(
        [
            main_own[0][:, main_cols:], main_own[1][:, main_cols:], small_far,
            main_other[0][:, main_cols:], main_other[1][:, main_cols:], got[2],
        ],
        axis=0,
    )
    latent_all = small_all[:, :LANES]
    token_group = jnp.concatenate([token_near, got[3]], axis=0)
    other_side = got[4]

    got = step([(main_own[2], "ring"), (main_own[2], "y"), (latent_all, "x"), firsts(grad_halves)[1]])
    main_own.append(got[0])
    main_other.append(got[1])
    latent_x = got[2]
    grad_first.append(got[3])
    grad_nears = nears(grad_halves, grad_first)

    got = step([(main_own[3], "y"), (jnp.stack([latent_all, latent_x]), "pair"), (grad_blocks[1], "ring")])
    main_other.append(got[0])
    latent_pair = got[1]
    grad_blocks.append(got[2])
    for k in range(4, ring):
        got = step([(main_own[k - 1], "ring")])
        main_own.append(got[0])
        got = step([(main_own[k], "y")])
        main_other.append(got[0])
    mains = main_own + main_other

    gain_at = ROPE + experts
    def attend(small_in, mains_in, *args):
        return attn_forward(heads, peers, score_scale, gain_at, list(args), small_in, mains_in)

    got, outs = step(
        [(near, two) for near, (_, two) in zip(grad_nears, orders)] + [(shared_ways[k], k) for k in range(1, ring)],
        attend, small_all, mains,
        places, token_group, latent_x, latent_pair, *around,
    )
    grad_tiles = {0: list(zip(grad_nears, got))}
    shared_all = pick_pieces(
        piece_of, [jnp.stack([pieces[flip] for flip in range(2) for pieces in (shared_ways[0], *got[2:])])]
    )
    shared_all = shared_all.transpose(1, 0, 2).reshape(3, shared, width)
    shared_own = jnp.pad(shared_all, ((0, 0), (0, tail - shared), (0, 0)))
    saved, attn_weights = outs[2:10], outs[12:]
    gain_attn, gain_ffn, gain_latent = outs[10][0:1], outs[10][1:2], outs[11]
    router_w = outs[15][:, ROPE : ROPE + experts]
    got = step([(outs[1], "pair"), (shared_own, "pair")])
    keep, away = split_half(add(outs[0], got[0]))
    shared_both = jnp.concatenate([shared_own, got[1]], axis=1)
    def grads_near(i, turn):
        half = zone_halves([grad_blocks[k] for k in zones[i]])[turn]
        return half, orders[turn][0]

    got, both_sides = step([(away, "x"), (grad_blocks[2], "ring")], join_pair, both_sides, other_side, shared_both)
    attn_term = keep.astype(F32) + got[0].astype(F32)
    grad_blocks.append(got[1])
    own_float = tokens.astype(F32)
    hidden_one = own_float + attn_term
    scale_ffn = inverse_rms(hidden_one)
    normed_ffn = (hidden_one * scale_ffn * gain_ffn).astype(BF16)
    logits = mm(normed_ffn, router_w)
    masked = jnp.where(routed_own, logits, -1e30)
    lifted = jnp.where(routed_own, jnp.exp(masked - jnp.max(masked, axis=1, keepdims=True)), 0.0)
    gates = lifted / jnp.sum(lifted, axis=1, keepdims=True)

    router_pad = jnp.pad(router_w, ((0, 0), (0, LANES - experts)))
    first_expert = (me_e * local).reshape(1)
    row_blocks = [normed_ffn]
    next_halves = [grads_near(1, turn) for turn in range(2)]
    got = step([(normed_ffn, "ring"), *next_halves])
    row_blocks.append(got[0])
    grad_nears = nears([half for half, _ in next_halves], got[1:])
    row_halves = zone_halves(row_blocks)
    got = step(firsts(row_halves) + [(row_blocks[1], "ring")])
    row_nears = nears(row_halves, got)
    row_blocks.append(got[2])
    got = step([(near, two) for near, (_, two) in zip(row_nears, orders)] + [(row_blocks[2], "ring")])
    row_tiles = {0: list(zip(row_nears, got))}
    row_blocks.append(got[2])

    for _ in range(4, ring):
        got = step([(row_blocks[-1], "ring"), (grad_blocks[-1], "ring")])
        row_blocks.append(got[0])
        grad_blocks.append(got[1])

    kept = None
    dx, dx_near, dx_home, outs_of, out_near, out_home = {}, {}, {}, {}, {}, {}
    for_pair, from_pair = [], []

    last_call = calls - 1

    def modes(call):
        if call < 2:
            return "ring", "ring"
        return ("near", "far") if call == last_call else ("far", "far")

    def moves(jobs):
        sends = []
        for what, call, stage in jobs:
            one, two = orders[call % 2]
            mode = modes(call)[what == "out"]
            ways = {"far": (two, one), "near": (one, two), "ring": (-1, two, one)}[mode]
            parts, near = (dx, dx_near) if what == "dx" else (outs_of, out_near)
            value = parts[call][1] if stage == 1 else split_half(near[call])[1]
            sends.append((value, ways[stage - 1]))

        def arrived(got):
            for (what, call, stage), g in zip(jobs, got):
                parts, near, home = (dx, dx_near, dx_home) if what == "dx" else (outs_of, out_near, out_home)
                if stage == 1:
                    near[call] = add(parts[call][0], g)
                elif stage == 2 and modes(call)[what == "out"] == "ring":
                    near[call] = add(split_half(near[call])[0], g)
                else:
                    home[call] = add(split_half(near[call])[0], g)

        return sends, arrived

    plan = {
        1: [("dx", 0, 1), ("out", 0, 1)],
        2: [("dx", 1, 1), ("dx", 0, 2), ("out", 0, 2)],
        3: [("out", 1, 1), ("dx", 1, 2), ("dx", 0, 3), ("out", 0, 3), ("dx", 2, 1)],
        4: [("out", 1, 2), ("dx", 1, 3)],
        5: [("out", 1, 3)],
    }
    for call in range(calls):
        i, turn = call // 2, call % 2
        more = i + 1 < len(zones)
        jobs = list(plan.get(call, []))
        if call >= 4:
            jobs += [("dx", call - 1, 1), ("dx", call - 2, 2), ("out", call - 2, 1)]
            jobs += [("out", call - 3, 2)] if call >= 5 else []
        sends = []
        if turn == 0 and more:
            row_halves = zone_halves([row_blocks[k] for k in zones[i + 1]])
            sends += firsts(row_halves) + [(near, two) for near, (_, two) in zip(grad_nears, orders)]
        if turn == 1 and more:
            sends += [(near, two) for near, (_, two) in zip(row_nears, orders)]
            if i + 2 < len(zones):
                next_halves = [grads_near(i + 2, turn) for turn in range(2)]
                sends += next_halves
        moved, arrived = moves(jobs)

        def tile(rows, grads, kept_in, call=call):
            return ffn_tile(
                first_expert, rows, grads, router_pad, both_sides, local, call, calls, kept_in, *modes(call)
            )

        got, (outs, kept) = step(moved + sends, tile, row_tiles[i][turn], grad_tiles[i][turn], kept)
        arrived(got)
        got = got[len(moved) :]
        dx[call], outs_of[call] = outs[:2], outs[2:4]
        if turn == 0 and more:
            row_nears = nears(row_halves, got)
            grad_tiles[i + 1] = list(zip(grad_nears, got[2:]))
        if turn == 1 and more:
            row_tiles[i + 1] = list(zip(row_nears, got))
            if i + 2 < len(zones):
                grad_nears = nears([half for half, _ in next_halves], got[2:])

    def planes_of(home, i, turn):
        part = home[2 * i + turn]
        if i == 0:
            return {0: part}
        part = part.reshape(len(zones[i]), -1, part.shape[1])
        return {k: part[j] for j, k in enumerate(zones[i])}

    def summed(terms):
        total = terms[0].astype(F32)
        for term in terms[1:]:
            total = total + term.astype(F32)
        return total

    def weight_part(d, v):
        return t_mm(d.reshape(-1, d.shape[-1])[:, side:], v.reshape(-1, v.shape[-1])).astype(BF16)

    x_all, g_all, hs_all, dg_all, du_all = kept
    dx_terms, out_terms = {0: [], 1: []}, {0: [], 1: []}

    def homeward(home, keys):
        return [(planes_of(home, i, turn)[k], -k) for i, turn, k in keys]

    late = range(1, len(zones) - 1)
    jobs = [("dx", last_call, 1), ("dx", last_call - 1, 2)]
    jobs += [("out", 1, 2)] if 1 not in out_near or out_near[1].shape[0] == 4 * own_rows // 2 else []
    moved, arrived = moves(jobs)
    keys = [(i, turn, k) for i in late for turn in range(2) for k in zones[i]]
    got, part = step(moved + homeward(dx_home, keys), weight_part, dg_all, x_all)
    arrived(got)
    for (_, turn, _), g in zip(keys, got[len(jobs) :]):
        dx_terms[turn].append(g)
    for_pair.append(part)

    jobs = [("dx", last_call, 2)] + [(what, 1, 3) for what, home in (("dx", dx_home), ("out", out_home)) if 1 not in home]
    moved, arrived = moves(jobs)
    keys = [(len(zones) - 1, 0, k) for k in zones[-1]]
    got, part = step(
        moved + homeward(dx_home, keys) + [(for_pair[0], "pair")], weight_part, du_all, x_all
    )
    arrived(got)
    dx_terms[0] += got[len(jobs) : -1]
    from_pair.append(got[-1])
    for_pair.append(part)

    jobs = [("out", call, 1) for call in range(2, calls) if call not in out_near]
    moved, arrived = moves(jobs)
    keys = [(len(zones) - 1, 1, k) for k in zones[-1]]
    got, part = step(
        moved + homeward(dx_home, keys) + [(for_pair[1], "pair")], weight_part, hs_all, g_all
    )
    arrived(got)
    dx_terms[1] += got[len(jobs) : -1]
    from_pair.append(got[-1])
    for_pair.append(part)

    d_rows = jnp.concatenate([summed([dx_home[turn], *dx_terms[turn]]) for turn in range(2)], axis=0)
    d_normed = d_rows[:, :width]
    d_gates = d_rows[:, width : width + experts]
    grad_in = cotangent.astype(F32)
    d_logits = (gates * (d_gates - jnp.sum(gates * d_gates, axis=1, keepdims=True))).astype(BF16)
    d_normed = d_normed + mm_t(d_logits, router_w)
    d_norm, grad_gain_ffn = norm_back(hidden_one, scale_ffn, gain_ffn, d_normed)
    d_hidden_one = grad_in + d_norm
    d_attn_own = d_hidden_one.astype(BF16)
    moved, arrived = moves([("out", call, 2) for call in range(2, last_call) if call not in out_home])
    got = step([(d_attn_own, "x"), (for_pair[2], "pair")] + moved)
    d_near = jnp.concatenate([d_attn_own, got[0]], axis=0)
    from_pair.append(got[1])
    arrived(got[2:])
    got = step([(d_near, "pair")])
    d_attn_group = jnp.concatenate([d_near, got[0]], axis=0)
    shared_back = jnp.concatenate(
        [
            add(own[side : side + shared], g[side + tail : side + tail + shared]).reshape(shared, peers, rows_dev)
            for own, g in zip(for_pair, from_pair)
        ],
        axis=0,
    ).transpose(1, 0, 2)
    g_output = t_mm(d_attn_group, saved[5]).astype(BF16)
    g_output = [lax.dynamic_slice_in_dim(g_output, e * rows_dev, rows_dev, 0) for e in piece_e]

    def attend_back(*args):
        return attn_backward(heads, peers, score_scale, gain_at, rows_dev, list(args))

    keys = [(i, turn, k) for i in range(1, len(zones)) for turn in range(2) for k in zones[i] if 2 * i + turn < last_call]
    moved, arrived = moves([("out", last_call, 2)])
    shared_home = lax.all_to_all(shared_back, "expert", 0, 0, tiled=True).astype(F32)
    got, (g_mains, g_others, (near_keep, near_send, d_in_keep, d_in_send)) = step(
        [(jnp.concatenate(g_output[ring:], axis=0), "y")] + moved + homeward(out_home, keys), attend_back,
        places, d_attn_group, *attn_weights, gain_latent, cos, sin, *saved[:5], *saved[6:], normed_ffn,
        jnp.pad(d_logits, ((0, 0), (ROPE, few - ROPE - experts))), token_group, grad_gain_ffn.reshape(1, width),
    )
    output_parts = [add(g_output[k], got[0][k * rows_dev : (k + 1) * rows_dev]) for k in range(ring)]
    arrived(got[1:2])
    for (_, turn, _), g in zip(keys, got[2:]):
        out_terms[turn].append(g)

    def own_part(d, v, g):
        return expert_grad(d.reshape(-1, d.shape[-1]), v.reshape(-1, v.shape[-1]), g, local, ff, seg)

    order = [*range(1, ring), 0]

    def two_parts(i, got):
        return [add(g_mains[k], got[j * rows_dev : (j + 1) * rows_dev]) for j, k in enumerate(order[2 * i : 2 * i + 2])]

    keys = [(len(zones) - 1, 1, k) for k in zones[-1]]
    got, grad_gate = step(
        [(g_others[0], "y"), (near_send, "pair"), (d_in_send, "pair"), *homeward(out_home, keys)],
        own_part, dg_all, x_all, from_pair[0],
    )
    main_parts = two_parts(0, got[0])
    near = add(near_keep, got[1])
    keep, d_away = split_half(add(d_in_keep, got[2]))
    few_away = jnp.concatenate([near[1:2], near[2:]], axis=0)
    few_keep = jnp.concatenate([near[0:1], near[2:]], axis=0)
    out_terms[1] += got[3:]
    ffn_out = jnp.concatenate([summed([out_home[turn], *out_terms[turn]]) for turn in range(2)], axis=0)
    block_out = (hidden_one + ffn_out).astype(BF16)

    got, grad_up = step(
        [(g_others[1], "y"), (few_away, "x"), (main_parts[0], "ring"), (output_parts[order[0]], "ring")],
        own_part, du_all, x_all, from_pair[1],
    )
    main_parts += two_parts(1, got[0])
    few_sum = add(few_keep, got[1])
    few_sum = jnp.concatenate([few_sum[j] for j in range(few_sum.shape[0])], axis=1)
    total = add(main_parts[1], got[2])
    total_out = add(output_parts[order[1]], got[3])

    few_half = few_sum.shape[0] // 2
    got, grad_down = step(
        [(few_sum[few_half:], "y"), (d_away, "x"), (total, "ring"), (total_out, "ring")],
        own_part, hs_all, g_all, from_pair[2],
    )
    few_sum = add(few_sum[:few_half], got[0])
    few_planes = [few_sum[k * rows_dev : (k + 1) * rows_dev] for k in range(ring)]
    d_normed_in = keep.astype(F32) + got[1].astype(F32)
    total = add(main_parts[2], got[2])
    total_out = add(output_parts[order[2]], got[3])

    got = step([(total, "ring"), (total_out, "ring"), *((few_planes[k], -k) for k in range(1, ring))])
    total = add(main_parts[3], got[0])
    total_out = add(output_parts[order[3]], got[1])
    few_home = summed([few_planes[0], *got[2:]])
    latent_home = few_home[:, :LANES].astype(BF16)
    for i in range(2, ring // 2):
        got = step([(g_others[i], "y")])
        parts = two_parts(i, got[0])
        for j, part in zip(order[2 * i : 2 * i + 2], parts):
            got = step([(total, "ring"), (total_out, "ring")])
            total = add(part, got[0])
            total_out = add(output_parts[j], got[1])
    home, home_out = total.astype(F32), total_out.astype(F32)

    got = step([(latent_home, "x")])
    latent_two = jnp.stack([latent_home, got[0]])
    got = step([(latent_two, "pair")])
    latent_four = jnp.concatenate([latent_two, got[0]], axis=0)
    grad_latent = jnp.zeros((shards, rows_dev, LANES), BF16)
    for r in range(shards):
        grad_latent = lax.dynamic_update_slice_in_dim(grad_latent, latent_four[r : r + 1], shard_order[r], 0)
    grad_latent = jnp.concatenate([*(grad_latent[j] for j in range(shards)), few_home[:, LANES : LANES + ROPE].astype(BF16)], axis=1)
    grad_router = few_home[:, LANES + ROPE : LANES + ROPE + experts].astype(F32)
    d_token, _ = norm_back(own_float, inverse_rms(own_float), gain_attn, d_normed_in)
    tokens_grad = d_hidden_one + d_token
    gain_home = few_home[:, LANES + gain_at : LANES + gain_at + 3].astype(F32).T

    grad_experts = [grad_gate, grad_up, grad_down]
    grad_shared = [shared_home[:, i * shared : (i + 1) * shared].reshape(shared_dev, rows_dev) for i in range(3)]

    nope_cols = heads * NOPE
    rope_cols = heads * half
    gq = home[:, :query_cols]
    grad_query_own = jnp.concatenate(
        [
            gq[:, :nope_cols].reshape(rows_dev, heads, NOPE),
            gq[:, nope_cols : nope_cols + rope_cols].reshape(rows_dev, heads, half),
            gq[:, nope_cols + rope_cols :].reshape(rows_dev, heads, half),
        ],
        axis=2,
    ).reshape(rows_dev, query_cols)
    g_expand = home[:, query_cols:]
    return (
        block_out,
        tokens_grad,
        gain_home[0],
        grad_query_own,
        grad_latent.astype(F32),
        gain_home[2, :rank_dev],
        jnp.concatenate([g_expand[h * rank_dev : (h + 1) * rank_dev] for h in range(heads)], axis=1),
        home_out.T,
        gain_home[1],
        grad_router,
        grad_shared[0].T,
        grad_shared[1].T,
        grad_shared[2],
        grad_experts[0].transpose(0, 2, 1),
        grad_experts[1].transpose(0, 2, 1),
        grad_experts[2],
    )


def solution(mesh):
    rows = P(("expert", "shard"), None)
    return jax.shard_map(
        body,
        mesh=mesh,
        in_specs=(
            rows,
            P("expert"),
            rows,
            rows,
            P("expert"),
            P("expert", "shard"),
            P("expert", None),
            P("expert"),
            P("expert", "shard"),
            P("shard", "expert"),
            P("expert"),
            P("expert", None),
            P("expert", "shard"),
            P("expert", "shard"),
            P("shard", "expert"),
            P("expert", None, "shard"),
            P("expert", None, "shard"),
            P("expert", "shard", None),
        ),
        out_specs=(
            rows,
            rows,
            P("expert"),
            P("expert", "shard"),
            P("expert", None),
            P("expert"),
            P("expert", "shard"),
            P("shard", "expert"),
            P("expert"),
            P("expert", None),
            P("expert", "shard"),
            P("expert", "shard"),
            P("shard", "expert"),
            P("expert", None, "shard"),
            P("expert", None, "shard"),
            P("expert", "shard", None),
        ),
        check_vma=False,
    )
```

```python
import jax
import jax.numpy as jnp
from jax import lax
from jax.experimental import pallas as pl
from jax.experimental.pallas import tpu as pltpu
from jax.sharding import PartitionSpec as P

NOPE = 128
ROPE = 64
V_HEAD = 128
KV_RANK = 512
TOP = 6
LANES = 128

epsilon = 1e-06
F32 = jnp.float32
BF16 = jnp.bfloat16


def pad_to(n, m):
    return -(-n // m) * m


def angles(places, width):
    half_width = width // 2
    spacing = 10000.0 ** (-2.0 * jnp.arange(half_width, dtype=F32) / width)
    turned = places.astype(F32)[:, None] * spacing[None, :]
    return (jnp.cos(turned), jnp.sin(turned))


def positions(segment):
    indices = jnp.arange(segment.shape[0], dtype=jnp.int32)
    prompt_len = jnp.sum((segment == 0).astype(jnp.int32))
    earlier = jnp.sum((segment[None, :] < segment[:, None]).astype(jnp.int32), axis=1)
    return jnp.where(segment == 0, indices, prompt_len + indices - earlier)


def inverse_rms(values):
    return lax.rsqrt(jnp.mean(values * values, axis=-1, keepdims=True) + epsilon)


def norm_back(values, scaling, gain, incoming):
    weighted = incoming * gain
    inner = jnp.mean(weighted * values, axis=-1, keepdims=True)
    return (
        scaling * weighted - values * scaling**3 * inner,
        jnp.sum(incoming * values * scaling, axis=0),
    )


def dot(a, b, dims):
    return lax.dot_general(a, b, (dims, ((), ())), preferred_element_type=F32)


def mm(a, b):
    return dot(a, b, ((1,), (0,)))


def mm_t(a, b):
    return dot(a, b, ((1,), (1,)))


def t_mm(a, b):
    return dot(a, b, ((0,), (0,)))


BOTH = ("expert", "shard")


def add(a, b):
    return (a.astype(F32) + b.astype(F32)).astype(BF16)


def routes_of(peers, shards):
    def table(step):
        return [
            (e * shards + s, step(e, s)[0] * shards + step(e, s)[1])
            for e in range(peers)
            for s in range(shards)
        ]

    ring = peers // 2

    def around(k):
        return table(lambda e, s: ((e // 2 + k) % ring * 2 + e % 2, s))

    return {
        "y": table(lambda e, s: (e ^ 1, s)),
        "x": table(lambda e, s: (e, s ^ 2)),
        "pair": table(lambda e, s: (e, s ^ 1)),
        "ring": around(1),
        **{k: around(k) for k in range(1 - ring, ring)},
    }


def spread(values, first, lane):
    kept = jnp.where((lane >= first) & (lane < first + ROPE // 2), values, 0.0)
    kept = kept + pltpu.roll(kept, ROPE // 2, 1)
    return kept + pltpu.roll(kept, ROPE, 1)


def attn_forward_kernel(
    heads, peers, score_scale,
    places, tokens, latent_x, latent_pair, cos, sin, index_c, index_r, segment_c, segment_r,
    small, mains,
    part_keep, part_send, normed_o, query_o, key_rope_o, expanded_o, soft_o, mixed_o, compressed_o, latent_o,
    gains, gain_latent, query_w, output_t, expand_w, extra_w, latent_w,
    *, gain_at,
):
    group = tokens.shape[0]
    rank = KV_RANK // peers
    rows = mains[0].shape[0]
    shards = latent_w.shape[0]
    cut = (query_w.shape[1], query_w.shape[1] + output_t.shape[1])
    for p in range(peers):
        to = pl.ds(pl.multiple_of(places[p] * rows, rows), rows)
        query_w[to, :] = mains[p][:, : cut[0]]
        output_t[to, :] = mains[p][:, cut[0] : cut[1]]
        expand_w[to, :] = mains[p][:, cut[1] : cut[1] + expand_w.shape[1]]
        at = slice(p * rows, (p + 1) * rows)
        latent_w[places[peers], to, :] = small[at, :LANES]
        extra_w[to, :] = small[at, LANES:]
        latent_w[places[peers + 1], to, :] = latent_x[at]
        latent_w[places[peers + 2], to, :] = latent_pair[0, at]
        latent_w[places[peers + 3], to, :] = latent_pair[1, at]
    block, at = gain_at // LANES * LANES, gain_at % LANES
    gains[...] = extra_w[:, block : block + LANES].astype(F32).T[at : at + 8]
    few_rows = [extra_w[p * rows : p * rows + rank, block : block + LANES] for p in range(peers)]
    gain_latent[...] = jnp.concatenate(few_rows, axis=0).astype(F32).T[at + 2 : at + 3]
    x = tokens[...].astype(F32)
    x = x * lax.rsqrt(jnp.mean(x * x, axis=1, keepdims=True) + epsilon) * gains[0:1]
    normed_o[...] = x.astype(BF16)
    normed = normed_o[...]
    lane = lax.broadcasted_iota(jnp.int32, (1, LANES), 1)
    c, s = cos[...], sin[...]
    raw = mm(normed, extra_w[:, :LANES])
    a, b = spread(raw, 0, lane), spread(raw, ROPE // 2, lane)
    key_rope_o[:, :LANES] = (a * c - b * s).astype(BF16)
    key_rope_o[:, LANES:] = (b * c + a * s).astype(BF16)
    for j in range(shards):
        compressed_o[:, j * LANES : (j + 1) * LANES] = mm(normed, latent_w[j])
    u = compressed_o[...]
    r = lax.rsqrt(jnp.mean(u * u, axis=1, keepdims=True) + epsilon)
    latent_o[...] = (u * r * gain_latent[...]).astype(BF16)
    q = mm(normed, query_w[...])
    nope = heads * NOPE
    query_o[:, :nope] = q[:, :nope].astype(BF16)
    a, b = q[:, nope : nope + LANES], q[:, nope + LANES :]
    query_o[:, nope : nope + LANES] = (a * c - b * s).astype(BF16)
    query_o[:, nope + LANES :] = (b * c + a * s).astype(BF16)
    allowed = (index_r[...] <= index_c[...]) & ((segment_r[...] == 0) | (segment_r[...] == segment_c[...]))
    lane2 = lax.rem(lax.broadcasted_iota(jnp.int32, (1, 2 * LANES), 1), LANES)
    for h in range(heads):
        w = jnp.concatenate(
            [expand_w[pl.ds((e * heads + h) * rank, rank), :] for e in range(peers)], axis=0
        )
        expanded_o[h] = mm(latent_o[...], w).astype(BF16)
        key_rope = jnp.where((lane2 >= h * ROPE // 2) & (lane2 < (h + 1) * ROPE // 2), key_rope_o[...], jnp.zeros((), BF16))
        scores = mm_t(query_o[:, h * NOPE : (h + 1) * NOPE], expanded_o[h, :, :NOPE]) + mm_t(query_o[:, nope:], key_rope)
        scores = jnp.where(allowed, scores * score_scale, -1e30)
        raised = jnp.exp(scores - jnp.max(scores, axis=1, keepdims=True))
        soft = raised * (1.0 / jnp.sum(raised, axis=1, keepdims=True))
        soft_o[h] = soft
        mixed_o[:, h * V_HEAD : (h + 1) * V_HEAD] = mm(soft.astype(BF16), expanded_o[h, :, NOPE:]).astype(BF16)
    half = group // 2
    part_keep[...] = mm_t(mixed_o[:half], output_t[...]).astype(BF16)
    part_send[...] = mm_t(mixed_o[half:], output_t[...]).astype(BF16)


def attn_backward_kernel(
    heads, peers, score_scale,
    places, d_attn, query_w, output_t, expand_w, extra_w, latent_w, gain_latent, cos, sin,
    normed, query, key_rope_all, expanded, soft_all, compressed, latent,
    normed_ffn, d_logits, tokens, g_gain_ffn,
    g_mains, near_keep, near_send, d_in_keep, d_in_send,
    g_all, g_few, d_query_s, d_latent_s, d_use_s,
    *, gain_at,
):
    group = d_attn.shape[0]
    rank = KV_RANK // peers
    shards = latent_w.shape[0]
    nope = heads * NOPE
    lane = lax.broadcasted_iota(jnp.int32, (1, LANES), 1)
    lane2 = lax.rem(lax.broadcasted_iota(jnp.int32, (1, 2 * LANES), 1), LANES)
    rows = g_mains[0][0].shape[0]
    query_cols = query_w.shape[1]
    width = d_attn.shape[1]
    strips = [slice(lo, lo + width // 4) for lo in range(0, width, width // 4)]
    expand_cols = expand_w.shape[1]
    d_mixed = mm(d_attn[...], output_t[...]).astype(BF16)
    d_query_rope = jnp.zeros((group, 2 * LANES), F32)
    d_key_rope = jnp.zeros((group, 2 * LANES), F32)
    for h in range(heads):
        mine = (lane2 >= h * ROPE // 2) & (lane2 < (h + 1) * ROPE // 2)
        key_rope = jnp.where(mine, key_rope_all[...], jnp.zeros((), BF16))
        soft = soft_all[h]
        d_out = d_mixed[:, h * V_HEAD : (h + 1) * V_HEAD]
        d_soft = mm_t(d_out, expanded[h, :, NOPE:])
        d_scores = score_scale * soft * (d_soft - jnp.sum(soft * d_soft, axis=1, keepdims=True))
        d_scores = d_scores.astype(BF16)
        d_query_s[:, h * NOPE : (h + 1) * NOPE] = mm(d_scores, expanded[h, :, :NOPE]).astype(BF16)
        d_query_rope = d_query_rope + mm(d_scores, key_rope)
        both = jnp.concatenate([query[:, h * NOPE : (h + 1) * NOPE], query[:, nope:]], axis=1)
        d_key = t_mm(d_scores, both)
        d_key_rope = d_key_rope + jnp.where(mine, d_key[:, NOPE:], 0.0)
        d_values = t_mm(soft.astype(BF16), d_out)
        d_expanded = jnp.concatenate([d_key[:, :NOPE], d_values], axis=1).astype(BF16)
        w = jnp.concatenate(
            [expand_w[pl.ds((e * heads + h) * rank, rank), :] for e in range(peers)], axis=0
        )
        g_w = t_mm(latent[...], d_expanded).astype(BF16)
        for e in range(peers):
            g_all[pl.ds((e * heads + h) * rank, rank), :expand_cols] = g_w[e * rank : (e + 1) * rank]
        back = mm_t(d_expanded, w)
        if h == 0:
            d_use_s[...] = back
        else:
            d_use_s[...] += back
    for p in range(peers):
        ref, to = g_mains[p]
        ref[to : to + rows, query_cols:] = g_all[pl.ds(pl.multiple_of(places[p] * rows, rows), rows), :expand_cols]
    c, s = cos[...], sin[...]
    a, b = d_query_rope[:, :LANES], d_query_rope[:, LANES:]
    d_query_s[:, nope : nope + LANES] = (a * c + b * s).astype(BF16)
    d_query_s[:, nope + LANES :] = (b * c - a * s).astype(BF16)
    u, n = compressed[...], d_use_s[...]
    r = lax.rsqrt(jnp.mean(u * u, axis=1, keepdims=True) + epsilon)
    weighted = n * gain_latent[...]
    inner = jnp.mean(weighted * u, axis=1, keepdims=True)
    g_gain_latent = jnp.sum(n * u * r, axis=0, keepdims=True)
    d_latent_s[...] = (r * weighted - u * (r * r * r * inner)).astype(BF16)

    def folded(v):
        v = v + pltpu.roll(v, ROPE // 2, 1)
        return v + pltpu.roll(v, ROPE, 1)

    a, b = folded(d_key_rope[:, :LANES]), folded(d_key_rope[:, LANES:])
    d_extra = jnp.where(
        lane < ROPE // 2, a * c + b * s, jnp.where(lane < ROPE, b * c - a * s, 0.0)
    ).astype(BF16)
    half = group // 2
    g_gain_attn = jnp.zeros((1, tokens.shape[1]), F32)
    fine = half // 2
    for lo in range(0, group, fine):
        part, to = slice(lo, lo + fine), (d_in_keep if lo < half else d_in_send).at[pl.ds(lo % half, fine)]
        total = mm_t(d_query_s[part], query_w[...]) + mm_t(d_extra[part], extra_w[:, :LANES])
        for j in range(shards):
            total = total + mm_t(d_latent_s[part, j * LANES : (j + 1) * LANES], latent_w[j])
        to[...] = total.astype(BF16)
        x = tokens[part].astype(F32)
        x = x * lax.rsqrt(jnp.mean(x * x, axis=1, keepdims=True) + epsilon)
        g_gain_attn = g_gain_attn + jnp.sum(total * x, axis=0, keepdims=True)
    for strip in strips:
        g_all[strip, :] = t_mm(normed[:, strip], d_query_s[...]).astype(BF16)
    wide = extra_w.shape[1] // LANES
    line = lax.broadcasted_iota(jnp.int32, (LANES, 1), 0)
    at_line = gain_at % LANES
    for j in range(wide):
        g_extra = t_mm(normed_ffn[...], d_logits[:, j * LANES : (j + 1) * LANES])
        if j == 0:
            g_extra = g_extra + t_mm(normed[...], d_extra)
        if j == gain_at // LANES:
            both = jnp.where(line == at_line, g_gain_attn, jnp.where(line == at_line + 1, g_gain_ffn[...], 0.0))
            g_extra = g_extra + both.T
        g_few[shards + j] = g_extra.astype(BF16)
    tall = jnp.where(line == at_line + 2, g_gain_latent, 0.0).T.astype(BF16)
    j = shards + gain_at // LANES
    for e in range(peers):
        at = slice(e * rows, e * rows + rank)
        g_few[j, at] = g_few[j, at] + tall[e * rank : (e + 1) * rank]
    for strip in strips:
        g_lat = t_mm(normed[:, strip], d_latent_s[...]).astype(BF16)
        for j in range(shards):
            g_few[j, strip] = g_lat[:, j * LANES : (j + 1) * LANES]
    for p in range(peers):
        at = pl.ds(pl.multiple_of(places[p] * rows, rows), rows)
        to = slice(p * rows, (p + 1) * rows)
        ref, down = g_mains[p]
        ref[down : down + rows, :query_cols] = g_all[at, :]
        for j in range(2):
            near_keep[j, to] = g_few[places[peers + j], at, :]
            near_send[j, to] = g_few[places[peers + 2 + j], at, :]
        for j in range(wide):
            near_keep[2 + j, to] = g_few[shards + j, at, :]
            near_send[2 + j, to] = g_few[shards + j, at, :]


def in_vmem(kernel, outs, scratch, flops, args):
    spec = pl.BlockSpec(memory_space=pltpu.VMEM)
    return pl.pallas_call(
        kernel,
        in_specs=[pl.BlockSpec(memory_space=pltpu.SMEM)] + [spec] * (len(args) - 1),
        out_specs=[spec] * len(outs),
        out_shape=outs,
        scratch_shapes=scratch,
        compiler_params=pltpu.CompilerParams(vmem_limit_bytes=60 * 2**20),
        cost_estimate=pl.CostEstimate(flops=flops, bytes_accessed=24 * 2**20, transcendentals=2**20),
    )(*args)


def attn_forward(heads, peers, score_scale, gain_at, args, small, mains):
    group, width = args[1].shape
    query_cols = heads * (NOPE + ROPE)
    shape = jax.ShapeDtypeStruct
    outs = [
        shape((group // 2, width), BF16), shape((group // 2, width), BF16), shape((group, width), BF16),
        shape((group, query_cols), BF16), shape((group, 2 * LANES), BF16),
        shape((heads, group, NOPE + V_HEAD), BF16), shape((heads, group, group), F32),
        shape((group, heads * V_HEAD), BF16), shape((group, KV_RANK), F32), shape((group, KV_RANK), BF16),
        shape((8, width), F32), shape((1, KV_RANK), F32),
        shape((width, query_cols), BF16), shape((width, heads * V_HEAD), BF16), shape((width, NOPE + V_HEAD), BF16),
        shape((width, small.shape[1] - LANES), BF16), shape((KV_RANK // LANES, width, LANES), BF16),
    ]
    n = len(args)

    def kernel(*refs):
        attn_forward_kernel(
            heads, peers, score_scale, *refs[: n + 1], refs[n + 1 : n + 1 + peers], *refs[n + 1 + peers :],
            gain_at=gain_at,
        )

    return in_vmem(kernel, outs, [], 6 * 10**9, [*args, small, *mains])


def attn_backward(heads, peers, score_scale, gain_at, rows, args):
    group, width = args[1].shape
    query_w, output_t, expand_w, extra_w, latent_w = args[2:7]
    main = query_w.shape[1] + expand_w.shape[1]
    few = extra_w.shape[1] // LANES
    shape = jax.ShapeDtypeStruct
    ring = peers // 2
    order = [*range(1, ring), 0]
    outs = [shape((rows, main), BF16)] * ring + [shape((2 * rows, main), BF16)] * (ring // 2) + [
        shape((2 + few, width, LANES), BF16), shape((2 + few, width, LANES), BF16),
        shape((group // 2, width), BF16), shape((group // 2, width), BF16),
    ]
    scratch = [
        pltpu.VMEM((width, query_w.shape[1]), BF16),
        pltpu.VMEM((latent_w.shape[0] + few, width, LANES), BF16),
        pltpu.VMEM((group, heads * NOPE + 2 * LANES), BF16),
        pltpu.VMEM((group, KV_RANK), BF16),
        pltpu.VMEM((group, KV_RANK), F32),
    ]
    n = len(args)

    def kernel(*refs):
        pieces = [(ref, 0) for ref in refs[n : n + ring]] + [None] * ring
        for i, k in enumerate(order):
            pieces[ring + k] = (refs[n + ring + i // 2], i % 2 * rows)
        rest = refs[n + ring + ring // 2 :]
        attn_backward_kernel(heads, peers, score_scale, *refs[:n], pieces, *rest, gain_at=gain_at)

    outs = in_vmem(kernel, outs, scratch, 12 * 10**9, args)
    return outs[:ring], outs[ring : ring + ring // 2], outs[ring + ring // 2 :]


PARTS = {
    "far": ((0, 1, 2, 3), (4, 5, 6, 7)),
    "near": ((0, 1, 4, 5), (2, 3, 6, 7)),
    "ring": ((0, 2, 4, 6), (1, 3, 5, 7)),
}


def ffn_kernel(
    local, segs_side, steps, width, dx_mode, out_mode,
    first_ref, x0, x1, g0, g1, router, wg, wu, wd,
    dx_keep, dx_send, out_keep, out_send, x_all, g_all, hs_all, dg_all, du_all,
    acc_out, acc_dx, gates_s, dgates_s,
):
    j = pl.program_id(0)
    half = x0.shape[0]
    unit = half // 4
    block = wg.shape[0]
    x = jnp.concatenate([x0[...], x1[...]], axis=0)
    g_in = jnp.concatenate([g0[:, :width], g1[:, :width]], axis=0)
    first = first_ref[0]
    lane = lax.broadcasted_iota(jnp.int32, (1, LANES), 1)

    @pl.when(j == 0)
    def _():
        logits = mm(x, router[...])
        routed = jnp.concatenate([g0[:, width:], g1[:, width:]], axis=0) > 0
        masked = jnp.where(routed, logits, -1e30)
        raised = jnp.where(routed, jnp.exp(masked - jnp.max(masked, axis=1, keepdims=True)), 0.0)
        gates_s[...] = raised / jnp.sum(raised, axis=1, keepdims=True)
        dgates_s[...] = jnp.zeros_like(dgates_s)
        acc_out[...] = jnp.zeros_like(acc_out)
        acc_dx[...] = jnp.zeros_like(acc_dx)
        x_all[0] = x
        g_all[0] = g_in

    gates = gates_s[...]
    wanted, columns = [], []
    for part in range(2):
        seg = 2 * j + part
        expert = jnp.where(seg < 2 * segs_side, lax.rem(seg, segs_side) * local // segs_side, local)
        want = jnp.where(expert < local, first + expert, -1)
        column = jnp.sum(jnp.where(lane == want, gates, 0.0), axis=1, keepdims=True)
        wanted.append(want)
        columns.append(jnp.where(expert < local, column, 1.0))
    lane_block = lax.broadcasted_iota(jnp.int32, (1, block), 1)
    column = jnp.where(lane_block < LANES, columns[0], columns[1])
    gate, up, d_hidden = mm_t(x, wg[...]), mm_t(x, wu[...]), mm_t(g_in, wd[...])
    logistic = 1.0 / (1.0 + jnp.exp(-gate))
    silu = gate * logistic
    hidden = silu * up
    scaled = (hidden * column).astype(BF16)
    product = hidden * d_hidden
    for part in range(2):
        dots = jnp.sum(product[:, part * LANES : (part + 1) * LANES], axis=1, keepdims=True)
        dgates_s[...] += jnp.where(lane == wanted[part], dots, 0.0)
    d_hidden = d_hidden * column
    d_gate = (d_hidden * up * (logistic * (1.0 + gate * (1.0 - logistic)))).astype(BF16)
    d_up = (d_hidden * silu).astype(BF16)
    hs_all[0], dg_all[0], du_all[0] = scaled, d_gate, d_up
    acc_out[...] += mm(scaled, wd[...])
    acc_dx[...] += mm(d_gate, wg[...]) + mm(d_up, wu[...])

    @pl.when(j == steps - 1)
    def _():
        for (keep, away), ranges, is_dx in (
            ((dx_keep, dx_send), PARTS[dx_mode], True),
            ((out_keep, out_send), PARTS[out_mode], False),
        ):
            for ref, blocks in zip((keep, away), ranges):
                for at, block_of in enumerate(blocks):
                    to, rows = pl.ds(at * unit, unit), pl.ds(block_of * unit, unit)
                    if is_dx:
                        ref[to, :width] = acc_dx[rows].astype(BF16)
                        ref[to, width:] = dgates_s[rows].astype(BF16)
                    else:
                        ref[to] = acc_out[rows].astype(BF16)


def ffn_tile(first, rows, grads, router, weights, local, call, calls, kept, dx_mode, out_mode):
    half, width = rows[0].shape
    hid = weights.shape[1]
    block = 2 * LANES
    steps = hid // block
    segs_side = (hid // LANES - 2) // 2

    def fixed(*shape):
        return pl.BlockSpec(shape, lambda j: (0,) * len(shape), pipeline_mode=pl.Buffered(1))

    def whole(*shape):
        return pl.BlockSpec(shape, lambda j: (0,) * len(shape))

    in_specs = [
        pl.BlockSpec(memory_space=pltpu.SMEM),
        fixed(half, width), fixed(half, width), fixed(half, width + LANES), fixed(half, width + LANES), fixed(width, LANES),
        *(pl.BlockSpec((None, block, width), lambda j, i=i: (i, j, 0)) for i in range(3)),
    ]
    args = [first, *rows, *grads, router, weights, weights, weights]
    plain = len(args)
    aliases = {}
    if kept is not None:
        in_specs += [pl.BlockSpec(memory_space=pl.ANY)] * len(kept)
        args += list(kept)
        aliases = {plain + i: 4 + i for i in range(len(kept))}
    tile_rows = pl.BlockSpec((1, 2 * half, width), lambda j: (call, 0, 0))
    tile_hidden = pl.BlockSpec((1, 2 * half, block), lambda j: (call, 0, j))
    shape = jax.ShapeDtypeStruct
    out_shape = (
        [shape((half, width + LANES), BF16)] * 2
        + [shape((half, width), BF16)] * 2
        + [shape((calls, 2 * half, width), BF16)] * 2
        + [shape((calls, 2 * half, hid), BF16)] * 3
    )
    out_specs = [whole(half, width + LANES)] * 2 + [whole(half, width)] * 2 + [tile_rows] * 2 + [tile_hidden] * 3

    def kernel(*refs):
        ffn_kernel(local, segs_side, steps, width, dx_mode, out_mode, *refs[:plain], *refs[len(args) :])

    outs = pl.pallas_call(
        kernel,
        grid=(steps,),
        in_specs=in_specs,
        out_specs=out_specs,
        out_shape=out_shape,
        scratch_shapes=[pltpu.VMEM((2 * half, width), F32)] * 2
        + [pltpu.VMEM((2 * half, LANES), F32)] * 2,
        input_output_aliases=aliases,
        compiler_params=pltpu.CompilerParams(
            vmem_limit_bytes=56 * 2**20, dimension_semantics=("arbitrary",)
        ),
        cost_estimate=pl.CostEstimate(
            flops=24 * half * width * hid,
            bytes_accessed=6 * width * hid + 16 * half * width,
            transcendentals=2 * half * hid,
        ),
    )(*args)
    return outs[:4], outs[4:]


def pick_pieces(order, sources):
    n, _, lanes = sources[0].shape
    heights = [v.shape[1] for v in sources]

    def kernel(order_ref, *refs):
        for p in range(n):
            at = 0
            for ref, high in zip(refs, heights):
                refs[-1][p, at : at + high] = ref[order_ref[p]]
                at += high

    outs = [jax.ShapeDtypeStruct((n, sum(heights), lanes), BF16)]
    return in_vmem(kernel, outs, [], 0, [order, *sources])[0]


def place_pieces(places, pieces):
    _, rows, lanes = pieces[0].shape
    n = len(pieces)

    def kernel(places_ref, *refs):
        for k in range(n):
            for flip in range(2):
                refs[-1][places_ref[flip * n + k]] = refs[k][flip]

    outs = [jax.ShapeDtypeStruct((2 * n, rows, lanes), BF16)]
    return in_vmem(kernel, outs, [], 0, [places, *pieces])[0]


def output_grad(places, d_attn, mixed, rows, peers):
    width, value_cols = d_attn.shape[1], mixed.shape[1]
    ring = peers // 2

    def kernel(places_ref, d_ref, mixed_ref, own, other, total):
        for lo in range(0, width, width // 4):
            total[lo : lo + width // 4] = t_mm(d_ref[:, lo : lo + width // 4], mixed_ref[...]).astype(BF16)
        for p in range(peers):
            at = pl.ds(pl.multiple_of(places_ref[p] * rows, rows), rows)
            to = p % ring * rows
            (own if p < ring else other)[to : to + rows] = total[at, :]

    outs = [jax.ShapeDtypeStruct((ring * rows, value_cols), BF16)] * 2
    scratch = [pltpu.VMEM((width, value_cols), BF16)]
    return in_vmem(kernel, outs, scratch, 2 * 10**9, [places, d_attn, mixed])


def expert_grad(d, v, got, local, ff, seg):
    rows, width = v.shape
    side = local * seg
    block = 2 * LANES

    def kernel(d_ref, v_ref, got_ref, out, turned):
        @pl.when(pl.program_id(0) == 0)
        def _():
            turned[...] = d_ref[...].T

        total = mm(turned[...], v_ref[...]) + got_ref[...].astype(F32)
        for j in range(local):
            out[j] = total[j * seg : j * seg + ff]

    return pl.pallas_call(
        kernel,
        grid=(width // block,),
        in_specs=[
            pl.BlockSpec((rows, side), lambda i: (0, 0), pipeline_mode=pl.Buffered(1)),
            pl.BlockSpec((rows, block), lambda i: (0, i)),
            pl.BlockSpec((side, block), lambda i: (0, i)),
        ],
        out_specs=pl.BlockSpec((local, ff, block), lambda i: (0, 0, i)),
        out_shape=jax.ShapeDtypeStruct((local, ff, width), F32),
        scratch_shapes=[pltpu.VMEM((side, rows), BF16)],
        compiler_params=pltpu.CompilerParams(vmem_limit_bytes=56 * 2**20, dimension_semantics=("arbitrary",)),
        cost_estimate=pl.CostEstimate(flops=2 * rows * width * side, bytes_accessed=20 * 2**20, transcendentals=0),
    )(d, v, got)


def pack_experts(parts, seg, room):
    local, ff, width = parts[0].shape
    side = local * seg
    block = 2 * LANES
    shape = jax.ShapeDtypeStruct

    def kernel(gate, up, down, own, both):
        for i, ref in enumerate((gate, up, down)):
            for j in range(local):
                own[i, j * seg : j * seg + ff] = ref[j]
                own[i, j * seg + ff : (j + 1) * seg] = jnp.zeros((seg - ff, block), BF16)
        both[...] = own[...]

    return pl.pallas_call(
        kernel,
        grid=(width // block,),
        in_specs=[pl.BlockSpec((local, ff, block), lambda i: (0, 0, i))] * 3,
        out_specs=[pl.BlockSpec((3, side, block), lambda i: (0, 0, i))] * 2,
        out_shape=[shape((3, side, width), BF16), shape((3, 2 * side + room, width), BF16)],
        compiler_params=pltpu.CompilerParams(vmem_limit_bytes=40 * 2**20),
        cost_estimate=pl.CostEstimate(flops=0, bytes_accessed=30 * 2**20, transcendentals=0),
    )(*parts)


def join_pair(both, other, shared):
    _, side, width = other.shape
    high, wide = shared.shape[1], 8 * LANES
    blocks = side // high

    def kernel(other_ref, shared_ref, _, out):
        @pl.when(pl.program_id(1) < blocks)
        def _():
            out[...] = other_ref[...]

        @pl.when(pl.program_id(1) == blocks)
        def _():
            out[...] = shared_ref[...]

    return pl.pallas_call(
        kernel,
        grid=(width // wide, blocks + 1),
        in_specs=[
            pl.BlockSpec((3, high, wide), lambda i, r: (0, jnp.minimum(r, blocks - 1), i)),
            pl.BlockSpec((3, high, wide), lambda i, r: (0, 0, i)),
            pl.BlockSpec(memory_space=pl.ANY),
        ],
        out_specs=pl.BlockSpec((3, high, wide), lambda i, r: (0, blocks + r, i)),
        out_shape=jax.ShapeDtypeStruct(both.shape, both.dtype),
        input_output_aliases={2: 0},
        compiler_params=pltpu.CompilerParams(vmem_limit_bytes=40 * 2**20),
        cost_estimate=pl.CostEstimate(flops=0, bytes_accessed=22 * 2**20, transcendentals=0),
    )(other, shared, both)


def after(values, *first):
    return lax.optimization_barrier((values, *first))[0]


def body(
    tokens,
    segments,
    routes,
    cotangent,
    attn_gain,
    w_query,
    w_latent,
    latent_gain,
    w_expand,
    w_output,
    ffn_gain,
    w_router,
    w_shared_gate,
    w_shared_up,
    w_shared_down,
    w_expert_gate,
    w_expert_up,
    w_expert_down,
):
    own_rows, width = tokens.shape
    peers = lax.axis_size("expert")
    shards = lax.axis_size("shard")
    ring = peers // 2
    group_len = segments.shape[0]
    experts = w_router.shape[1]
    local, _, ff = w_expert_gate.shape
    rows_dev = w_query.shape[0]
    heads = w_query.shape[1] // (NOPE + ROPE)
    half = ROPE // 2
    rank_dev = w_expand.shape[0]
    expand_cols = w_expand.shape[1]
    value_cols = heads * V_HEAD
    query_cols = heads * (NOPE + ROPE)
    me_e = lax.axis_index("expert").astype(jnp.int32)
    me_s = lax.axis_index("shard").astype(jnp.int32)
    score_scale = (NOPE + ROPE) ** (-0.5)
    shared_dev = w_shared_gate.shape[1]
    shared = shared_dev // peers
    tables = routes_of(peers, shards)
    last = []

    def send(values, way):
        return lax.ppermute(values, BOTH, tables[way])

    def step(sends, work=None, *args):
        nonlocal last
        values = [v for v, _ in sends]
        if last:
            values, tied = after((values, args[:1]), last)
            args = (*tied, *args[1:])
        got = [send(v, way) for v, (_, way) in zip(values, sends)]
        done = work(*args) if work else None
        last = [got, done]
        return (got, done) if work else got

    plane_e = [lax.rem(me_e // 2 + ring - k, ring) * 2 + lax.rem(me_e, 2) for k in range(ring)]
    piece_e = plane_e + [e ^ 1 for e in plane_e]
    shard_order = [me_s, me_s ^ 2, me_s ^ 1, me_s ^ 3]
    places = jnp.stack([*piece_e, *shard_order]).astype(jnp.int32)

    orders = (("y", "x"), ("x", "y"))
    zones = [list(range(k, min(k + 2, ring))) for k in range(0, ring, 2)]
    calls = 2 * len(zones)

    def zone_halves(planes):
        zone = jnp.stack(planes)
        n = zone.shape[1] // 2
        return [zone[:, i * n : (i + 1) * n].reshape(zone.shape[0] * n, zone.shape[2]) for i in range(2)]

    def firsts(halves):
        return [(half, one) for half, (one, _) in zip(halves, orders)]

    def nears(halves, got):
        return [jnp.concatenate([half, g], axis=0) for half, g in zip(halves, got)]

    def split_half(near):
        n = near.shape[0] // 2
        return near[:n], near[n:]

    few = pad_to(ROPE + experts + 3, LANES)
    latent_own = lax.dynamic_slice_in_dim(w_latent, me_s * LANES, LANES, 1)
    gain_cols = jnp.stack([attn_gain, ffn_gain, jnp.pad(latent_gain, (0, rows_dev - rank_dev))], axis=1)
    small = jnp.concatenate(
        [
            latent_own,
            w_latent[:, KV_RANK:],
            w_router,
            gain_cols,
            jnp.zeros((rows_dev, few - ROPE - experts - 3), BF16),
        ],
        axis=1,
    )
    q3 = w_query.reshape(rows_dev, heads, NOPE + ROPE)
    main = jnp.concatenate(
        [
            q3[..., :NOPE].reshape(rows_dev, -1),
            q3[..., NOPE : NOPE + half].reshape(rows_dev, -1),
            q3[..., NOPE + half :].reshape(rows_dev, -1),
            w_output.T,
            jnp.concatenate([w_expand[:, h * (NOPE + V_HEAD) : (h + 1) * (NOPE + V_HEAD)] for h in range(heads)], axis=0),
        ],
        axis=1,
    )
    seg = pad_to(ff, LANES)
    side = seg * local
    tail = pad_to(shared, LANES)
    expert_parts = [w_expert_gate.transpose(0, 2, 1), w_expert_up.transpose(0, 2, 1), w_expert_down]
    ahead = [lax.rem(me_e // 2 + k, ring) * 2 + lax.rem(me_e, 2) for k in range(ring)]
    shared_pack = pick_pieces(
        jnp.stack(ahead + [e ^ 1 for e in ahead]).astype(jnp.int32),
        [
            w_shared_gate.T.reshape(peers, shared, rows_dev),
            w_shared_up.T.reshape(peers, shared, rows_dev),
            w_shared_down.reshape(peers, shared, rows_dev),
        ],
    )
    shared_keep, shared_away = shared_pack[:ring], shared_pack[ring:]
    lane_experts = jnp.arange(experts, dtype=jnp.int32)
    routed_own = jnp.any(routes[:, :, None] == lane_experts[None, None, :], axis=1)
    grad_pack = jnp.concatenate(
        [cotangent, jnp.pad(routed_own.astype(BF16), ((0, 0), (0, LANES - experts)))], axis=1
    )

    def pack(*parts):
        return pack_experts(parts, seg, 2 * tail)

    got = step([(tokens, "x"), (grad_pack, "ring"), (shared_away, "y")])
    token_near = jnp.concatenate([tokens, got[0]], axis=0)
    grad_blocks = [grad_pack, got[1]]
    grad_halves = zone_halves(grad_blocks)
    shared_ways = [jnp.stack([shared_keep[k], got[2][k]]) for k in range(ring)]

    def places_in_group(segments):
        order = jnp.concatenate([s * own_rows + jnp.arange(own_rows, dtype=jnp.int32) for s in shard_order])
        segment = jnp.concatenate(
            [lax.dynamic_slice_in_dim(segments, s * own_rows, own_rows, 0) for s in shard_order], axis=0
        )
        place = positions(segments)
        place = jnp.concatenate(
            [lax.dynamic_slice_in_dim(place, s * own_rows, own_rows, 0) for s in shard_order], axis=0
        )
        cos, sin = angles(place, ROPE)
        return (
            jnp.tile(cos, (1, heads)), jnp.tile(sin, (1, heads)),
            order[:, None], order[None, :], segment[:, None], segment[None, :],
        )

    piece = jnp.concatenate([main, small], axis=1)
    main_own, main_other = [piece], []
    got, (own_side, both_sides) = step(
        [(piece, "ring"), (piece, "y"), firsts(grad_halves)[0]] + [(small, k) for k in range(2, ring)],
        pack, *expert_parts,
    )
    main_own.append(got[0])
    main_other.append(got[1])
    grad_first = [got[2]]
    main_cols = main.shape[1]
    small_far = jnp.concatenate(got[3:], axis=0)

    got, around = step(
        [
            (main_own[1][:, :main_cols], "ring"), (main_own[1], "y"), (small_far, "y"), (token_near, "pair"),
            (own_side, "pair"),
        ],
        places_in_group, segments,
    )
    cos, sin = around[:2]
    main_own.append(got[0])
    main_other.append(got[1])
    small_all = jnp.concatenate(
        [
            main_own[0][:, main_cols:], main_own[1][:, main_cols:], small_far,
            main_other[0][:, main_cols:], main_other[1][:, main_cols:], got[2],
        ],
        axis=0,
    )
    latent_all = small_all[:, :LANES]
    token_group = jnp.concatenate([token_near, got[3]], axis=0)
    other_side = got[4]

    got = step([(main_own[2], "ring"), (main_own[2], "y"), (latent_all, "x"), firsts(grad_halves)[1]])
    main_own.append(got[0])
    main_other.append(got[1])
    latent_x = got[2]
    grad_first.append(got[3])
    grad_nears = nears(grad_halves, grad_first)

    got = step([(main_own[3], "y"), (jnp.stack([latent_all, latent_x]), "pair"), (grad_blocks[1], "ring")])
    main_other.append(got[0])
    latent_pair = got[1]
    grad_blocks.append(got[2])
    for k in range(4, ring):
        got = step([(main_own[k - 1], "ring")])
        main_own.append(got[0])
        got = step([(main_own[k], "y")])
        main_other.append(got[0])
    mains = main_own + main_other

    gain_at = ROPE + experts
    def attend(token_in, small_in, mains_in, places_in, *args):
        return attn_forward(heads, peers, score_scale, gain_at, [places_in, token_in, *args], small_in, mains_in)

    got, outs = step(
        [(near, two) for near, (_, two) in zip(grad_nears, orders)] + [(shared_ways[k], k) for k in range(1, ring)],
        attend, token_group, small_all, mains, places, latent_x, latent_pair, *around,
    )
    grad_tiles = {0: list(zip(grad_nears, got))}
    shared_all = place_pieces(places[:peers], [shared_ways[0], *got[2:]])
    shared_all = shared_all.transpose(1, 0, 2).reshape(3, shared, width)
    shared_own = jnp.pad(shared_all, ((0, 0), (0, tail - shared), (0, 0)))
    saved, attn_weights = outs[2:10], outs[12:]
    gain_attn, gain_ffn, gain_latent = outs[10][0:1], outs[10][1:2], outs[11]
    router_w = outs[15][:, ROPE : ROPE + experts]
    got = step([(outs[1], "pair"), (shared_own, "pair")])
    keep, away = split_half(add(outs[0], got[0]))
    shared_both = jnp.concatenate([shared_own, got[1]], axis=1)
    def grads_near(i, turn):
        half = zone_halves([grad_blocks[k] for k in zones[i]])[turn]
        return half, orders[turn][0]

    got, both_sides = step([(away, "x"), (grad_blocks[2], "ring")], join_pair, both_sides, other_side, shared_both)
    attn_term = keep.astype(F32) + got[0].astype(F32)
    grad_blocks.append(got[1])
    own_float = tokens.astype(F32)
    hidden_one = own_float + attn_term
    scale_ffn = inverse_rms(hidden_one)
    normed_ffn = (hidden_one * scale_ffn * gain_ffn).astype(BF16)
    logits = mm(normed_ffn, router_w)
    masked = jnp.where(routed_own, logits, -1e30)
    lifted = jnp.where(routed_own, jnp.exp(masked - jnp.max(masked, axis=1, keepdims=True)), 0.0)
    gates = lifted / jnp.sum(lifted, axis=1, keepdims=True)

    router_pad = jnp.pad(router_w, ((0, 0), (0, LANES - experts)))
    first_expert = (me_e * local).reshape(1)
    row_blocks = [normed_ffn]
    next_halves = [grads_near(1, turn) for turn in range(2)]
    got = step([(normed_ffn, "ring"), *next_halves])
    row_blocks.append(got[0])
    grad_nears = nears([half for half, _ in next_halves], got[1:])
    row_halves = zone_halves(row_blocks)
    got = step(firsts(row_halves) + [(row_blocks[1], "ring")])
    row_nears = nears(row_halves, got)
    row_blocks.append(got[2])
    got = step([(near, two) for near, (_, two) in zip(row_nears, orders)] + [(row_blocks[2], "ring")])
    row_tiles = {0: list(zip(row_nears, got))}
    row_blocks.append(got[2])

    for _ in range(4, ring):
        got = step([(row_blocks[-1], "ring"), (grad_blocks[-1], "ring")])
        row_blocks.append(got[0])
        grad_blocks.append(got[1])

    kept = None
    dx, dx_near, dx_home, outs_of, out_near, out_home = {}, {}, {}, {}, {}, {}
    for_pair, from_pair = [], []

    last_call = calls - 1

    def modes(call):
        if call < 2:
            return "ring", "ring"
        return ("near", "far") if call == last_call else ("far", "far")

    def moves(jobs):
        sends = []
        for what, call, stage in jobs:
            one, two = orders[call % 2]
            mode = modes(call)[what == "out"]
            ways = {"far": (two, one), "near": (one, two), "ring": (-1, two, one)}[mode]
            parts, near = (dx, dx_near) if what == "dx" else (outs_of, out_near)
            value = parts[call][1] if stage == 1 else split_half(near[call])[1]
            sends.append((value, ways[stage - 1]))

        def arrived(got):
            for (what, call, stage), g in zip(jobs, got):
                parts, near, home = (dx, dx_near, dx_home) if what == "dx" else (outs_of, out_near, out_home)
                if stage == 1:
                    near[call] = add(parts[call][0], g)
                elif stage == 2 and modes(call)[what == "out"] == "ring":
                    near[call] = add(split_half(near[call])[0], g)
                else:
                    home[call] = add(split_half(near[call])[0], g)

        return sends, arrived

    plan = {
        1: [("dx", 0, 1), ("out", 0, 1)],
        2: [("dx", 1, 1), ("dx", 0, 2), ("out", 0, 2)],
        3: [("out", 1, 1), ("dx", 1, 2), ("dx", 0, 3), ("out", 0, 3), ("dx", 2, 1)],
        4: [("out", 1, 2), ("dx", 1, 3)],
        5: [("out", 1, 3)],
    }
    for call in range(calls):
        i, turn = call // 2, call % 2
        more = i + 1 < len(zones)
        jobs = list(plan.get(call, []))
        if call >= 4:
            jobs += [("dx", call - 1, 1), ("dx", call - 2, 2), ("out", call - 2, 1)]
            jobs += [("out", call - 3, 2)] if call >= 5 else []
        sends = []
        if turn == 0 and more:
            row_halves = zone_halves([row_blocks[k] for k in zones[i + 1]])
            sends += firsts(row_halves) + [(near, two) for near, (_, two) in zip(grad_nears, orders)]
        if turn == 1 and more:
            sends += [(near, two) for near, (_, two) in zip(row_nears, orders)]
            if i + 2 < len(zones):
                next_halves = [grads_near(i + 2, turn) for turn in range(2)]
                sends += next_halves
        moved, arrived = moves(jobs)

        def tile(rows, grads, kept_in, call=call):
            return ffn_tile(
                first_expert, rows, grads, router_pad, both_sides, local, call, calls, kept_in, *modes(call)
            )

        got, (outs, kept) = step(moved + sends, tile, row_tiles[i][turn], grad_tiles[i][turn], kept)
        arrived(got)
        got = got[len(moved) :]
        dx[call], outs_of[call] = outs[:2], outs[2:4]
        if turn == 0 and more:
            row_nears = nears(row_halves, got)
            grad_tiles[i + 1] = list(zip(grad_nears, got[2:]))
        if turn == 1 and more:
            row_tiles[i + 1] = list(zip(row_nears, got))
            if i + 2 < len(zones):
                grad_nears = nears([half for half, _ in next_halves], got[2:])

    def planes_of(home, i, turn):
        part = home[2 * i + turn]
        if i == 0:
            return {0: part}
        part = part.reshape(len(zones[i]), -1, part.shape[1])
        return {k: part[j] for j, k in enumerate(zones[i])}

    def summed(terms):
        total = terms[0].astype(F32)
        for term in terms[1:]:
            total = total + term.astype(F32)
        return total

    def weight_part(d, v):
        return t_mm(d.reshape(-1, d.shape[-1])[:, side:], v.reshape(-1, v.shape[-1])).astype(BF16)

    x_all, g_all, hs_all, dg_all, du_all = kept
    dx_terms, out_terms = {0: [], 1: []}, {0: [], 1: []}

    def homeward(home, keys):
        return [(planes_of(home, i, turn)[k], -k) for i, turn, k in keys]

    late = range(1, len(zones) - 1)
    jobs = [("dx", last_call, 1), ("dx", last_call - 1, 2)]
    jobs += [("out", 1, 2)] if 1 not in out_near or out_near[1].shape[0] == 4 * own_rows // 2 else []
    moved, arrived = moves(jobs)
    keys = [(i, turn, k) for i in late for turn in range(2) for k in zones[i]]
    got, part = step(moved + homeward(dx_home, keys), weight_part, dg_all, x_all)
    arrived(got)
    for (_, turn, _), g in zip(keys, got[len(jobs) :]):
        dx_terms[turn].append(g)
    for_pair.append(part)

    jobs = [("dx", last_call, 2)] + ([("dx", 1, 3)] if 1 not in dx_home else [])
    moved, arrived = moves(jobs)
    keys = [(len(zones) - 1, 0, k) for k in zones[-1]]
    got, part = step(
        moved + homeward(dx_home, keys) + [(for_pair[0], "pair")], weight_part, du_all, x_all
    )
    arrived(got)
    dx_terms[0] += got[len(jobs) : -1]
    from_pair.append(got[-1])
    for_pair.append(part)

    jobs = [("out", call, 1) for call in range(2, calls) if call not in out_near]
    moved, arrived = moves(jobs)
    keys = [(len(zones) - 1, 1, k) for k in zones[-1]]
    got, part = step(
        moved + homeward(dx_home, keys) + [(for_pair[1], "pair")], weight_part, hs_all, g_all
    )
    arrived(got)
    dx_terms[1] += got[len(jobs) : -1]
    from_pair.append(got[-1])
    for_pair.append(part)

    d_rows = jnp.concatenate([summed([dx_home[turn], *dx_terms[turn]]) for turn in range(2)], axis=0)
    d_normed = d_rows[:, :width]
    d_gates = d_rows[:, width : width + experts]
    grad_in = cotangent.astype(F32)
    d_logits = (gates * (d_gates - jnp.sum(gates * d_gates, axis=1, keepdims=True))).astype(BF16)
    d_normed = d_normed + mm_t(d_logits, router_w)
    d_norm, grad_gain_ffn = norm_back(hidden_one, scale_ffn, gain_ffn, d_normed)
    d_hidden_one = grad_in + d_norm
    d_attn_own = d_hidden_one.astype(BF16)
    moved, arrived = moves([("out", call, 2) for call in range(2, last_call) if call not in out_home])
    got = step([(d_attn_own, "x"), (for_pair[2], "pair")] + moved)
    d_near = jnp.concatenate([d_attn_own, got[0]], axis=0)
    from_pair.append(got[1])
    arrived(got[2:])
    got = step([(d_near, "pair")])
    d_attn_group = jnp.concatenate([d_near, got[0]], axis=0)
    shared_back = jnp.concatenate(
        [
            add(own[side : side + shared], g[side + tail : side + tail + shared]).reshape(shared, peers, rows_dev)
            for own, g in zip(for_pair, from_pair)
        ],
        axis=0,
    ).transpose(1, 0, 2)
    output_own, output_other = output_grad(places, d_attn_group, saved[5], rows_dev, peers)

    def attend_back(d_attn, *args):
        return attn_backward(heads, peers, score_scale, gain_at, rows_dev, [places, d_attn, *args])

    keys = [(i, turn, k) for i in range(1, len(zones)) for turn in range(2) for k in zones[i] if 2 * i + turn < last_call]
    jobs = [("out", last_call, 2)] + ([("out", 1, 3)] if 1 not in out_home else [])
    moved, arrived = moves(jobs)
    shared_home = lax.all_to_all(shared_back, "expert", 0, 0, tiled=True).astype(F32)
    got, (g_mains, g_others, (near_keep, near_send, d_in_keep, d_in_send)) = step(
        [(output_other, "y")] + moved + homeward(out_home, keys), attend_back,
        d_attn_group, *attn_weights, gain_latent, cos, sin, *saved[:5], *saved[6:], normed_ffn,
        jnp.pad(d_logits, ((0, 0), (ROPE, few - ROPE - experts))), token_group, grad_gain_ffn.reshape(1, width),
    )
    output_parts = [
        add(output_own[k * rows_dev : (k + 1) * rows_dev], got[0][k * rows_dev : (k + 1) * rows_dev]) for k in range(ring)
    ]
    arrived(got[1:])
    for (_, turn, _), g in zip(keys, got[1 + len(jobs) :]):
        out_terms[turn].append(g)

    def own_part(d, v, g):
        return expert_grad(d.reshape(-1, d.shape[-1]), v.reshape(-1, v.shape[-1]), g, local, ff, seg)

    order = [*range(1, ring), 0]

    def two_parts(i, got):
        return [add(g_mains[k], got[j * rows_dev : (j + 1) * rows_dev]) for j, k in enumerate(order[2 * i : 2 * i + 2])]

    keys = [(len(zones) - 1, 1, k) for k in zones[-1]]
    got, grad_gate = step(
        [(g_others[0], "y"), (near_send, "pair"), (d_in_send, "pair"), *homeward(out_home, keys)],
        own_part, dg_all, x_all, from_pair[0],
    )
    main_parts = two_parts(0, got[0])
    near = add(near_keep, got[1])
    keep, d_away = split_half(add(d_in_keep, got[2]))
    few_away = jnp.concatenate([near[1:2], near[2:]], axis=0)
    few_keep = jnp.concatenate([near[0:1], near[2:]], axis=0)
    out_terms[1] += got[3:]
    ffn_out = jnp.concatenate([summed([out_home[turn], *out_terms[turn]]) for turn in range(2)], axis=0)
    block_out = (hidden_one + ffn_out).astype(BF16)

    got, grad_up = step(
        [(g_others[1], "y"), (few_away, "x"), (main_parts[0], "ring"), (output_parts[order[0]], "ring")],
        own_part, du_all, x_all, from_pair[1],
    )
    main_parts += two_parts(1, got[0])
    few_sum = add(few_keep, got[1])
    few_sum = jnp.concatenate([few_sum[j] for j in range(few_sum.shape[0])], axis=1)
    total = add(main_parts[1], got[2])
    total_out = add(output_parts[order[1]], got[3])

    few_half = few_sum.shape[0] // 2
    got, grad_down = step(
        [(few_sum[few_half:], "y"), (d_away, "x"), (total, "ring"), (total_out, "ring")],
        own_part, hs_all, g_all, from_pair[2],
    )
    few_sum = add(few_sum[:few_half], got[0])
    few_planes = [few_sum[k * rows_dev : (k + 1) * rows_dev] for k in range(ring)]
    d_normed_in = keep.astype(F32) + got[1].astype(F32)
    total = add(main_parts[2], got[2])
    total_out = add(output_parts[order[2]], got[3])

    got = step([(total, "ring"), (total_out, "ring"), *((few_planes[k], -k) for k in range(1, ring))])
    total = add(main_parts[3], got[0])
    total_out = add(output_parts[order[3]], got[1])
    few_home = summed([few_planes[0], *got[2:]])
    latent_home = few_home[:, :LANES].astype(BF16)
    for i in range(2, ring // 2):
        got = step([(g_others[i], "y")])
        parts = two_parts(i, got[0])
        for j, part in zip(order[2 * i : 2 * i + 2], parts):
            got = step([(total, "ring"), (total_out, "ring")])
            total = add(part, got[0])
            total_out = add(output_parts[j], got[1])
    home, home_out = total.astype(F32), total_out.astype(F32)

    got = step([(latent_home, "x")])
    latent_two = jnp.stack([latent_home, got[0]])
    got = step([(latent_two, "pair")])
    latent_four = jnp.concatenate([latent_two, got[0]], axis=0)
    grad_latent = jnp.zeros((shards, rows_dev, LANES), BF16)
    for r in range(shards):
        grad_latent = lax.dynamic_update_slice_in_dim(grad_latent, latent_four[r : r + 1], shard_order[r], 0)
    grad_latent = jnp.concatenate([*(grad_latent[j] for j in range(shards)), few_home[:, LANES : LANES + ROPE].astype(BF16)], axis=1)
    grad_router = few_home[:, LANES + ROPE : LANES + ROPE + experts].astype(F32)
    d_token, _ = norm_back(own_float, inverse_rms(own_float), gain_attn, d_normed_in)
    tokens_grad = d_hidden_one + d_token
    gain_home = few_home[:, LANES + gain_at : LANES + gain_at + 3].astype(F32).T

    grad_experts = [grad_gate, grad_up, grad_down]
    grad_shared = [shared_home[:, i * shared : (i + 1) * shared].reshape(shared_dev, rows_dev) for i in range(3)]

    nope_cols = heads * NOPE
    rope_cols = heads * half
    gq = home[:, :query_cols]
    grad_query_own = jnp.concatenate(
        [
            gq[:, :nope_cols].reshape(rows_dev, heads, NOPE),
            gq[:, nope_cols : nope_cols + rope_cols].reshape(rows_dev, heads, half),
            gq[:, nope_cols + rope_cols :].reshape(rows_dev, heads, half),
        ],
        axis=2,
    ).reshape(rows_dev, query_cols)
    g_expand = home[:, query_cols:]
    return (
        block_out,
        tokens_grad,
        gain_home[0],
        grad_query_own,
        grad_latent.astype(F32),
        gain_home[2, :rank_dev],
        jnp.concatenate([g_expand[h * rank_dev : (h + 1) * rank_dev] for h in range(heads)], axis=1),
        home_out.T,
        gain_home[1],
        grad_router,
        grad_shared[0].T,
        grad_shared[1].T,
        grad_shared[2],
        grad_experts[0].transpose(0, 2, 1),
        grad_experts[1].transpose(0, 2, 1),
        grad_experts[2],
    )


def solution(mesh):
    rows = P(("expert", "shard"), None)
    return jax.shard_map(
        body,
        mesh=mesh,
        in_specs=(
            rows,
            P("expert"),
            rows,
            rows,
            P("expert"),
            P("expert", "shard"),
            P("expert", None),
            P("expert"),
            P("expert", "shard"),
            P("shard", "expert"),
            P("expert"),
            P("expert", None),
            P("expert", "shard"),
            P("expert", "shard"),
            P("shard", "expert"),
            P("expert", None, "shard"),
            P("expert", None, "shard"),
            P("expert", "shard", None),
        ),
        out_specs=(
            rows,
            rows,
            P("expert"),
            P("expert", "shard"),
            P("expert", None),
            P("expert"),
            P("expert", "shard"),
            P("shard", "expert"),
            P("expert"),
            P("expert", None),
            P("expert", "shard"),
            P("expert", "shard"),
            P("shard", "expert"),
            P("expert", None, "shard"),
            P("expert", None, "shard"),
            P("expert", "shard", None),
        ),
        check_vma=False,
    )
```

```python
import jax
import jax.numpy as jnp
from jax import lax
from jax.experimental import pallas as pl
from jax.experimental.pallas import tpu as pltpu
from jax.sharding import PartitionSpec as P

NOPE = 128
ROPE = 64
V_HEAD = 128
KV_RANK = 512
TOP = 6
LANES = 128

epsilon = 1e-06
F32 = jnp.float32
BF16 = jnp.bfloat16


def pad_to(n, m):
    return -(-n // m) * m


def angles(places, width):
    half_width = width // 2
    spacing = 10000.0 ** (-2.0 * jnp.arange(half_width, dtype=F32) / width)
    turned = places.astype(F32)[:, None] * spacing[None, :]
    return (jnp.cos(turned), jnp.sin(turned))


def positions(segment):
    indices = jnp.arange(segment.shape[0], dtype=jnp.int32)
    prompt_len = jnp.sum((segment == 0).astype(jnp.int32))
    earlier = jnp.sum((segment[None, :] < segment[:, None]).astype(jnp.int32), axis=1)
    return jnp.where(segment == 0, indices, prompt_len + indices - earlier)


def inverse_rms(values):
    return lax.rsqrt(jnp.mean(values * values, axis=-1, keepdims=True) + epsilon)


def norm_back(values, scaling, gain, incoming):
    weighted = incoming * gain
    inner = jnp.mean(weighted * values, axis=-1, keepdims=True)
    return (
        scaling * weighted - values * scaling**3 * inner,
        jnp.sum(incoming * values * scaling, axis=0),
    )


def dot(a, b, dims):
    return lax.dot_general(a, b, (dims, ((), ())), preferred_element_type=F32)


def mm(a, b):
    return dot(a, b, ((1,), (0,)))


def mm_t(a, b):
    return dot(a, b, ((1,), (1,)))


def t_mm(a, b):
    return dot(a, b, ((0,), (0,)))


BOTH = ("expert", "shard")


def add(a, b):
    return (a.astype(F32) + b.astype(F32)).astype(BF16)


def routes_of(peers, shards):
    def table(step):
        return [
            (e * shards + s, step(e, s)[0] * shards + step(e, s)[1])
            for e in range(peers)
            for s in range(shards)
        ]

    ring = peers // 2

    def around(k):
        return table(lambda e, s: ((e // 2 + k) % ring * 2 + e % 2, s))

    return {
        "y": table(lambda e, s: (e ^ 1, s)),
        "x": table(lambda e, s: (e, s ^ 2)),
        "pair": table(lambda e, s: (e, s ^ 1)),
        "ring": around(1),
        **{k: around(k) for k in range(1 - ring, ring)},
    }


def spread(values, first, lane):
    kept = jnp.where((lane >= first) & (lane < first + ROPE // 2), values, 0.0)
    kept = kept + pltpu.roll(kept, ROPE // 2, 1)
    return kept + pltpu.roll(kept, ROPE, 1)


def attn_forward_kernel(
    heads, peers, score_scale,
    places, tokens, latent_x, latent_pair, cos, sin, index_c, index_r, segment_c, segment_r,
    small, mains,
    part_keep, part_send, normed_o, query_o, key_rope_o, expanded_o, soft_o, mixed_o, compressed_o, latent_o,
    gains, gain_latent, query_w, output_t, expand_w, extra_w, latent_w,
    *, gain_at,
):
    group = tokens.shape[0]
    rank = KV_RANK // peers
    rows = mains[0].shape[0]
    shards = latent_w.shape[0]
    cut = (query_w.shape[1], query_w.shape[1] + output_t.shape[1])
    for p in range(peers):
        to = pl.ds(pl.multiple_of(places[p] * rows, rows), rows)
        query_w[to, :] = mains[p][:, : cut[0]]
        output_t[to, :] = mains[p][:, cut[0] : cut[1]]
        expand_w[to, :] = mains[p][:, cut[1] : cut[1] + expand_w.shape[1]]
        at = slice(p * rows, (p + 1) * rows)
        latent_w[places[peers], to, :] = small[at, :LANES]
        extra_w[to, :] = small[at, LANES:]
        latent_w[places[peers + 1], to, :] = latent_x[at]
        latent_w[places[peers + 2], to, :] = latent_pair[0, at]
        latent_w[places[peers + 3], to, :] = latent_pair[1, at]
    block, at = gain_at // LANES * LANES, gain_at % LANES
    gains[...] = extra_w[:, block : block + LANES].astype(F32).T[at : at + 8]
    few_rows = [extra_w[p * rows : p * rows + rank, block : block + LANES] for p in range(peers)]
    gain_latent[...] = jnp.concatenate(few_rows, axis=0).astype(F32).T[at + 2 : at + 3]
    x = tokens[...].astype(F32)
    x = x * lax.rsqrt(jnp.mean(x * x, axis=1, keepdims=True) + epsilon) * gains[0:1]
    normed_o[...] = x.astype(BF16)
    normed = normed_o[...]
    lane = lax.broadcasted_iota(jnp.int32, (1, LANES), 1)
    c, s = cos[...], sin[...]
    raw = mm(normed, extra_w[:, :LANES])
    a, b = spread(raw, 0, lane), spread(raw, ROPE // 2, lane)
    key_rope_o[:, :LANES] = (a * c - b * s).astype(BF16)
    key_rope_o[:, LANES:] = (b * c + a * s).astype(BF16)
    for j in range(shards):
        compressed_o[:, j * LANES : (j + 1) * LANES] = mm(normed, latent_w[j])
    u = compressed_o[...]
    r = lax.rsqrt(jnp.mean(u * u, axis=1, keepdims=True) + epsilon)
    latent_o[...] = (u * r * gain_latent[...]).astype(BF16)
    q = mm(normed, query_w[...])
    nope = heads * NOPE
    query_o[:, :nope] = q[:, :nope].astype(BF16)
    a, b = q[:, nope : nope + LANES], q[:, nope + LANES :]
    query_o[:, nope : nope + LANES] = (a * c - b * s).astype(BF16)
    query_o[:, nope + LANES :] = (b * c + a * s).astype(BF16)
    allowed = (index_r[...] <= index_c[...]) & ((segment_r[...] == 0) | (segment_r[...] == segment_c[...]))
    lane2 = lax.rem(lax.broadcasted_iota(jnp.int32, (1, 2 * LANES), 1), LANES)
    for h in range(heads):
        w = jnp.concatenate(
            [expand_w[pl.ds((e * heads + h) * rank, rank), :] for e in range(peers)], axis=0
        )
        expanded_o[h] = mm(latent_o[...], w).astype(BF16)
        key_rope = jnp.where((lane2 >= h * ROPE // 2) & (lane2 < (h + 1) * ROPE // 2), key_rope_o[...], jnp.zeros((), BF16))
        scores = mm_t(query_o[:, h * NOPE : (h + 1) * NOPE], expanded_o[h, :, :NOPE]) + mm_t(query_o[:, nope:], key_rope)
        scores = jnp.where(allowed, scores * score_scale, -1e30)
        raised = jnp.exp(scores - jnp.max(scores, axis=1, keepdims=True))
        soft = raised * (1.0 / jnp.sum(raised, axis=1, keepdims=True))
        soft_o[h] = soft
        mixed_o[:, h * V_HEAD : (h + 1) * V_HEAD] = mm(soft.astype(BF16), expanded_o[h, :, NOPE:]).astype(BF16)
    half = group // 2
    part_keep[...] = mm_t(mixed_o[:half], output_t[...]).astype(BF16)
    part_send[...] = mm_t(mixed_o[half:], output_t[...]).astype(BF16)


def attn_backward_kernel(
    heads, peers, score_scale,
    places, d_attn, query_w, output_t, expand_w, extra_w, latent_w, gain_latent, cos, sin,
    normed, query, key_rope_all, expanded, soft_all, compressed, latent,
    normed_ffn, d_logits, tokens, g_gain_ffn,
    g_mains, near_keep, near_send, d_in_keep, d_in_send,
    g_all, g_few, d_query_s, d_latent_s, d_use_s,
    *, gain_at,
):
    group = d_attn.shape[0]
    rank = KV_RANK // peers
    shards = latent_w.shape[0]
    nope = heads * NOPE
    lane = lax.broadcasted_iota(jnp.int32, (1, LANES), 1)
    lane2 = lax.rem(lax.broadcasted_iota(jnp.int32, (1, 2 * LANES), 1), LANES)
    rows = g_mains[0][0].shape[0]
    query_cols = query_w.shape[1]
    width = d_attn.shape[1]
    strips = [slice(lo, lo + width // 4) for lo in range(0, width, width // 4)]
    expand_cols = expand_w.shape[1]
    d_mixed = mm(d_attn[...], output_t[...]).astype(BF16)
    d_query_rope = jnp.zeros((group, 2 * LANES), F32)
    d_key_rope = jnp.zeros((group, 2 * LANES), F32)
    for h in range(heads):
        mine = (lane2 >= h * ROPE // 2) & (lane2 < (h + 1) * ROPE // 2)
        key_rope = jnp.where(mine, key_rope_all[...], jnp.zeros((), BF16))
        soft = soft_all[h]
        d_out = d_mixed[:, h * V_HEAD : (h + 1) * V_HEAD]
        d_soft = mm_t(d_out, expanded[h, :, NOPE:])
        d_scores = score_scale * soft * (d_soft - jnp.sum(soft * d_soft, axis=1, keepdims=True))
        d_scores = d_scores.astype(BF16)
        d_query_s[:, h * NOPE : (h + 1) * NOPE] = mm(d_scores, expanded[h, :, :NOPE]).astype(BF16)
        d_query_rope = d_query_rope + mm(d_scores, key_rope)
        both = jnp.concatenate([query[:, h * NOPE : (h + 1) * NOPE], query[:, nope:]], axis=1)
        d_key = t_mm(d_scores, both)
        d_key_rope = d_key_rope + jnp.where(mine, d_key[:, NOPE:], 0.0)
        d_values = t_mm(soft.astype(BF16), d_out)
        d_expanded = jnp.concatenate([d_key[:, :NOPE], d_values], axis=1).astype(BF16)
        w = jnp.concatenate(
            [expand_w[pl.ds((e * heads + h) * rank, rank), :] for e in range(peers)], axis=0
        )
        g_w = t_mm(latent[...], d_expanded).astype(BF16)
        for e in range(peers):
            g_all[pl.ds((e * heads + h) * rank, rank), :expand_cols] = g_w[e * rank : (e + 1) * rank]
        back = mm_t(d_expanded, w)
        if h == 0:
            d_use_s[...] = back
        else:
            d_use_s[...] += back
    for p in range(peers):
        ref, to = g_mains[p]
        ref[to : to + rows, query_cols:] = g_all[pl.ds(pl.multiple_of(places[p] * rows, rows), rows), :expand_cols]
    c, s = cos[...], sin[...]
    a, b = d_query_rope[:, :LANES], d_query_rope[:, LANES:]
    d_query_s[:, nope : nope + LANES] = (a * c + b * s).astype(BF16)
    d_query_s[:, nope + LANES :] = (b * c - a * s).astype(BF16)
    u, n = compressed[...], d_use_s[...]
    r = lax.rsqrt(jnp.mean(u * u, axis=1, keepdims=True) + epsilon)
    weighted = n * gain_latent[...]
    inner = jnp.mean(weighted * u, axis=1, keepdims=True)
    g_gain_latent = jnp.sum(n * u * r, axis=0, keepdims=True)
    d_latent_s[...] = (r * weighted - u * (r * r * r * inner)).astype(BF16)

    def folded(v):
        v = v + pltpu.roll(v, ROPE // 2, 1)
        return v + pltpu.roll(v, ROPE, 1)

    a, b = folded(d_key_rope[:, :LANES]), folded(d_key_rope[:, LANES:])
    d_extra = jnp.where(
        lane < ROPE // 2, a * c + b * s, jnp.where(lane < ROPE, b * c - a * s, 0.0)
    ).astype(BF16)
    half = group // 2
    g_gain_attn = jnp.zeros((1, tokens.shape[1]), F32)
    fine = half // 2
    for lo in range(0, group, fine):
        part, to = slice(lo, lo + fine), (d_in_keep if lo < half else d_in_send).at[pl.ds(lo % half, fine)]
        total = mm_t(d_query_s[part], query_w[...]) + mm_t(d_extra[part], extra_w[:, :LANES])
        for j in range(shards):
            total = total + mm_t(d_latent_s[part, j * LANES : (j + 1) * LANES], latent_w[j])
        to[...] = total.astype(BF16)
        x = tokens[part].astype(F32)
        x = x * lax.rsqrt(jnp.mean(x * x, axis=1, keepdims=True) + epsilon)
        g_gain_attn = g_gain_attn + jnp.sum(total * x, axis=0, keepdims=True)
    for strip in strips:
        g_all[strip, :] = t_mm(normed[:, strip], d_query_s[...]).astype(BF16)
    wide = extra_w.shape[1] // LANES
    line = lax.broadcasted_iota(jnp.int32, (LANES, 1), 0)
    at_line = gain_at % LANES
    for j in range(wide):
        g_extra = t_mm(normed_ffn[...], d_logits[:, j * LANES : (j + 1) * LANES])
        if j == 0:
            g_extra = g_extra + t_mm(normed[...], d_extra)
        if j == gain_at // LANES:
            both = jnp.where(line == at_line, g_gain_attn, jnp.where(line == at_line + 1, g_gain_ffn[...], 0.0))
            g_extra = g_extra + both.T
        g_few[shards + j] = g_extra.astype(BF16)
    tall = jnp.where(line == at_line + 2, g_gain_latent, 0.0).T.astype(BF16)
    j = shards + gain_at // LANES
    for e in range(peers):
        at = slice(e * rows, e * rows + rank)
        g_few[j, at] = g_few[j, at] + tall[e * rank : (e + 1) * rank]
    for strip in strips:
        g_lat = t_mm(normed[:, strip], d_latent_s[...]).astype(BF16)
        for j in range(shards):
            g_few[j, strip] = g_lat[:, j * LANES : (j + 1) * LANES]
    for p in range(peers):
        at = pl.ds(pl.multiple_of(places[p] * rows, rows), rows)
        to = slice(p * rows, (p + 1) * rows)
        ref, down = g_mains[p]
        ref[down : down + rows, :query_cols] = g_all[at, :]
        for j in range(2):
            near_keep[j, to] = g_few[places[peers + j], at, :]
            near_send[j, to] = g_few[places[peers + 2 + j], at, :]
        for j in range(wide):
            near_keep[2 + j, to] = g_few[shards + j, at, :]
            near_send[2 + j, to] = g_few[shards + j, at, :]


def in_vmem(kernel, outs, scratch, flops, args):
    spec = pl.BlockSpec(memory_space=pltpu.VMEM)
    return pl.pallas_call(
        kernel,
        in_specs=[pl.BlockSpec(memory_space=pltpu.SMEM)] + [spec] * (len(args) - 1),
        out_specs=[spec] * len(outs),
        out_shape=outs,
        scratch_shapes=scratch,
        compiler_params=pltpu.CompilerParams(vmem_limit_bytes=60 * 2**20),
        cost_estimate=pl.CostEstimate(flops=flops, bytes_accessed=24 * 2**20, transcendentals=2**20),
    )(*args)


def attn_forward(heads, peers, score_scale, gain_at, args, small, mains):
    group, width = args[1].shape
    query_cols = heads * (NOPE + ROPE)
    shape = jax.ShapeDtypeStruct
    outs = [
        shape((group // 2, width), BF16), shape((group // 2, width), BF16), shape((group, width), BF16),
        shape((group, query_cols), BF16), shape((group, 2 * LANES), BF16),
        shape((heads, group, NOPE + V_HEAD), BF16), shape((heads, group, group), F32),
        shape((group, heads * V_HEAD), BF16), shape((group, KV_RANK), F32), shape((group, KV_RANK), BF16),
        shape((8, width), F32), shape((1, KV_RANK), F32),
        shape((width, query_cols), BF16), shape((width, heads * V_HEAD), BF16), shape((width, NOPE + V_HEAD), BF16),
        shape((width, small.shape[1] - LANES), BF16), shape((KV_RANK // LANES, width, LANES), BF16),
    ]
    n = len(args)

    def kernel(*refs):
        attn_forward_kernel(
            heads, peers, score_scale, *refs[: n + 1], refs[n + 1 : n + 1 + peers], *refs[n + 1 + peers :],
            gain_at=gain_at,
        )

    return in_vmem(kernel, outs, [], 6 * 10**9, [*args, small, *mains])


def attn_backward(heads, peers, score_scale, gain_at, rows, args):
    group, width = args[1].shape
    query_w, output_t, expand_w, extra_w, latent_w = args[2:7]
    main = query_w.shape[1] + expand_w.shape[1]
    few = extra_w.shape[1] // LANES
    shape = jax.ShapeDtypeStruct
    ring = peers // 2
    order = [*range(1, ring), 0]
    outs = [shape((rows, main), BF16)] * ring + [shape((2 * rows, main), BF16)] * (ring // 2) + [
        shape((2 + few, width, LANES), BF16), shape((2 + few, width, LANES), BF16),
        shape((group // 2, width), BF16), shape((group // 2, width), BF16),
    ]
    scratch = [
        pltpu.VMEM((width, query_w.shape[1]), BF16),
        pltpu.VMEM((latent_w.shape[0] + few, width, LANES), BF16),
        pltpu.VMEM((group, heads * NOPE + 2 * LANES), BF16),
        pltpu.VMEM((group, KV_RANK), BF16),
        pltpu.VMEM((group, KV_RANK), F32),
    ]
    n = len(args)

    def kernel(*refs):
        pieces = [(ref, 0) for ref in refs[n : n + ring]] + [None] * ring
        for i, k in enumerate(order):
            pieces[ring + k] = (refs[n + ring + i // 2], i % 2 * rows)
        rest = refs[n + ring + ring // 2 :]
        attn_backward_kernel(heads, peers, score_scale, *refs[:n], pieces, *rest, gain_at=gain_at)

    outs = in_vmem(kernel, outs, scratch, 12 * 10**9, args)
    return outs[:ring], outs[ring : ring + ring // 2], outs[ring + ring // 2 :]


PARTS = {
    "far": ((0, 1, 2, 3), (4, 5, 6, 7)),
    "near": ((0, 1, 4, 5), (2, 3, 6, 7)),
    "ring": ((0, 2, 4, 6), (1, 3, 5, 7)),
}


def ffn_kernel(
    local, segs_side, steps, width, dx_mode, out_mode,
    first_ref, x0, x1, g0, g1, router, wg, wu, wd,
    dx_keep, dx_send, out_keep, out_send, hs_all, dg_all, du_all,
    acc_out, acc_dx, gates_s, dgates_s,
):
    j = pl.program_id(0)
    half = x0.shape[0]
    unit = half // 4
    block = wg.shape[0]
    x = jnp.concatenate([x0[...], x1[...]], axis=0)
    g_in = jnp.concatenate([g0[:, :width], g1[:, :width]], axis=0)
    first = first_ref[0]
    lane = lax.broadcasted_iota(jnp.int32, (1, LANES), 1)

    @pl.when(j == 0)
    def _():
        logits = mm(x, router[...])
        routed = jnp.concatenate([g0[:, width:], g1[:, width:]], axis=0) > 0
        masked = jnp.where(routed, logits, -1e30)
        raised = jnp.where(routed, jnp.exp(masked - jnp.max(masked, axis=1, keepdims=True)), 0.0)
        gates_s[...] = raised / jnp.sum(raised, axis=1, keepdims=True)
        dgates_s[...] = jnp.zeros_like(dgates_s)
        acc_out[...] = jnp.zeros_like(acc_out)
        acc_dx[...] = jnp.zeros_like(acc_dx)

    gates = gates_s[...]
    wanted, columns = [], []
    for part in range(2):
        seg = 2 * j + part
        expert = jnp.where(seg < 2 * segs_side, lax.rem(seg, segs_side) * local // segs_side, local)
        want = jnp.where(expert < local, first + expert, -1)
        column = jnp.sum(jnp.where(lane == want, gates, 0.0), axis=1, keepdims=True)
        wanted.append(want)
        columns.append(jnp.where(expert < local, column, 1.0))
    lane_block = lax.broadcasted_iota(jnp.int32, (1, block), 1)
    column = jnp.where(lane_block < LANES, columns[0], columns[1])
    gate, up, d_hidden = mm_t(x, wg[...]), mm_t(x, wu[...]), mm_t(g_in, wd[...])
    logistic = 1.0 / (1.0 + jnp.exp(-gate))
    silu = gate * logistic
    hidden = silu * up
    scaled = (hidden * column).astype(BF16)
    product = hidden * d_hidden
    for part in range(2):
        dots = jnp.sum(product[:, part * LANES : (part + 1) * LANES], axis=1, keepdims=True)
        dgates_s[...] += jnp.where(lane == wanted[part], dots, 0.0)
    d_hidden = d_hidden * column
    d_gate = (d_hidden * up * (logistic * (1.0 + gate * (1.0 - logistic)))).astype(BF16)
    d_up = (d_hidden * silu).astype(BF16)
    hs_all[0], dg_all[0], du_all[0] = scaled, d_gate, d_up
    acc_out[...] += mm(scaled, wd[...])
    acc_dx[...] += mm(d_gate, wg[...]) + mm(d_up, wu[...])

    @pl.when(j == steps - 1)
    def _():
        for (keep, away), ranges, is_dx in (
            ((dx_keep, dx_send), PARTS[dx_mode], True),
            ((out_keep, out_send), PARTS[out_mode], False),
        ):
            for ref, blocks in zip((keep, away), ranges):
                for at, block_of in enumerate(blocks):
                    to, rows = pl.ds(at * unit, unit), pl.ds(block_of * unit, unit)
                    if is_dx:
                        ref[to, :width] = acc_dx[rows].astype(BF16)
                        ref[to, width:] = dgates_s[rows].astype(BF16)
                    else:
                        ref[to] = acc_out[rows].astype(BF16)


def ffn_tile(first, rows, grads, router, weights, local, call, calls, kept, dx_mode, out_mode):
    half, width = rows[0].shape
    hid = weights.shape[1]
    block = 2 * LANES
    steps = hid // block
    segs_side = (hid // LANES - 2) // 2

    def fixed(*shape):
        return pl.BlockSpec(shape, lambda j: (0,) * len(shape), pipeline_mode=pl.Buffered(1))

    def whole(*shape):
        return pl.BlockSpec(shape, lambda j: (0,) * len(shape))

    in_specs = [
        pl.BlockSpec(memory_space=pltpu.SMEM),
        fixed(half, width), fixed(half, width), fixed(half, width + LANES), fixed(half, width + LANES), fixed(width, LANES),
        *(pl.BlockSpec((None, block, width), lambda j, i=i: (i, j, 0)) for i in range(3)),
    ]
    args = [first, *rows, *grads, router, weights, weights, weights]
    plain = len(args)
    aliases = {}
    if kept is not None:
        in_specs += [pl.BlockSpec(memory_space=pl.ANY)] * len(kept)
        args += list(kept)
        aliases = {plain + i: 4 + i for i in range(len(kept))}
    tile_hidden = pl.BlockSpec((1, 2 * half, block), lambda j: (call, 0, j))
    shape = jax.ShapeDtypeStruct
    out_shape = (
        [shape((half, width + LANES), BF16)] * 2
        + [shape((half, width), BF16)] * 2
        + [shape((calls, 2 * half, hid), BF16)] * 3
    )
    out_specs = [whole(half, width + LANES)] * 2 + [whole(half, width)] * 2 + [tile_hidden] * 3

    def kernel(*refs):
        ffn_kernel(local, segs_side, steps, width, dx_mode, out_mode, *refs[:plain], *refs[len(args) :])

    outs = pl.pallas_call(
        kernel,
        grid=(steps,),
        in_specs=in_specs,
        out_specs=out_specs,
        out_shape=out_shape,
        scratch_shapes=[pltpu.VMEM((2 * half, width), F32)] * 2
        + [pltpu.VMEM((2 * half, LANES), F32)] * 2,
        input_output_aliases=aliases,
        compiler_params=pltpu.CompilerParams(
            vmem_limit_bytes=56 * 2**20, dimension_semantics=("arbitrary",)
        ),
        cost_estimate=pl.CostEstimate(
            flops=24 * half * width * hid,
            bytes_accessed=6 * width * hid + 16 * half * width,
            transcendentals=2 * half * hid,
        ),
    )(*args)
    return outs[:4], outs[4:]


def pick_pieces(order, sources):
    n, _, lanes = sources[0].shape
    heights = [v.shape[1] for v in sources]

    def kernel(order_ref, *refs):
        for p in range(n):
            at = 0
            for ref, high in zip(refs, heights):
                refs[-1][p, at : at + high] = ref[order_ref[p]]
                at += high

    outs = [jax.ShapeDtypeStruct((n, sum(heights), lanes), BF16)]
    return in_vmem(kernel, outs, [], 0, [order, *sources])[0]


def place_pieces(places, pieces):
    _, rows, lanes = pieces[0].shape
    n = len(pieces)

    def kernel(places_ref, *refs):
        for k in range(n):
            for flip in range(2):
                refs[-1][places_ref[flip * n + k]] = refs[k][flip]

    outs = [jax.ShapeDtypeStruct((2 * n, rows, lanes), BF16)]
    return in_vmem(kernel, outs, [], 0, [places, *pieces])[0]


def output_grad(places, d_attn, mixed, rows, peers):
    width, value_cols = d_attn.shape[1], mixed.shape[1]
    ring = peers // 2

    def kernel(places_ref, d_ref, mixed_ref, own, other, total):
        for lo in range(0, width, width // 4):
            total[lo : lo + width // 4] = t_mm(d_ref[:, lo : lo + width // 4], mixed_ref[...]).astype(BF16)
        for p in range(peers):
            at = pl.ds(pl.multiple_of(places_ref[p] * rows, rows), rows)
            to = p % ring * rows
            (own if p < ring else other)[to : to + rows] = total[at, :]

    outs = [jax.ShapeDtypeStruct((ring * rows, value_cols), BF16)] * 2
    scratch = [pltpu.VMEM((width, value_cols), BF16)]
    return in_vmem(kernel, outs, scratch, 2 * 10**9, [places, d_attn, mixed])


def weight_grad(d, first, cols, tiles, emit, out, got=None):
    rows, width = d.shape[0], out.shape[-1]
    block = 2 * LANES
    pieces, n = cols // block, len(tiles)
    more = [] if got is None else [got]

    def kernel(*refs):
        turned = refs[-1]

        @pl.when(pl.program_id(0) == 0)
        def _():
            for c in range(pieces):
                turned[c * block : (c + 1) * block] = refs[c][...].T

        total = mm(turned[...], jnp.concatenate([ref[...] for ref in refs[pieces : pieces + n]], axis=0))
        emit(refs[-2], total, refs[pieces + n] if more else None)

    return pl.pallas_call(
        kernel,
        grid=(width // block,),
        in_specs=[
            pl.BlockSpec((rows, block), lambda i, c=c: (0, first // block + c), pipeline_mode=pl.Buffered(1))
            for c in range(pieces)
        ]
        + [pl.BlockSpec((v.shape[0], block), lambda i: (0, i)) for v in tiles]
        + [pl.BlockSpec((cols, block), lambda i: (0, i)) for _ in more],
        out_specs=pl.BlockSpec((*out.shape[:-1], block), lambda i: (0,) * (len(out.shape) - 1) + (i,)),
        out_shape=out,
        scratch_shapes=[pltpu.VMEM((cols, rows), BF16)],
        compiler_params=pltpu.CompilerParams(vmem_limit_bytes=56 * 2**20, dimension_semantics=("arbitrary",)),
        cost_estimate=pl.CostEstimate(flops=2 * rows * width * cols, bytes_accessed=20 * 2**20, transcendentals=0),
    )(*[d] * pieces, *tiles, *more)


def expert_grad(d, tiles, got, local, ff, seg, width):
    def emit(ref, total, got_ref):
        total = total + got_ref[...].astype(F32)
        for j in range(local):
            ref[j] = total[j * seg : j * seg + ff]

    return weight_grad(d, 0, local * seg, tiles, emit, jax.ShapeDtypeStruct((local, ff, width), F32), got)


def pair_grad(d, tiles, side, width):
    def emit(ref, total, _):
        ref[...] = total.astype(BF16)

    cols = d.shape[1] - side
    return weight_grad(d, side, cols, tiles, emit, jax.ShapeDtypeStruct((cols, width), BF16))


def pack_experts(parts, seg, room):
    local, ff, width = parts[0].shape
    side = local * seg
    block = 2 * LANES
    shape = jax.ShapeDtypeStruct

    def kernel(gate, up, down, own, both):
        for i, ref in enumerate((gate, up, down)):
            for j in range(local):
                own[i, j * seg : j * seg + ff] = ref[j]
                own[i, j * seg + ff : (j + 1) * seg] = jnp.zeros((seg - ff, block), BF16)
        both[...] = own[...]

    return pl.pallas_call(
        kernel,
        grid=(width // block,),
        in_specs=[pl.BlockSpec((local, ff, block), lambda i: (0, 0, i))] * 3,
        out_specs=[pl.BlockSpec((3, side, block), lambda i: (0, 0, i))] * 2,
        out_shape=[shape((3, side, width), BF16), shape((3, 2 * side + room, width), BF16)],
        compiler_params=pltpu.CompilerParams(vmem_limit_bytes=40 * 2**20),
        cost_estimate=pl.CostEstimate(flops=0, bytes_accessed=30 * 2**20, transcendentals=0),
    )(*parts)


def join_pair(both, other, shared):
    _, side, width = other.shape
    high, wide = shared.shape[1], 8 * LANES
    blocks = side // high

    def kernel(other_ref, shared_ref, _, out):
        @pl.when(pl.program_id(1) < blocks)
        def _():
            out[...] = other_ref[...]

        @pl.when(pl.program_id(1) == blocks)
        def _():
            out[...] = shared_ref[...]

    return pl.pallas_call(
        kernel,
        grid=(width // wide, blocks + 1),
        in_specs=[
            pl.BlockSpec((3, high, wide), lambda i, r: (0, jnp.minimum(r, blocks - 1), i)),
            pl.BlockSpec((3, high, wide), lambda i, r: (0, 0, i)),
            pl.BlockSpec(memory_space=pl.ANY),
        ],
        out_specs=pl.BlockSpec((3, high, wide), lambda i, r: (0, blocks + r, i)),
        out_shape=jax.ShapeDtypeStruct(both.shape, both.dtype),
        input_output_aliases={2: 0},
        compiler_params=pltpu.CompilerParams(vmem_limit_bytes=40 * 2**20),
        cost_estimate=pl.CostEstimate(flops=0, bytes_accessed=22 * 2**20, transcendentals=0),
    )(other, shared, both)


def after(values, *first):
    return lax.optimization_barrier((values, *first))[0]


def body(
    tokens,
    segments,
    routes,
    cotangent,
    attn_gain,
    w_query,
    w_latent,
    latent_gain,
    w_expand,
    w_output,
    ffn_gain,
    w_router,
    w_shared_gate,
    w_shared_up,
    w_shared_down,
    w_expert_gate,
    w_expert_up,
    w_expert_down,
):
    own_rows, width = tokens.shape
    peers = lax.axis_size("expert")
    shards = lax.axis_size("shard")
    ring = peers // 2
    group_len = segments.shape[0]
    experts = w_router.shape[1]
    local, _, ff = w_expert_gate.shape
    rows_dev = w_query.shape[0]
    heads = w_query.shape[1] // (NOPE + ROPE)
    half = ROPE // 2
    rank_dev = w_expand.shape[0]
    expand_cols = w_expand.shape[1]
    value_cols = heads * V_HEAD
    query_cols = heads * (NOPE + ROPE)
    me_e = lax.axis_index("expert").astype(jnp.int32)
    me_s = lax.axis_index("shard").astype(jnp.int32)
    score_scale = (NOPE + ROPE) ** (-0.5)
    shared_dev = w_shared_gate.shape[1]
    shared = shared_dev // peers
    tables = routes_of(peers, shards)
    last = []

    def send(values, way):
        return lax.ppermute(values, BOTH, tables[way])

    def step(sends, work=None, *args):
        nonlocal last
        values = [v for v, _ in sends]
        if last:
            values, tied = after((values, args[:1]), last)
            args = (*tied, *args[1:])
        got = [send(v, way) for v, (_, way) in zip(values, sends)]
        done = work(*args) if work else None
        last = [got, done]
        return (got, done) if work else got

    plane_e = [lax.rem(me_e // 2 + ring - k, ring) * 2 + lax.rem(me_e, 2) for k in range(ring)]
    piece_e = plane_e + [e ^ 1 for e in plane_e]
    shard_order = [me_s, me_s ^ 2, me_s ^ 1, me_s ^ 3]
    places = jnp.stack([*piece_e, *shard_order]).astype(jnp.int32)

    orders = (("y", "x"), ("x", "y"))
    zones = [list(range(k, min(k + 2, ring))) for k in range(0, ring, 2)]
    calls = 2 * len(zones)

    def zone_halves(planes):
        zone = jnp.stack(planes)
        n = zone.shape[1] // 2
        return [zone[:, i * n : (i + 1) * n].reshape(zone.shape[0] * n, zone.shape[2]) for i in range(2)]

    def firsts(halves):
        return [(half, one) for half, (one, _) in zip(halves, orders)]

    def nears(halves, got):
        return [jnp.concatenate([half, g], axis=0) for half, g in zip(halves, got)]

    def split_half(near):
        n = near.shape[0] // 2
        return near[:n], near[n:]

    few = pad_to(ROPE + experts + 3, LANES)
    latent_own = lax.dynamic_slice_in_dim(w_latent, me_s * LANES, LANES, 1)
    gain_cols = jnp.stack([attn_gain, ffn_gain, jnp.pad(latent_gain, (0, rows_dev - rank_dev))], axis=1)
    small = jnp.concatenate(
        [
            latent_own,
            w_latent[:, KV_RANK:],
            w_router,
            gain_cols,
            jnp.zeros((rows_dev, few - ROPE - experts - 3), BF16),
        ],
        axis=1,
    )
    q3 = w_query.reshape(rows_dev, heads, NOPE + ROPE)
    main = jnp.concatenate(
        [
            q3[..., :NOPE].reshape(rows_dev, -1),
            q3[..., NOPE : NOPE + half].reshape(rows_dev, -1),
            q3[..., NOPE + half :].reshape(rows_dev, -1),
            w_output.T,
            jnp.concatenate([w_expand[:, h * (NOPE + V_HEAD) : (h + 1) * (NOPE + V_HEAD)] for h in range(heads)], axis=0),
        ],
        axis=1,
    )
    seg = pad_to(ff, LANES)
    side = seg * local
    tail = pad_to(shared, LANES)
    expert_parts = [w_expert_gate.transpose(0, 2, 1), w_expert_up.transpose(0, 2, 1), w_expert_down]
    ahead = [lax.rem(me_e // 2 + k, ring) * 2 + lax.rem(me_e, 2) for k in range(ring)]
    shared_pack = pick_pieces(
        jnp.stack(ahead + [e ^ 1 for e in ahead]).astype(jnp.int32),
        [
            w_shared_gate.T.reshape(peers, shared, rows_dev),
            w_shared_up.T.reshape(peers, shared, rows_dev),
            w_shared_down.reshape(peers, shared, rows_dev),
        ],
    )
    shared_keep, shared_away = shared_pack[:ring], shared_pack[ring:]
    lane_experts = jnp.arange(experts, dtype=jnp.int32)
    routed_own = jnp.any(routes[:, :, None] == lane_experts[None, None, :], axis=1)
    grad_pack = jnp.concatenate(
        [cotangent, jnp.pad(routed_own.astype(BF16), ((0, 0), (0, LANES - experts)))], axis=1
    )

    def pack(*parts):
        return pack_experts(parts, seg, 2 * tail)

    got = step([(tokens, "x"), (grad_pack, "ring"), (shared_away, "y")])
    token_near = jnp.concatenate([tokens, got[0]], axis=0)
    grad_blocks = [grad_pack, got[1]]
    grad_halves = zone_halves(grad_blocks)
    shared_ways = [jnp.stack([shared_keep[k], got[2][k]]) for k in range(ring)]

    def places_in_group(segments):
        order = jnp.concatenate([s * own_rows + jnp.arange(own_rows, dtype=jnp.int32) for s in shard_order])
        segment = jnp.concatenate(
            [lax.dynamic_slice_in_dim(segments, s * own_rows, own_rows, 0) for s in shard_order], axis=0
        )
        place = positions(segments)
        place = jnp.concatenate(
            [lax.dynamic_slice_in_dim(place, s * own_rows, own_rows, 0) for s in shard_order], axis=0
        )
        cos, sin = angles(place, ROPE)
        return (
            jnp.tile(cos, (1, heads)), jnp.tile(sin, (1, heads)),
            order[:, None], order[None, :], segment[:, None], segment[None, :],
        )

    piece = jnp.concatenate([main, small], axis=1)
    main_own, main_other = [piece], []
    got, (own_side, both_sides) = step(
        [(piece, "ring"), (piece, "y"), firsts(grad_halves)[0]] + [(small, k) for k in range(2, ring)],
        pack, *expert_parts,
    )
    main_own.append(got[0])
    main_other.append(got[1])
    grad_first = [got[2]]
    main_cols = main.shape[1]
    small_far = jnp.concatenate(got[3:], axis=0)

    got, around = step(
        [
            (main_own[1][:, :main_cols], "ring"), (main_own[1], "y"), (small_far, "y"), (token_near, "pair"),
            (own_side, "pair"),
        ],
        places_in_group, segments,
    )
    cos, sin = around[:2]
    main_own.append(got[0])
    main_other.append(got[1])
    small_all = jnp.concatenate(
        [
            main_own[0][:, main_cols:], main_own[1][:, main_cols:], small_far,
            main_other[0][:, main_cols:], main_other[1][:, main_cols:], got[2],
        ],
        axis=0,
    )
    latent_all = small_all[:, :LANES]
    token_group = jnp.concatenate([token_near, got[3]], axis=0)
    other_side = got[4]

    got = step([(main_own[2], "ring"), (main_own[2], "y"), (latent_all, "x"), firsts(grad_halves)[1]])
    main_own.append(got[0])
    main_other.append(got[1])
    latent_x = got[2]
    grad_first.append(got[3])
    grad_nears = nears(grad_halves, grad_first)

    got = step([(main_own[3], "y"), (jnp.stack([latent_all, latent_x]), "pair"), (grad_blocks[1], "ring")])
    main_other.append(got[0])
    latent_pair = got[1]
    grad_blocks.append(got[2])
    for k in range(4, ring):
        got = step([(main_own[k - 1], "ring")])
        main_own.append(got[0])
        got = step([(main_own[k], "y")])
        main_other.append(got[0])
    mains = main_own + main_other

    gain_at = ROPE + experts
    def attend(token_in, small_in, mains_in, places_in, *args):
        return attn_forward(heads, peers, score_scale, gain_at, [places_in, token_in, *args], small_in, mains_in)

    got, outs = step(
        [(near, two) for near, (_, two) in zip(grad_nears, orders)] + [(shared_ways[k], k) for k in range(1, ring)],
        attend, token_group, small_all, mains, places, latent_x, latent_pair, *around,
    )
    grad_tiles = {0: list(zip(grad_nears, got))}
    shared_all = place_pieces(places[:peers], [shared_ways[0], *got[2:]])
    shared_all = shared_all.transpose(1, 0, 2).reshape(3, shared, width)
    shared_own = jnp.pad(shared_all, ((0, 0), (0, tail - shared), (0, 0)))
    saved, attn_weights = outs[2:10], outs[12:]
    gain_attn, gain_ffn, gain_latent = outs[10][0:1], outs[10][1:2], outs[11]
    router_w = outs[15][:, ROPE : ROPE + experts]
    got = step([(outs[1], "pair"), (shared_own, "pair")])
    keep, away = split_half(add(outs[0], got[0]))
    shared_both = jnp.concatenate([shared_own, got[1]], axis=1)
    def grads_near(i, turn):
        half = zone_halves([grad_blocks[k] for k in zones[i]])[turn]
        return half, orders[turn][0]

    got, both_sides = step([(away, "x"), (grad_blocks[2], "ring")], join_pair, both_sides, other_side, shared_both)
    attn_term = keep.astype(F32) + got[0].astype(F32)
    grad_blocks.append(got[1])
    own_float = tokens.astype(F32)
    hidden_one = own_float + attn_term
    scale_ffn = inverse_rms(hidden_one)
    normed_ffn = (hidden_one * scale_ffn * gain_ffn).astype(BF16)
    logits = mm(normed_ffn, router_w)
    masked = jnp.where(routed_own, logits, -1e30)
    lifted = jnp.where(routed_own, jnp.exp(masked - jnp.max(masked, axis=1, keepdims=True)), 0.0)
    gates = lifted / jnp.sum(lifted, axis=1, keepdims=True)

    router_pad = jnp.pad(router_w, ((0, 0), (0, LANES - experts)))
    first_expert = (me_e * local).reshape(1)
    row_blocks = [normed_ffn]
    next_halves = [grads_near(1, turn) for turn in range(2)]
    got = step([(normed_ffn, "ring"), *next_halves])
    row_blocks.append(got[0])
    grad_nears = nears([half for half, _ in next_halves], got[1:])
    row_halves = zone_halves(row_blocks)
    got = step(firsts(row_halves) + [(row_blocks[1], "ring")])
    row_nears = nears(row_halves, got)
    row_blocks.append(got[2])
    got = step([(near, two) for near, (_, two) in zip(row_nears, orders)] + [(row_blocks[2], "ring")])
    row_tiles = {0: list(zip(row_nears, got))}
    row_blocks.append(got[2])

    for _ in range(4, ring):
        got = step([(row_blocks[-1], "ring"), (grad_blocks[-1], "ring")])
        row_blocks.append(got[0])
        grad_blocks.append(got[1])

    kept = None
    dx, dx_near, dx_home, outs_of, out_near, out_home = {}, {}, {}, {}, {}, {}
    for_pair, from_pair = [], []

    last_call = calls - 1

    def modes(call):
        if call < 2:
            return "ring", "ring"
        return ("near", "far") if call == last_call else ("far", "far")

    def moves(jobs):
        sends = []
        for what, call, stage in jobs:
            one, two = orders[call % 2]
            mode = modes(call)[what == "out"]
            ways = {"far": (two, one), "near": (one, two), "ring": (-1, two, one)}[mode]
            parts, near = (dx, dx_near) if what == "dx" else (outs_of, out_near)
            value = parts[call][1] if stage == 1 else split_half(near[call])[1]
            sends.append((value, ways[stage - 1]))

        def arrived(got):
            for (what, call, stage), g in zip(jobs, got):
                parts, near, home = (dx, dx_near, dx_home) if what == "dx" else (outs_of, out_near, out_home)
                if stage == 1:
                    near[call] = add(parts[call][0], g)
                elif stage == 2 and modes(call)[what == "out"] == "ring":
                    near[call] = add(split_half(near[call])[0], g)
                else:
                    home[call] = add(split_half(near[call])[0], g)

        return sends, arrived

    plan = {
        1: [("dx", 0, 1), ("out", 0, 1)],
        2: [("dx", 1, 1), ("dx", 0, 2), ("out", 0, 2)],
        3: [("out", 1, 1), ("dx", 1, 2), ("dx", 0, 3), ("out", 0, 3), ("dx", 2, 1)],
        4: [("out", 1, 2), ("dx", 1, 3)],
        5: [("out", 1, 3)],
    }
    for call in range(calls):
        i, turn = call // 2, call % 2
        more = i + 1 < len(zones)
        jobs = list(plan.get(call, []))
        if call >= 4:
            jobs += [("dx", call - 1, 1), ("dx", call - 2, 2), ("out", call - 2, 1)]
            jobs += [("out", call - 3, 2)] if call >= 5 else []
        sends = []
        if turn == 0 and more:
            row_halves = zone_halves([row_blocks[k] for k in zones[i + 1]])
            sends += firsts(row_halves) + [(near, two) for near, (_, two) in zip(grad_nears, orders)]
        if turn == 1 and more:
            sends += [(near, two) for near, (_, two) in zip(row_nears, orders)]
            if i + 2 < len(zones):
                next_halves = [grads_near(i + 2, turn) for turn in range(2)]
                sends += next_halves
        moved, arrived = moves(jobs)

        def tile(rows, grads, kept_in, call=call):
            return ffn_tile(
                first_expert, rows, grads, router_pad, both_sides, local, call, calls, kept_in, *modes(call)
            )

        got, (outs, kept) = step(moved + sends, tile, row_tiles[i][turn], grad_tiles[i][turn], kept)
        arrived(got)
        got = got[len(moved) :]
        dx[call], outs_of[call] = outs[:2], outs[2:4]
        if turn == 0 and more:
            row_nears = nears(row_halves, got)
            grad_tiles[i + 1] = list(zip(grad_nears, got[2:]))
        if turn == 1 and more:
            row_tiles[i + 1] = list(zip(row_nears, got))
            if i + 2 < len(zones):
                grad_nears = nears([half for half, _ in next_halves], got[2:])

    def planes_of(home, i, turn):
        part = home[2 * i + turn]
        if i == 0:
            return {0: part}
        part = part.reshape(len(zones[i]), -1, part.shape[1])
        return {k: part[j] for j, k in enumerate(zones[i])}

    def summed(terms):
        total = terms[0].astype(F32)
        for term in terms[1:]:
            total = total + term.astype(F32)
        return total

    def weight_part(d, *tiles):
        return pair_grad(d.reshape(-1, d.shape[-1]), tiles, side, width)

    hs_all, dg_all, du_all = kept
    x_all = [v for i in range(len(zones)) for pair in row_tiles[i] for v in pair]
    g_all = [v for i in range(len(zones)) for pair in grad_tiles[i] for v in pair]
    dx_terms, out_terms = {0: [], 1: []}, {0: [], 1: []}

    def homeward(home, keys):
        return [(planes_of(home, i, turn)[k], -k) for i, turn, k in keys]

    late = range(1, len(zones) - 1)
    jobs = [("dx", last_call, 1), ("dx", last_call - 1, 2)]
    jobs += [("out", 1, 2)] if 1 not in out_near or out_near[1].shape[0] == 4 * own_rows // 2 else []
    moved, arrived = moves(jobs)
    keys = [(i, turn, k) for i in late for turn in range(2) for k in zones[i]]
    got, part = step(moved + homeward(dx_home, keys), weight_part, dg_all, *x_all)
    arrived(got)
    for (_, turn, _), g in zip(keys, got[len(jobs) :]):
        dx_terms[turn].append(g)
    for_pair.append(part)

    jobs = [("dx", last_call, 2)] + ([("dx", 1, 3)] if 1 not in dx_home else [])
    moved, arrived = moves(jobs)
    keys = [(len(zones) - 1, 0, k) for k in zones[-1]]
    got, part = step(
        moved + homeward(dx_home, keys) + [(for_pair[0], "pair")], weight_part, du_all, *x_all
    )
    arrived(got)
    dx_terms[0] += got[len(jobs) : -1]
    from_pair.append(got[-1])
    for_pair.append(part)

    jobs = [("out", call, 1) for call in range(2, calls) if call not in out_near]
    moved, arrived = moves(jobs)
    keys = [(len(zones) - 1, 1, k) for k in zones[-1]]
    got, part = step(
        moved + homeward(dx_home, keys) + [(for_pair[1], "pair")], weight_part, hs_all, *g_all
    )
    arrived(got)
    dx_terms[1] += got[len(jobs) : -1]
    from_pair.append(got[-1])
    for_pair.append(part)

    d_rows = jnp.concatenate([summed([dx_home[turn], *dx_terms[turn]]) for turn in range(2)], axis=0)
    d_normed = d_rows[:, :width]
    d_gates = d_rows[:, width : width + experts]
    grad_in = cotangent.astype(F32)
    d_logits = (gates * (d_gates - jnp.sum(gates * d_gates, axis=1, keepdims=True))).astype(BF16)
    d_normed = d_normed + mm_t(d_logits, router_w)
    d_norm, grad_gain_ffn = norm_back(hidden_one, scale_ffn, gain_ffn, d_normed)
    d_hidden_one = grad_in + d_norm
    d_attn_own = d_hidden_one.astype(BF16)
    moved, arrived = moves([("out", call, 2) for call in range(2, last_call) if call not in out_home])
    got = step([(d_attn_own, "x"), (for_pair[2], "pair")] + moved)
    d_near = jnp.concatenate([d_attn_own, got[0]], axis=0)
    from_pair.append(got[1])
    arrived(got[2:])
    got = step([(d_near, "pair")])
    d_attn_group = jnp.concatenate([d_near, got[0]], axis=0)
    shared_back = jnp.concatenate(
        [
            add(own[side : side + shared], g[side + tail : side + tail + shared]).reshape(shared, peers, rows_dev)
            for own, g in zip(for_pair, from_pair)
        ],
        axis=0,
    ).transpose(1, 0, 2)
    output_own, output_other = output_grad(places, d_attn_group, saved[5], rows_dev, peers)

    def attend_back(d_attn, *args):
        return attn_backward(heads, peers, score_scale, gain_at, rows_dev, [places, d_attn, *args])

    keys = [(i, turn, k) for i in range(1, len(zones)) for turn in range(2) for k in zones[i] if 2 * i + turn < last_call]
    jobs = [("out", last_call, 2)] + ([("out", 1, 3)] if 1 not in out_home else [])
    moved, arrived = moves(jobs)
    shared_home = lax.all_to_all(shared_back, "expert", 0, 0, tiled=True).astype(F32)
    got, (g_mains, g_others, (near_keep, near_send, d_in_keep, d_in_send)) = step(
        [(output_other, "y")] + moved + homeward(out_home, keys), attend_back,
        d_attn_group, *attn_weights, gain_latent, cos, sin, *saved[:5], *saved[6:], normed_ffn,
        jnp.pad(d_logits, ((0, 0), (ROPE, few - ROPE - experts))), token_group, grad_gain_ffn.reshape(1, width),
    )
    output_parts = [
        add(output_own[k * rows_dev : (k + 1) * rows_dev], got[0][k * rows_dev : (k + 1) * rows_dev]) for k in range(ring)
    ]
    arrived(got[1:])
    for (_, turn, _), g in zip(keys, got[1 + len(jobs) :]):
        out_terms[turn].append(g)

    def own_part(d, g, *tiles):
        return expert_grad(d.reshape(-1, d.shape[-1]), tiles, g, local, ff, seg, width)

    order = [*range(1, ring), 0]

    def two_parts(i, got):
        return [add(g_mains[k], got[j * rows_dev : (j + 1) * rows_dev]) for j, k in enumerate(order[2 * i : 2 * i + 2])]

    keys = [(len(zones) - 1, 1, k) for k in zones[-1]]
    got, grad_gate = step(
        [(g_others[0], "y"), (near_send, "pair"), (d_in_send, "pair"), *homeward(out_home, keys)],
        own_part, dg_all, from_pair[0], *x_all,
    )
    main_parts = two_parts(0, got[0])
    near = add(near_keep, got[1])
    keep, d_away = split_half(add(d_in_keep, got[2]))
    few_away = jnp.concatenate([near[1:2], near[2:]], axis=0)
    few_keep = jnp.concatenate([near[0:1], near[2:]], axis=0)
    out_terms[1] += got[3:]
    ffn_out = jnp.concatenate([summed([out_home[turn], *out_terms[turn]]) for turn in range(2)], axis=0)
    block_out = (hidden_one + ffn_out).astype(BF16)

    got, grad_up = step(
        [(g_others[1], "y"), (few_away, "x"), (main_parts[0], "ring"), (output_parts[order[0]], "ring")],
        own_part, du_all, from_pair[1], *x_all,
    )
    main_parts += two_parts(1, got[0])
    few_sum = add(few_keep, got[1])
    few_sum = jnp.concatenate([few_sum[j] for j in range(few_sum.shape[0])], axis=1)
    total = add(main_parts[1], got[2])
    total_out = add(output_parts[order[1]], got[3])

    few_half = few_sum.shape[0] // 2
    got, grad_down = step(
        [(few_sum[few_half:], "y"), (d_away, "x"), (total, "ring"), (total_out, "ring")],
        own_part, hs_all, from_pair[2], *g_all,
    )
    few_sum = add(few_sum[:few_half], got[0])
    few_planes = [few_sum[k * rows_dev : (k + 1) * rows_dev] for k in range(ring)]
    d_normed_in = keep.astype(F32) + got[1].astype(F32)
    total = add(main_parts[2], got[2])
    total_out = add(output_parts[order[2]], got[3])

    got = step([(total, "ring"), (total_out, "ring"), *((few_planes[k], -k) for k in range(1, ring))])
    total = add(main_parts[3], got[0])
    total_out = add(output_parts[order[3]], got[1])
    few_home = summed([few_planes[0], *got[2:]])
    latent_home = few_home[:, :LANES].astype(BF16)
    for i in range(2, ring // 2):
        got = step([(g_others[i], "y")])
        parts = two_parts(i, got[0])
        for j, part in zip(order[2 * i : 2 * i + 2], parts):
            got = step([(total, "ring"), (total_out, "ring")])
            total = add(part, got[0])
            total_out = add(output_parts[j], got[1])
    home, home_out = total.astype(F32), total_out.astype(F32)

    got = step([(latent_home, "x")])
    latent_two = jnp.stack([latent_home, got[0]])
    got = step([(latent_two, "pair")])
    latent_four = jnp.concatenate([latent_two, got[0]], axis=0)
    grad_latent = jnp.zeros((shards, rows_dev, LANES), BF16)
    for r in range(shards):
        grad_latent = lax.dynamic_update_slice_in_dim(grad_latent, latent_four[r : r + 1], shard_order[r], 0)
    grad_latent = jnp.concatenate([*(grad_latent[j] for j in range(shards)), few_home[:, LANES : LANES + ROPE].astype(BF16)], axis=1)
    grad_router = few_home[:, LANES + ROPE : LANES + ROPE + experts].astype(F32)
    d_token, _ = norm_back(own_float, inverse_rms(own_float), gain_attn, d_normed_in)
    tokens_grad = d_hidden_one + d_token
    gain_home = few_home[:, LANES + gain_at : LANES + gain_at + 3].astype(F32).T

    grad_experts = [grad_gate, grad_up, grad_down]
    grad_shared = [shared_home[:, i * shared : (i + 1) * shared].reshape(shared_dev, rows_dev) for i in range(3)]

    nope_cols = heads * NOPE
    rope_cols = heads * half
    gq = home[:, :query_cols]
    grad_query_own = jnp.concatenate(
        [
            gq[:, :nope_cols].reshape(rows_dev, heads, NOPE),
            gq[:, nope_cols : nope_cols + rope_cols].reshape(rows_dev, heads, half),
            gq[:, nope_cols + rope_cols :].reshape(rows_dev, heads, half),
        ],
        axis=2,
    ).reshape(rows_dev, query_cols)
    g_expand = home[:, query_cols:]
    return (
        block_out,
        tokens_grad,
        gain_home[0],
        grad_query_own,
        grad_latent.astype(F32),
        gain_home[2, :rank_dev],
        jnp.concatenate([g_expand[h * rank_dev : (h + 1) * rank_dev] for h in range(heads)], axis=1),
        home_out.T,
        gain_home[1],
        grad_router,
        grad_shared[0].T,
        grad_shared[1].T,
        grad_shared[2],
        grad_experts[0].transpose(0, 2, 1),
        grad_experts[1].transpose(0, 2, 1),
        grad_experts[2],
    )


def solution(mesh):
    rows = P(("expert", "shard"), None)
    return jax.shard_map(
        body,
        mesh=mesh,
        in_specs=(
            rows,
            P("expert"),
            rows,
            rows,
            P("expert"),
            P("expert", "shard"),
            P("expert", None),
            P("expert"),
            P("expert", "shard"),
            P("shard", "expert"),
            P("expert"),
            P("expert", None),
            P("expert", "shard"),
            P("expert", "shard"),
            P("shard", "expert"),
            P("expert", None, "shard"),
            P("expert", None, "shard"),
            P("expert", "shard", None),
        ),
        out_specs=(
            rows,
            rows,
            P("expert"),
            P("expert", "shard"),
            P("expert", None),
            P("expert"),
            P("expert", "shard"),
            P("shard", "expert"),
            P("expert"),
            P("expert", None),
            P("expert", "shard"),
            P("expert", "shard"),
            P("shard", "expert"),
            P("expert", None, "shard"),
            P("expert", None, "shard"),
            P("expert", "shard", None),
        ),
        check_vma=False,
    )
```
